32 devices in a mesh: fsdp: 4 (over z), ctx: 4 (over x, core), tp: 2 (over y).
Axes of the slice: x: 2, y: 2, z: 4, core: 2. Of those that a mesh axis runs over, the one named last changes fastest.
Arguments:
- tokens: bfloat16 [4096, 1536], P(('fsdp', 'ctx')), may hold values from -6 to 6
- cotangent: bfloat16 [4096, 1536], P(('fsdp', 'ctx')), may hold values from -6 to 6
- norm_in: float32 [1, 1536], replicated, may hold values from 0.25 to 1.75
- w_qkv: bfloat16 [1, 1536, 2, 1024], P(None, ('fsdp', 'ctx'), 'tp'), may hold values from -0.15625 to 0.15625
- b_qkv: float32 [1, 2, 1024], P(None, 'tp'), may hold values from -3 to 3
- w_out: bfloat16 [1, 1536, 1536], P(None, ('fsdp', 'ctx'), 'tp'), may hold values from -0.625 to 0.625
- norm_mid: float32 [1, 1536], replicated, may hold values from 0.25 to 1.75
- w_gate_up: bfloat16 [1, 1536, 2, 8960], P(None, ('fsdp', 'ctx'), None, 'tp'), may hold values from -0.15625 to 0.15625
- w_down: bfloat16 [1, 1536, 8960], P(None, ('fsdp', 'ctx'), 'tp'), may hold values from -0.09375 to 0.09375
- segments: int32 [4096], P(('fsdp', 'ctx')), may hold values from 0 to 5, as said below
- positions: int32 [4096], P(('fsdp', 'ctx')), may hold values from 0 to 1023, as said below
Outputs:
- output: bfloat16 [4096, 1536], P(('fsdp', 'ctx'))
- grad_tokens: float32 [4096, 1536], P(('fsdp', 'ctx'))
- grad_norm_in: float32 [1, 1536], replicated
- grad_qkv: float32 [1, 1536, 2, 1024], P(None, ('fsdp', 'ctx'), 'tp')
- grad_qkv_bias: float32 [1, 2, 1024], P(None, 'tp')
- grad_out: float32 [1, 1536, 1536], P(None, ('fsdp', 'ctx'), 'tp')
- grad_norm_mid: float32 [1, 1536], replicated
- grad_gate_up: float32 [1, 1536, 2, 8960], P(None, ('fsdp', 'ctx'), None, 'tp')
- grad_down: float32 [1, 1536, 8960], P(None, ('fsdp', 'ctx'), 'tp')
The draws below stay inside these ranges and needn't reach their ends.
Inputs may be any that keep to these rules, and one draw needn't show every extreme that they name: `segments`: within each sequence of 1024 tokens the segment number starts at 0 and rises by one at each document start; every document but a sequence's last has 200 to 2000 tokens, the last is cut off by the sequence's end; the most is reached in some sequence. `positions`: A token's index within its document: 0 at each document start, rising by one along the sequence; the most is reached in some sequence.
All inputs are finite; a program needn't handle non-finite values.
Results may differ from the reference program's by a relative error of at most 0.014.
Values may be sent and summed in bfloat16 or wider, within the bound.
No kernel may reach another device: no remote copies, remote signals or barrier semaphores. Data moves between devices by JAX's collectives and lax.ppermute only.
A program may use at most 256 MiB of HBM per device.

```python
import jax
import jax.numpy as jnp
from jax import lax

D = 1536
H = 12
KV = 2
HD = 128
FF = 8960
LAYERS = 1
DOC_MIN = 200
DOC_MAX = 2000
LEN = 1024
SEQS = 4
TOKENS = 4096


def doc_layout(key):
    count = LEN // DOC_MIN + 1
    lengths = jax.random.randint(jax.random.fold_in(key, 11), (SEQS, count), DOC_MIN, DOC_MAX + 1)
    first_pick = jax.random.randint(jax.random.fold_in(key, 12), (), 0, SEQS)
    offset_pick = jax.random.randint(jax.random.fold_in(key, 13), (), 1, SEQS)
    second_pick = (first_pick + offset_pick) % SEQS
    seq_index = jnp.arange(SEQS, dtype=jnp.int32)[:, None]
    lengths = jnp.where(seq_index == first_pick, DOC_MIN, lengths)
    lengths = jnp.where(seq_index == second_pick, DOC_MAX, lengths)
    starts = jnp.cumsum(lengths, axis=1) - lengths
    token_index = jnp.arange(LEN, dtype=jnp.int32)
    inside = starts[:, None, :] <= token_index[None, :, None]
    segment = jnp.sum(inside.astype(jnp.int32), axis=-1) - 1
    begin = jnp.max(jnp.where(inside, starts[:, None, :], 0), axis=-1)
    return (segment.reshape(-1).astype(jnp.int32), (token_index[None, :] - begin).reshape(-1).astype(jnp.int32))


def draw_segments(key, part):
    return doc_layout(key)[0]


def draw_positions(key, part):
    return doc_layout(key)[1]


def strengthened(values, rng, source, target, parts, factor):
    def block_of(dim):
        return (jnp.arange(values.shape[dim]) // (values.shape[dim] // parts)).reshape((-1,) + (1,) * (values.ndim - 1 - dim))

    one_side = jax.random.permutation(rng, parts)[block_of(target)]
    second = (block_of(target) + parts // 2) % parts
    return jnp.where((block_of(source) == one_side) | (block_of(source) == second), factor * values, values)


def block_scale(stream_key, extent, shards, smallest, largest):
    level, own = 1.0, jax.random.fold_in(stream_key, 6)
    for position, blocks in shards:
        draws = jnp.exp(jax.random.uniform(jax.random.fold_in(own, position), (blocks,), jnp.float32, smallest / len(shards), largest / len(shards)))
        level = level * jnp.repeat(draws, extent[position] // blocks).reshape([-1 if axis == position else 1 for axis in range(len(extent))])
    return level


def scatter_about(rng, shape, deviation, limit, pieces=(), kind=jnp.bfloat16):
    drawn = deviation * jax.random.normal(rng, shape, jnp.float32)
    if pieces:
        drawn = drawn * block_scale(rng, shape, pieces, -0.22, 0.18)
    return jnp.clip(drawn, -limit, limit).astype(kind)


def bell_draw_with(key, dims, deviation, bound, split, heavy, kind=jnp.bfloat16):
    entries = deviation * jax.random.normal(key, dims, jnp.float32)
    if split:
        entries = entries * block_scale(key, dims, split, -0.22, 0.18)
    return jnp.clip(strengthened(entries, jax.random.fold_in(key, 3), *heavy), -bound, bound).astype(kind)


def setup_inputs(seed: int = 0) -> dict:
    splits = jax.random.split(jax.random.key(seed), 12)
    tokens = bell_draw_with(splits[0], (TOKENS, D), 1.0, 6.0, ((0, 16),), (0, 1, 16, 2.0))
    cotangent = bell_draw_with(splits[1], (TOKENS, D), 1.0, 6.0, ((0, 16),), (0, 1, 16, 2.0))
    norm_in = jnp.clip(1.0 + 0.15 * jax.random.normal(splits[2], (LAYERS, D), jnp.float32), 0.25, 1.75)
    w_qkv = scatter_about(splits[3], (LAYERS, D, KV, (H // KV + 2) * HD), D ** -0.5, 0.15625, ((1, 16), (2, 2)))
    b_qkv = scatter_about(splits[4], (LAYERS, KV, (H // KV + 2) * HD), 0.5, 3.0, ((1, 2),), jnp.float32)
    w_out = scatter_about(splits[5], (LAYERS, D, H * HD), (H * HD // 16) ** -0.5, 0.625, ((1, 16), (2, 2)))
    norm_mid = jnp.clip(1.0 + 0.15 * jax.random.normal(splits[6], (LAYERS, D), jnp.float32), 0.25, 1.75)
    w_gate_up = scatter_about(splits[7], (LAYERS, D, 2, FF), D ** -0.5, 0.15625, ((1, 16), (3, 2)))
    w_down = scatter_about(splits[8], (LAYERS, D, FF), (FF // 2) ** -0.5, 0.09375, ((1, 16), (2, 2)))
    segments = draw_segments(jax.random.fold_in(splits[11], 71), 0)
    positions = draw_positions(jax.random.fold_in(splits[11], 71), 0)
    return dict(tokens=tokens, cotangent=cotangent, norm_in=norm_in, w_qkv=w_qkv, b_qkv=b_qkv, w_out=w_out, norm_mid=norm_mid, w_gate_up=w_gate_up, w_down=w_down, segments=segments, positions=positions)


EPS = 1e-06
THETA = 1000000.0
HIGH = lax.Precision.HIGHEST

@jax.custom_vjp
def low(v):
    return lax.optimization_barrier(v.astype(jnp.bfloat16)).astype(jnp.float32)

@jax.custom_vjp
def low_back(v):
    return v

def low_keep(v):
    return (low(v), None)

def low_pass(kept, grad):
    return (grad,)

def back_keep(v):
    return (v, None)

def back_low(kept, grad):
    return (low(grad),)
low.defvjp(low_keep, low_pass)
low_back.defvjp(back_keep, back_low)

def angle_tables(positions):
    exponent = jnp.arange(HD // 2, dtype=jnp.float32) * (2.0 / HD)
    inverse = THETA ** (-exponent)
    phase_angle = positions.astype(jnp.float32)[:, None] * inverse[None, :]
    phase_angle = jnp.concatenate([phase_angle, phase_angle], axis=-1)
    return (jnp.cos(phase_angle), jnp.sin(phase_angle))

def rotary(vectors, cos_table, sin_table):
    half_width = vectors.shape[-1] // 2
    turned = jnp.concatenate([-vectors[..., half_width:], vectors[..., :half_width]], axis=-1)
    return vectors * cos_table + turned * sin_table

def rms_norm(values, gain):
    return values * lax.rsqrt(lax.optimization_barrier(jnp.mean(values * values, axis=-1, keepdims=True)) + EPS) * gain

def attend(queries, key_rows, value_rows, seg_row):
    key_index = jnp.arange(LEN)
    allowed = (seg_row[:, None] == seg_row[None, :]) & (key_index[None, :] <= key_index[:, None])
    scores = jnp.einsum('qgjd,kgd->gjqk', queries, key_rows, precision=HIGH) * HD ** (-0.5)
    scores = low_back(jnp.where(allowed, scores, -1e+30))
    probabilities = low(jax.nn.softmax(scores, axis=-1))
    return jnp.einsum('gjqk,kgd->qgjd', probabilities, value_rows, precision=HIGH)

def layer(residual, seg_rows, cos_table, sin_table, gain_one, weight_qkv, bias_qkv, weight_out, gain_two, weight_pair, weight_down):
    group_heads = H // KV
    normed_one = low(rms_norm(residual, gain_one))
    project = jnp.dot(normed_one, weight_qkv.reshape(D, -1), precision=HIGH) + bias_qkv.reshape(-1)
    project = low_back(project).reshape(TOKENS, KV, group_heads + 2, HD)
    queries = low(rotary(project[:, :, :group_heads], cos_table[:, None, None, :], sin_table[:, None, None, :]))
    key_rows = low(rotary(project[:, :, group_heads], cos_table[:, None, :], sin_table[:, None, :]))
    value_rows = low(project[:, :, group_heads + 1])
    checked = jax.checkpoint(attend)
    attended = lax.map(lambda operands: checked(*operands), (queries.reshape(SEQS, LEN, KV, group_heads, HD), key_rows.reshape(SEQS, LEN, KV, HD), value_rows.reshape(SEQS, LEN, KV, HD), seg_rows))
    attended = low(low_back(attended.reshape(TOKENS, H * HD)))
    middle = residual + low_back(jnp.dot(attended, weight_out.T, precision=HIGH))
    normed_two = low(rms_norm(middle, gain_two))
    gate_up = low_back(jnp.einsum('td,dcf->tcf', normed_two, weight_pair, precision=HIGH))
    activated = low(jax.nn.silu(gate_up[:, 0]) * gate_up[:, 1])
    return middle + low_back(jnp.dot(activated, weight_down.T, precision=HIGH))

def reference(tokens, cotangent, norm_in, w_qkv, b_qkv, w_out, norm_mid, w_gate_up, w_down, segments, positions):
    cos_table, sin_table = angle_tables(positions)
    seg_rows = segments.reshape(SEQS, LEN)

    def forward(residual, gains_one, qkv_all, bias_all, out_all, gains_two, pair_all, down_all):
        for layer_idx in range(LAYERS):
            residual = layer(residual, seg_rows, cos_table, sin_table, gains_one[layer_idx], qkv_all[layer_idx], bias_all[layer_idx], out_all[layer_idx], gains_two[layer_idx], pair_all[layer_idx], down_all[layer_idx])
        return residual
    inputs_float = [entry.astype(jnp.float32) for entry in (tokens, norm_in, w_qkv, b_qkv, w_out, norm_mid, w_gate_up, w_down)]
    result, pullback = jax.vjp(forward, *inputs_float)
    gradients = pullback(cotangent.astype(jnp.float32))
    return (result.astype(jnp.bfloat16), gradients[0], gradients[1], gradients[2], gradients[3], gradients[4], gradients[5], gradients[6], gradients[7])
```

```python
import jax
import jax.numpy as jnp
from jax import lax
from jax.sharding import PartitionSpec as P

HD = 128
EPS = 1e-06
THETA = 1000000.0
BF = jnp.bfloat16
F32 = jnp.float32


def angle_tables(positions):
    exponent = jnp.arange(HD // 2, dtype=F32) * (2.0 / HD)
    inverse = THETA ** (-exponent)
    phase_angle = positions.astype(F32)[:, None] * inverse[None, :]
    phase_angle = jnp.concatenate([phase_angle, phase_angle], axis=-1)
    return (jnp.cos(phase_angle), jnp.sin(phase_angle))


def rotary(vectors, cos_table, sin_table):
    half_width = vectors.shape[-1] // 2
    turned = jnp.concatenate([-vectors[..., half_width:], vectors[..., :half_width]], axis=-1)
    return vectors * cos_table + turned * sin_table


def rotary_back(gradient, cos_table, sin_table):
    scaled = gradient * sin_table
    half_width = gradient.shape[-1] // 2
    turned = jnp.concatenate([scaled[..., half_width:], -scaled[..., :half_width]], axis=-1)
    return gradient * cos_table + turned


def dot(left, right):
    return jnp.dot(left, right, preferred_element_type=F32)


def dot_nt(left, right):
    return lax.dot_general(left, right, (((1,), (1,)), ((), ())), preferred_element_type=F32)


def dot_tn(left, right):
    return lax.dot_general(left, right, (((0,), (0,)), ((), ())), preferred_element_type=F32)


def rotate(block, axis, distance):
    n = lax.axis_size(axis)
    return lax.ppermute(block, axis, [(i, (i + distance) % n) for i in range(n)])


def flip(block, axis, bit):
    n = lax.axis_size(axis)
    return lax.ppermute(block, axis, [(i, i ^ bit) for i in range(n)])


def pick(pieces, index):
    return lax.dynamic_index_in_dim(pieces, index, axis=0, keepdims=False)


def in_order(slots):
    n = len(slots)
    z = lax.axis_index("fsdp")
    whole = jnp.zeros((n,) + slots[0].shape, slots[0].dtype)
    for k, slot in enumerate(slots):
        whole = lax.dynamic_update_index_in_dim(whole, slot, (z - k) % n, axis=0)
    return whole


def over_ctx(block):
    n = lax.axis_size("ctx")
    bit = n // 2
    while bit:
        block = jnp.concatenate([block, flip(block, "ctx", bit)], axis=0)
        bit //= 2
    return block


def whole_weight(rows):
    n = lax.axis_size("fsdp")
    slots = [rows] + [rotate(rows, "fsdp", k) for k in range(1, n)]
    stacked = in_order(slots)
    return over_ctx(stacked.reshape(-1, rows.shape[1]))


def gather_tokens(block):
    n = lax.axis_size("fsdp")
    z = lax.axis_index("fsdp")
    up = down = block
    ups, downs = {}, {}
    other_up, other_down = {}, {}
    other_own = flip(block, "tp", 1)

    def cross(piece, first, last):
        pairs = []
        for i in range(first, last + 1):
            pairs += [(2 * i, 2 * i + 1), (2 * i + 1, 2 * i)]
        return lax.ppermute(piece, ("fsdp", "tp"), pairs)

    for s in range(1, n):
        up = lax.ppermute(up, "fsdp", [(i, i + 1) for i in range(s - 1, n - 1)])
        down = lax.ppermute(down, "fsdp", [(i, i - 1) for i in range(1, n - s + 1)])
        ups[s], downs[s] = up, down
        other_up[s] = cross(up, s, n - 1)
        other_down[s] = cross(down, 0, n - 1 - s)
    own = [block] + [jnp.where(z >= k, ups[k], downs[n - k]) for k in range(1, n)]
    other = [other_own] + [jnp.where(z >= k, other_up[k], other_down[n - k]) for k in range(1, n)]
    return jnp.concatenate(own + other, axis=0)


def scatter_tokens(partial):
    n = lax.axis_size("fsdp")
    rows = partial.shape[0] // (2 * n)
    parts = partial.reshape(2, n, rows, partial.shape[1])
    sums = [parts[0, k] + flip(parts[1, k].astype(BF), "tp", 1).astype(F32) for k in range(n)]
    up = down = None
    for s in range(1, n):
        up_acc = sums[s] if up is None else sums[s] + up.astype(F32)
        down_acc = sums[n - s] if down is None else sums[n - s] + down.astype(F32)
        up = lax.ppermute(up_acc.astype(BF), "fsdp", [(i, i + 1) for i in range(s)])
        down = lax.ppermute(down_acc.astype(BF), "fsdp", [(i, i - 1) for i in range(n - s, n)])
    return sums[0] + up.astype(F32) + down.astype(F32)


def reduce_ctx(left, right):
    n = lax.axis_size("ctx")
    half = left.shape[1] // 2
    total = dot_tn(left[:, :half], right)
    arrived = flip(dot_tn(left[:, half:], right).astype(BF), "ctx", 1)
    total = total + arrived.astype(F32)
    bit = 2
    while bit < n:
        half //= 2
        total = total[:half] + flip(total[half:].astype(BF), "ctx", bit).astype(F32)
        bit *= 2
    return total


def reduce_weight(left, right):
    n = lax.axis_size("fsdp")
    z = lax.axis_index("fsdp")
    total = reduce_ctx(left, right)
    parts = total.reshape(n, total.shape[0] // n, total.shape[1])
    out = pick(parts, z)
    for k in range(1, n):
        out = out + rotate(pick(parts, (z + k) % n).astype(BF), "fsdp", k).astype(F32)
    return out


def deal_weight(left, right):
    n = lax.axis_size("fsdp")
    z = lax.axis_index("fsdp")
    total = reduce_ctx(left, right).astype(BF)
    parts = total.reshape(n, total.shape[0] // n, total.shape[1])
    return [pick(parts, z)] + [rotate(pick(parts, (z + k) % n), "fsdp", k) for k in range(1, n)]


def sum_everywhere(vector, axes):
    for axis in axes:
        bit = 1
        while bit < lax.axis_size(axis):
            vector = vector + flip(vector, axis, bit)
            bit *= 2
    return vector


def body(
    tokens,
    cotangent,
    norm_in,
    w_qkv,
    b_qkv,
    w_out,
    norm_mid,
    w_gate_up,
    w_down,
    segments,
    positions,
):
    n, ctx_size = lax.axis_size("fsdp"), lax.axis_size("ctx")
    z, ctx, y = lax.axis_index("fsdp"), lax.axis_index("ctx"), lax.axis_index("tp")
    count, width = tokens.shape
    h = count // 2
    rows = w_qkv.shape[1]
    heads = w_qkv.shape[3] // HD - 2
    hidden = w_down.shape[2]
    piece = -(-hidden // (n * HD)) * HD
    scale = HD ** (-0.5)

    order = [0]
    bit = ctx_size // 2
    while bit:
        order = order + [j ^ bit for j in order]
        bit //= 2
    places = [ctx ^ j for j in order]

    def to_relative(values):
        parts = values.reshape(values.shape[0], n, ctx_size, rows)
        picked = [lax.dynamic_index_in_dim(parts, place, axis=2, keepdims=False) for place in places]
        return jnp.stack(picked, axis=1).reshape(values.shape)

    def to_natural(values):
        parts = values.reshape(values.shape[0], ctx_size, n, rows)
        where = [order.index(j) for j in range(ctx_size)]
        relative = [parts[:, place] for place in where]
        stacked = jnp.stack(relative, axis=1)
        natural = [lax.dynamic_index_in_dim(stacked, ctx ^ j, axis=1, keepdims=False) for j in range(ctx_size)]
        return jnp.stack(natural, axis=2).reshape(values.shape)

    def own_half(values):
        return lax.dynamic_slice_in_dim(values, y * h, h, axis=0)

    def other_half(values):
        return lax.dynamic_slice_in_dim(values, (1 - y) * h, h, axis=0)

    def both_halves(own):
        other = flip(own, "tp", 1)
        return jnp.where(
            y == 0, jnp.concatenate([own, other], axis=0), jnp.concatenate([other, own], axis=0)
        )

    qkv_whole = whole_weight(w_qkv[0].reshape(rows, -1))
    out_whole = whole_weight(w_out[0])

    pad = n * piece - hidden
    gate_rows = jnp.pad(w_gate_up[0, :, 0], ((0, 0), (0, pad)))
    up_rows = jnp.pad(w_gate_up[0, :, 1], ((0, 0), (0, pad)))
    down_rows = jnp.pad(w_down[0], ((0, 0), (0, pad)))

    def columns(values, index):
        return lax.dynamic_slice_in_dim(values, index * piece, piece, axis=1)

    pair_slots, down_slots = [], []
    for k in range(n):
        index = (z + k) % n
        pair = jnp.concatenate([columns(gate_rows, index), columns(up_rows, index)], axis=1)
        pair_slots.append(rotate(pair, "fsdp", k) if k else pair)
    for k in range(n):
        down = columns(down_rows, (z + k) % n)
        down_slots.append(rotate(down, "fsdp", k) if k else down)
    pair_whole = over_ctx(in_order(pair_slots).reshape(n * rows, -1))
    down_whole = over_ctx(in_order(down_slots).reshape(n * rows, -1))

    x0 = to_relative(tokens).astype(F32)
    grad_in = to_relative(cotangent)
    gain_one = to_relative(norm_in)
    gain_two = to_relative(norm_mid)

    cos_table, sin_table = angle_tables(positions)
    inverse_one = lax.rsqrt(jnp.mean(x0 * x0, axis=-1, keepdims=True) + EPS)
    normed_one = (x0 * inverse_one * gain_one).astype(BF)
    project = dot(normed_one, qkv_whole) + b_qkv[0].reshape(-1)
    project = project.reshape(count, heads + 2, HD)
    queries = rotary(project[:, :heads], cos_table[:, None], sin_table[:, None]).astype(BF)
    key_local = rotary(project[:, heads], cos_table, sin_table).astype(BF)
    value_local = project[:, heads + 1].astype(BF)
    local_pair = jnp.stack([key_local, value_local])
    pairs_all = [local_pair] + [flip(local_pair, "ctx", j) for j in range(1, ctx_size)]
    key_rows = jnp.concatenate([p[0] for p in pairs_all], axis=0)
    value_rows = jnp.concatenate([p[1] for p in pairs_all], axis=0)
    query_index = ctx * count + jnp.arange(count, dtype=jnp.int32)
    key_index = jnp.concatenate(
        [(ctx ^ j) * count + jnp.arange(count, dtype=jnp.int32) for j in range(ctx_size)]
    )
    first_key = query_index - positions
    allowed = (key_index[None, :] <= query_index[:, None]) & (
        key_index[None, :] >= first_key[:, None]
    )

    def attention_scores():
        scores = jnp.einsum("tgd,kd->gtk", queries, key_rows, preferred_element_type=F32) * scale
        return jnp.where(allowed[None], scores, -1e30)

    scores = attention_scores()
    peak = jnp.max(scores, axis=-1, keepdims=True)
    shifted = jnp.exp(scores - peak)
    total = jnp.sum(shifted, axis=-1, keepdims=True)
    probabilities = (shifted / total).astype(BF)
    log_total = peak + jnp.log(total)
    attended = jnp.einsum("gtk,kd->tgd", probabilities, value_rows, preferred_element_type=F32)
    attended = attended.astype(BF).reshape(count, -1)
    branch = dot_nt(attended, out_whole)
    arrived = flip(other_half(branch).astype(BF), "tp", 1)
    middle = own_half(x0) + own_half(branch) + arrived.astype(F32)

    inverse_two = lax.rsqrt(jnp.mean(middle * middle, axis=-1, keepdims=True) + EPS)
    normed_two = (middle * inverse_two * gain_two).astype(BF)
    grad_half = own_half(grad_in)
    grad_all = gather_tokens(grad_half)
    normed_all = gather_tokens(normed_two)
    gate_up = dot(normed_all, pair_whole)
    gate, upward = gate_up[:, :piece], gate_up[:, piece:]
    sigma = jax.nn.sigmoid(gate)
    activated = (gate * sigma * upward).astype(BF)
    grad_activated = dot(grad_all, down_whole)
    grad_gate = grad_activated * upward * sigma * (1.0 + gate * (1.0 - sigma))
    grad_upward = grad_activated * (gate * sigma)
    grad_pair = jnp.concatenate([grad_gate.astype(BF), grad_upward.astype(BF)], axis=1)
    grad_normed_two = scatter_tokens(dot_nt(grad_pair, pair_whole))

    scaled = grad_normed_two * gain_two
    gain_two_grad = jnp.sum(grad_normed_two * middle * inverse_two, axis=0)
    grad_middle = (
        inverse_two * scaled
        - middle * inverse_two**3 * jnp.mean(scaled * middle, axis=-1, keepdims=True)
        + grad_half.astype(F32)
    )
    out_in = both_halves(grad_middle.astype(BF))

    grad_heads = dot(out_in, out_whole).astype(BF).reshape(count, heads, HD)
    exact = jnp.exp(attention_scores() - log_total)
    grad_probs = jnp.einsum("tgd,kd->gtk", grad_heads, value_rows, preferred_element_type=F32)
    grad_scores = exact * (grad_probs - jnp.sum(exact * grad_probs, axis=-1, keepdims=True))
    grad_scores = grad_scores.astype(BF)
    grad_queries = (
        jnp.einsum("gtk,kd->tgd", grad_scores, key_rows, preferred_element_type=F32) * scale
    )
    grad_key_rows = (
        jnp.einsum("gtk,tgd->kd", grad_scores, queries, preferred_element_type=F32) * scale
    )
    grad_value_rows = jnp.einsum(
        "gtk,tgd->kd", exact.astype(BF), grad_heads, preferred_element_type=F32
    )
    grad_pairs = jnp.stack([grad_key_rows, grad_value_rows]).reshape(2, ctx_size, count, HD)
    grad_kv = grad_pairs[:, 0]
    for j in range(1, ctx_size):
        grad_kv = grad_kv + flip(grad_pairs[:, j].astype(BF), "ctx", j).astype(F32)
    grad_project = (
        jnp.concatenate(
            [
                rotary_back(grad_queries, cos_table[:, None], sin_table[:, None]),
                rotary_back(grad_kv[0], cos_table, sin_table)[:, None],
                grad_kv[1][:, None],
            ],
            axis=1,
        )
        .astype(BF)
        .reshape(count, -1)
    )
    bias_grad = jnp.sum(grad_project, axis=0, dtype=F32)
    partial_one = dot_nt(grad_project, qkv_whole).astype(BF)
    grad_normed_one = partial_one.astype(F32) + flip(partial_one, "tp", 1).astype(F32)
    scaled = grad_normed_one * gain_one
    gain_one_grad = jnp.sum(grad_normed_one * x0 * inverse_one, axis=0)
    grad_tokens = (
        inverse_one * scaled
        - x0 * inverse_one**3 * jnp.mean(scaled * x0, axis=-1, keepdims=True)
        + out_in.astype(F32)
    )

    residual = middle + scatter_tokens(dot_nt(activated, down_whole))
    output = to_natural(both_halves(residual.astype(BF)))

    def natural_columns(slots):
        whole = jnp.zeros((rows, n * piece), F32)
        for k, slot in enumerate(slots):
            whole = lax.dynamic_update_slice_in_dim(
                whole, slot.astype(F32), ((z - k) % n) * piece, axis=1
            )
        return whole[:, :hidden]

    down_grad = natural_columns(deal_weight(grad_all, activated))
    pair_grads = deal_weight(normed_all, grad_pair)
    pair_grad = jnp.stack(
        [
            natural_columns([slot[:, :piece] for slot in pair_grads]),
            natural_columns([slot[:, piece:] for slot in pair_grads]),
        ],
        axis=1,
    )
    out_grad = reduce_weight(out_in, attended)
    qkv_grad = reduce_weight(normed_one, grad_project)

    gain_two_all = sum_everywhere(to_natural(gain_two_grad[None]), ("tp", "ctx", "fsdp"))
    small = jnp.concatenate([to_natural(gain_one_grad[None]), bias_grad[None]], axis=1)
    small_all = sum_everywhere(small, ("ctx", "fsdp"))
    return (
        output,
        to_natural(grad_tokens),
        small_all[:, :width],
        qkv_grad.reshape(1, rows, 1, -1),
        small_all[:, width:].reshape(1, 1, -1),
        out_grad[None],
        gain_two_all,
        pair_grad[None],
        down_grad[None],
    )


def solution(mesh):
    rows = ("fsdp", "ctx")
    in_specs = (
        P(rows, None),
        P(rows, None),
        P(),
        P(None, rows, "tp", None),
        P(None, "tp", None),
        P(None, rows, "tp"),
        P(),
        P(None, rows, None, "tp"),
        P(None, rows, "tp"),
        P(rows),
        P(rows),
    )
    out_specs = (
        P(rows, None),
        P(rows, None),
        P(),
        P(None, rows, "tp", None),
        P(None, "tp", None),
        P(None, rows, "tp"),
        P(),
        P(None, rows, None, "tp"),
        P(None, rows, "tp"),
    )
    return jax.shard_map(body, mesh=mesh, in_specs=in_specs, out_specs=out_specs, check_vma=False)
```

```python
import jax
import jax.numpy as jnp
from jax import lax
from jax.experimental import pallas as pl
from jax.experimental.pallas import tpu as pltpu
from jax.sharding import PartitionSpec as P

HD = 128
EPS = 1e-06
THETA = 1000000.0
BF = jnp.bfloat16
F32 = jnp.float32


def angle_tables(positions):
    exponent = jnp.arange(HD // 2, dtype=F32) * (2.0 / HD)
    inverse = THETA ** (-exponent)
    phase_angle = positions.astype(F32)[:, None] * inverse[None, :]
    phase_angle = jnp.concatenate([phase_angle, phase_angle], axis=-1)
    return (jnp.cos(phase_angle), jnp.sin(phase_angle))


def rotary(vectors, cos_table, sin_table):
    half_width = vectors.shape[-1] // 2
    turned = jnp.concatenate([-vectors[..., half_width:], vectors[..., :half_width]], axis=-1)
    return vectors * cos_table + turned * sin_table


def rotary_back(gradient, cos_table, sin_table):
    scaled = gradient * sin_table
    half_width = gradient.shape[-1] // 2
    turned = jnp.concatenate([scaled[..., half_width:], -scaled[..., :half_width]], axis=-1)
    return gradient * cos_table + turned


def dot(left, right):
    return jnp.dot(left, right, preferred_element_type=F32)


def dot_nt(left, right):
    return lax.dot_general(left, right, (((1,), (1,)), ((), ())), preferred_element_type=F32)


def dot_tn(left, right):
    return lax.dot_general(left, right, (((0,), (0,)), ((), ())), preferred_element_type=F32)


def after(value, *earlier):
    return lax.optimization_barrier((value,) + earlier)[0]


def rotate(block, axis, distance):
    n = lax.axis_size(axis)
    return lax.ppermute(block, axis, [(i, (i + distance) % n) for i in range(n)])


def flip(block, axis, bit):
    n = lax.axis_size(axis)
    return lax.ppermute(block, axis, [(i, i ^ bit) for i in range(n)])


def pick(pieces, index):
    return lax.dynamic_index_in_dim(pieces, index, axis=0, keepdims=False)


def in_order(slots):
    n = len(slots)
    z = lax.axis_index("fsdp")
    if n <= 4:
        return jnp.stack([lax.select_n((z - b) % n, *slots) for b in range(n)])
    whole = jnp.zeros((n,) + slots[0].shape, slots[0].dtype)
    for k, slot in enumerate(slots):
        whole = lax.dynamic_update_index_in_dim(whole, slot, (z - k) % n, axis=0)
    return whole


def deal(blocks, axis):
    return lax.all_to_all(blocks, axis, 0, 0, tiled=True)


def gather_up(block, s):
    n = lax.axis_size("fsdp")
    return lax.ppermute(block, "fsdp", [(i, i + 1) for i in range(s - 1, n - 1)])


def gather_down(block, s):
    n = lax.axis_size("fsdp")
    return lax.ppermute(block, "fsdp", [(i, i - 1) for i in range(1, n - s + 1)])


def slots_of(own, ups, downs):
    n = lax.axis_size("fsdp")
    z = lax.axis_index("fsdp")
    return [own] + [jnp.where(z >= k, ups[k], downs[n - k]) for k in range(1, n)]


def sum_up(block, s):
    n = lax.axis_size("fsdp")
    return lax.ppermute(block.astype(BF), "fsdp", [(i, i + 1) for i in range(s)])


def sum_down(block, s):
    n = lax.axis_size("fsdp")
    return lax.ppermute(block.astype(BF), "fsdp", [(i, i - 1) for i in range(n - s, n)])


def chain_sum(sums, *earlier):
    n = len(sums)
    up, down = sums[1], sums[n - 1]
    if earlier:
        up, down = after(up, *earlier), after(down, *earlier)
    for s in range(1, n):
        up, down = sum_up(up, s), sum_down(down, s)
        if s < n - 1:
            up = sums[s + 1] + up.astype(F32)
            down = sums[n - s - 1] + down.astype(F32)
    return sums[0] + up.astype(F32) + down.astype(F32)


def split_x(total):
    half = total.shape[0] * 2 // lax.axis_size("ctx")
    return [total[:half]] + [
        total[start : start + half].astype(BF) for start in range(half, total.shape[0], half)
    ]


def join_x(parts, *earlier):
    total = parts[0]
    order = [0]
    bit = lax.axis_size("ctx") // 2
    while bit > 1:
        order = order + [j ^ bit for j in order]
        bit //= 2
    moved = [flip(part, "ctx", j) for part, j in zip(parts[1:], order[1:], strict=True)]
    if earlier:
        moved = [after(part, *earlier) for part in moved]
    for part in moved:
        total = total + part.astype(F32)
    return total


def hidden_kernel(blocks, x_ref, g_ref, *refs):
    pairs, downs = refs[:blocks], refs[blocks : 2 * blocks]
    act_ref, grad_ref, pair_ref, down_ref = refs[2 * blocks :]
    block, tile = downs[0].shape
    for b in range(blocks):
        pair_ref[b * block : (b + 1) * block, :] = pairs[b][...]
        down_ref[b * block : (b + 1) * block, :] = downs[b][...]
    chunk = min(512, x_ref.shape[0])
    for start in range(0, x_ref.shape[0], chunk):
        here = pl.ds(start, chunk)
        both = dot(x_ref[here, :], pair_ref[...])
        grad = dot(g_ref[here, :], down_ref[...])
        gate, upward = both[:, :tile], both[:, tile:]
        sigma = 1.0 / (1.0 + jnp.exp(-gate))
        silu = gate * sigma
        act_ref[here, :] = (silu * upward).astype(BF)
        grad_ref[here, :tile] = (grad * upward * sigma * (1.0 + gate * (1.0 - sigma))).astype(BF)
        grad_ref[here, tile:] = (grad * silu).astype(BF)


def hidden_pass(x, g, pairs, downs, tile):
    count, width = x.shape
    block, piece = downs[0].shape
    rows = min(1024, count)
    token = pl.BlockSpec((rows, width), lambda t, r: (r, 0))
    pair = pl.BlockSpec((block, 2 * tile), lambda t, r: (0, t))
    down = pl.BlockSpec((block, tile), lambda t, r: (0, t))
    return pl.pallas_call(
        lambda *refs: hidden_kernel(len(pairs), *refs),
        grid=(piece // tile, count // rows),
        in_specs=[token, token] + [pair] * len(pairs) + [down] * len(downs),
        out_specs=[
            pl.BlockSpec((rows, tile), lambda t, r: (r, t)),
            pl.BlockSpec((rows, 2 * tile), lambda t, r: (r, t)),
            pl.BlockSpec((width, 2 * tile), lambda t, r: (0, t)),
            pl.BlockSpec((width, tile), lambda t, r: (0, t)),
        ],
        out_shape=[
            jax.ShapeDtypeStruct((count, piece), BF),
            jax.ShapeDtypeStruct((count, 2 * piece), BF),
            jax.ShapeDtypeStruct((width, 2 * piece), BF),
            jax.ShapeDtypeStruct((width, piece), BF),
        ],
        compiler_params=pltpu.CompilerParams(vmem_limit_bytes=58 * 2**20),
        cost_estimate=pl.CostEstimate(
            flops=6 * count * width * piece,
            bytes_accessed=2 * (2 * count * width + 6 * width * piece + 3 * count * piece),
            transcendentals=count * piece,
        ),
    )(x, g, *pairs, *downs)


def add_z(total, *earlier):
    n = lax.axis_size("fsdp")
    if earlier:
        total = after(total, *earlier)
    parts = deal(total.astype(BF).reshape(n, total.shape[0] // n, total.shape[1]), "fsdp")
    return jnp.sum(parts.astype(F32), axis=0)


def sum_everywhere(vector, axes):
    for axis in axes:
        bit = 1
        while bit < lax.axis_size(axis):
            vector = vector + flip(vector, axis, bit)
            bit *= 2
    return vector


def body(
    tokens,
    cotangent,
    norm_in,
    w_qkv,
    b_qkv,
    w_out,
    norm_mid,
    w_gate_up,
    w_down,
    segments,
    positions,
):
    n, ctx_size = lax.axis_size("fsdp"), lax.axis_size("ctx")
    z, ctx, y = lax.axis_index("fsdp"), lax.axis_index("ctx"), lax.axis_index("tp")
    count, width = tokens.shape
    h = count // 2
    rows = w_qkv.shape[1]
    heads = w_qkv.shape[3] // HD - 2
    hidden = w_down.shape[2]
    piece = -(-hidden // (n * HD)) * HD
    scale = HD ** (-0.5)

    order = [0]
    bit = ctx_size // 2
    while bit:
        order = order + [j ^ bit for j in order]
        bit //= 2

    def one_hot():
        at = jnp.arange(width, dtype=jnp.int32)
        block = sum(jnp.where(at // (n * rows) == b, ctx ^ j, 0) for b, j in enumerate(order))
        layer = (at // rows) % n
        source = (layer * ctx_size + block) * rows + at % rows
        return (jnp.arange(width, dtype=jnp.int32)[:, None] == source[None, :]).astype(BF)

    def to_relative(values):
        parts = values.reshape(values.shape[0], n, ctx_size, rows)
        picked = [
            lax.dynamic_index_in_dim(parts, ctx ^ j, axis=2, keepdims=False) for j in order
        ]
        return jnp.stack(picked, axis=1).reshape(values.shape)

    def to_natural(values):
        parts = values.reshape(values.shape[0], ctx_size, n, rows)
        where = [order.index(j) for j in range(ctx_size)]
        stacked = jnp.stack([parts[:, place] for place in where], axis=1)
        natural = [
            lax.dynamic_index_in_dim(stacked, ctx ^ j, axis=1, keepdims=False)
            for j in range(ctx_size)
        ]
        return jnp.stack(natural, axis=2).reshape(values.shape)

    def own_half(values):
        return lax.dynamic_slice_in_dim(values, y * h, h, axis=0)

    def other_half(values):
        return lax.dynamic_slice_in_dim(values, (1 - y) * h, h, axis=0)

    def both_halves(own):
        other = flip(own, "tp", 1)
        return jnp.where(
            y == 0, jnp.concatenate([own, other], axis=0), jnp.concatenate([other, own], axis=0)
        )

    half_d = width // 2
    qkv_whole = lax.all_gather(w_qkv[0].reshape(rows, -1), ("fsdp", "ctx"), axis=0, tiled=True)
    out_slots = [w_out[0]] + [rotate(w_out[0], "fsdp", k) for k in range(1, n)]

    x0 = tokens.astype(F32)
    inverse_one = lax.rsqrt(jnp.mean(x0 * x0, axis=-1, keepdims=True) + EPS)
    normed_one = (x0 * inverse_one * norm_in).astype(BF)
    place = one_hot()
    placed = dot(jnp.concatenate([own_half(tokens), cotangent, normed_one]), place)
    x0_half, grad_in = placed[:h], placed[h : h + count].astype(BF)
    normed_placed = placed[h + count :].astype(BF)
    grad_half = own_half(grad_in)
    gain_two = to_relative(norm_mid)
    cos_table, sin_table = angle_tables(positions)

    tile = 3 * HD if piece % (3 * HD) == 0 else HD
    pad = n * piece - hidden
    gate_rows = jnp.pad(w_gate_up[0, :, 0], ((0, 0), (0, pad)))
    up_rows = jnp.pad(w_gate_up[0, :, 1], ((0, 0), (0, pad)))
    down_rows = jnp.pad(w_down[0], ((0, 0), (0, pad)))
    pair_out, down_out = [], []
    for index in range(n):
        columns = []
        for start in range(index * piece, (index + 1) * piece, tile):
            columns += [gate_rows[:, start : start + tile], up_rows[:, start : start + tile]]
        pair_out.append(jnp.concatenate(columns, axis=1))
        down_out.append(down_rows[:, index * piece : (index + 1) * piece])
    pair_block = deal(jnp.stack(pair_out), "fsdp").reshape(n * rows, 2 * piece)
    down_block = deal(after(jnp.stack(down_out), pair_block), "fsdp").reshape(n * rows, piece)

    def over_x(piece_rows):
        held = [piece_rows]
        bit = ctx_size // 2
        while bit > 1:
            held = held + [flip(part, "ctx", bit) for part in held]
            bit //= 2
        return held

    def over_cores(held):
        return held + [flip(part, "ctx", 1) for part in held]

    out_a = jnp.concatenate(over_x(in_order(out_slots).reshape(n * rows, -1)))
    out_b = flip(out_a, "ctx", 1)

    project = dot(normed_one, qkv_whole)
    project = project + b_qkv[0].reshape(-1)
    project = project.reshape(count, heads + 2, HD)
    queries = rotary(project[:, :heads], cos_table[:, None], sin_table[:, None]).astype(BF)
    key_local = rotary(project[:, heads], cos_table, sin_table).astype(BF)
    value_local = project[:, heads + 1].astype(BF)
    local_pair = jnp.stack([key_local, value_local])
    pairs_all = [local_pair] + [flip(local_pair, "ctx", j) for j in range(1, ctx_size)]
    pair_x = over_x(pair_block)
    grad_natural = lax.all_gather(
        after(grad_half, project), ("fsdp", "tp"), axis=0, tiled=True
    ).reshape(n, 2, h, width)
    key_rows = jnp.concatenate([p[0] for p in pairs_all], axis=0)
    value_rows = jnp.concatenate([p[1] for p in pairs_all], axis=0)
    query_index = ctx * count + jnp.arange(count, dtype=jnp.int32)
    key_index = jnp.concatenate(
        [(ctx ^ j) * count + jnp.arange(count, dtype=jnp.int32) for j in range(ctx_size)]
    )
    first_key = query_index - positions
    allowed = (key_index[None, :] <= query_index[:, None]) & (
        key_index[None, :] >= first_key[:, None]
    )

    def attention_scores():
        scores = jnp.einsum("tgd,kd->gtk", queries, key_rows, preferred_element_type=F32) * scale
        return jnp.where(allowed[None], scores, -1e30)

    scores = attention_scores()
    peak = jnp.max(scores, axis=-1, keepdims=True)
    shifted = jnp.exp(scores - peak)
    total = jnp.sum(shifted, axis=-1, keepdims=True)
    probabilities = (shifted / total).astype(BF)
    log_total = peak + jnp.log(total)
    attended = jnp.einsum("gtk,kd->tgd", probabilities, value_rows, preferred_element_type=F32)
    attended = attended.astype(BF).reshape(count, -1)
    def features(values, weight_a, weight_b):
        return jnp.concatenate([dot_nt(values, weight_a), dot_nt(values, weight_b)], axis=1)

    branch_away = features(other_half(attended), out_a, out_b).astype(BF)
    arrived = flip(branch_away, "tp", 1)
    down_x = over_x(after(down_block, branch_away))
    branch = features(own_half(attended), out_a, out_b)
    middle = x0_half + branch + arrived.astype(F32)

    inverse_two = lax.rsqrt(jnp.mean(middle * middle, axis=-1, keepdims=True) + EPS)
    normed_two = (middle * inverse_two * gain_two).astype(BF)
    ups, downs = {}, {}
    up = down = normed_two
    away_own = flip(normed_two, "tp", 1)
    swapped = []
    for step in range(1, n):
        up, down = gather_up(up, step), gather_down(down, step)
        ups[step], downs[step] = up, down
        if n == 4:
            if step == 1:
                passed = jnp.where(z == 0, down, up)
            if step == 2:
                passed = jnp.where(z == 0, down, jnp.where(z == 3, up, downs[1]))
            if step == 3:
                passed = jnp.where(
                    z == 0, down, jnp.where(z == 3, up, jnp.where(z == 1, downs[2], ups[2]))
                )
            swapped.append(flip(passed, "tp", 1))
    own_slots = slots_of(normed_two, ups, downs)
    if n == 4:
        one, two, three = swapped
        away_slots = [
            away_own,
            jnp.where(z == 0, three, one),
            jnp.where((z == 0) | (z == 3), two, three),
            jnp.where(z == 0, one, jnp.where(z == 3, three, two)),
        ]
    else:
        away_slots = [away_own] + [flip(slot, "tp", 1) for slot in own_slots[1:]]
    normed_all = jnp.concatenate(own_slots + away_slots)
    grad_slots = [pick(grad_natural, (z - k) % n) for k in range(n)]
    grad_all = jnp.concatenate(
        [pick(slot, y) for slot in grad_slots] + [pick(slot, 1 - y) for slot in grad_slots]
    )
    pair_blocks = over_cores(pair_x)
    down_blocks = over_cores(down_x)
    activated, grad_pair, pair_whole, down_whole = hidden_pass(
        normed_all, grad_all, pair_blocks, down_blocks, tile
    )

    own_tokens = n * h
    away = dot_nt(grad_pair[own_tokens:], pair_whole).astype(BF).reshape(n, h, width)
    low = z < n // 2
    early = jnp.where(low, 1, n - 1)
    if n == 4:
        y_early = flip(pick(away, early), "tp", 1)
        y_mid = flip(after(away[2], y_early), "tp", 1)
        y_late = flip(after(pick(away, n - early), y_mid), "tp", 1)
        y_own = flip(after(away[0], y_late), "tp", 1)
        crossed = [y_own, jnp.where(low, y_early, y_late), y_mid, jnp.where(low, y_late, y_early)]
    else:
        crossed = [flip(away[k], "tp", 1) for k in range(n)]
        y_early = y_mid = y_late = y_own = crossed[0]
    kept = dot_nt(grad_pair[:own_tokens], pair_whole).reshape(n, h, width)

    def term(k):
        return kept[k] + crossed[k].astype(F32)

    def turned(left, right, part, *earlier):
        columns = left[:, half_d:] if part else left[:, :half_d]
        if earlier:
            columns = after(columns, *earlier)
        return dot_tn(columns, right)

    down_core = flip(turned(grad_all, activated, 1, away).astype(BF), "ctx", 1)
    pair_core = flip(turned(normed_all, grad_pair, 1, away).astype(BF), "ctx", 1)
    down_kept = turned(grad_all, activated, 0, y_early)
    pair_kept = turned(normed_all, grad_pair, 0, y_early)
    down_total = split_x(after(down_kept, y_mid) + down_core.astype(F32))
    pair_total = split_x(after(pair_kept, y_mid) + pair_core.astype(F32))
    act_late = after(activated, *pair_total)
    result_away = dot_nt(act_late[own_tokens:], down_whole).astype(BF)

    if n == 4:
        up = sum_up(kept[1] + y_early.astype(F32), 1)
        down = sum_down(kept[3] + y_early.astype(F32), 1)
        up, down = up.astype(F32) + term(2), down.astype(F32) + term(2)
        up, down = sum_up(up, 2), sum_down(down, 2)
        up, down = up.astype(F32) + term(3), down.astype(F32) + term(1)
        up, down = after(up, *down_total, *pair_total), after(down, *down_total, *pair_total)
        up, down = sum_up(up, 3), sum_down(down, 3)
        grad_normed_two = term(0) + up.astype(F32) + down.astype(F32)
    else:
        grad_normed_two = chain_sum([term(k) for k in range(n)])
    result_crossed = flip(after(result_away, y_own), "tp", 1).reshape(n, h, width)

    scaled = grad_normed_two * gain_two
    gain_two_grad = jnp.sum(grad_normed_two * middle * inverse_two, axis=0)
    grad_middle = (
        inverse_two * scaled
        - middle * inverse_two**3 * jnp.mean(scaled * middle, axis=-1, keepdims=True)
        + grad_half.astype(F32)
    )
    out_in = both_halves(after(grad_middle.astype(BF), result_away))

    def deal_rows(total, *earlier):
        return deal(after(total.astype(BF), *earlier).reshape(n, rows, total.shape[1]), "fsdp")

    down_dealt = deal_rows(join_x(down_total, grad_normed_two))
    out_away = turned(out_in, attended, 1).astype(BF)
    out_core = flip(out_away, "ctx", 1)
    result_kept = dot_nt(after(activated, grad_middle)[:own_tokens], down_whole)
    result_kept = result_kept.reshape(n, h, width)
    result_sums = result_kept + result_crossed.astype(F32)

    out_in_late = after(out_in, out_away)
    grad_heads = dot(out_in_late[:, :half_d], out_a) + dot(out_in_late[:, half_d:], out_b)
    grad_heads = grad_heads.astype(BF).reshape(count, heads, HD)
    exact = jnp.exp(attention_scores() - log_total)
    grad_probs = jnp.einsum("tgd,kd->gtk", grad_heads, value_rows, preferred_element_type=F32)
    grad_scores = exact * (grad_probs - jnp.sum(exact * grad_probs, axis=-1, keepdims=True))
    grad_scores = grad_scores.astype(BF)
    pair_dealt = deal_rows(join_x(pair_total, grad_heads), down_dealt)
    grad_queries = (
        jnp.einsum("gtk,kd->tgd", grad_scores, key_rows, preferred_element_type=F32) * scale
    )
    grad_key_rows = (
        jnp.einsum("gtk,tgd->kd", grad_scores, queries, preferred_element_type=F32) * scale
    )
    grad_value_rows = jnp.einsum(
        "gtk,tgd->kd", exact.astype(BF), grad_heads, preferred_element_type=F32
    )
    grad_pairs = jnp.stack([grad_key_rows, grad_value_rows]).reshape(2, ctx_size, count, HD)
    grad_kv = grad_pairs[:, 0]
    moved = [flip(grad_pairs[:, j].astype(BF), "ctx", j) for j in range(1, ctx_size)]
    out_total = turned(out_in, attended, 0, *[grad_pairs]) + out_core.astype(F32)
    out_total = split_x(out_total)
    for part in moved:
        grad_kv = grad_kv + after(part, *out_total).astype(F32)
    result_rows = jnp.stack([pick(result_sums, (z - b) % n) for b in range(n)]).astype(BF)
    result_terms = deal(after(result_rows, pair_dealt), "fsdp")
    residual = (middle + jnp.sum(result_terms.astype(F32), axis=0)).astype(BF)
    grad_project = (
        jnp.concatenate(
            [
                rotary_back(grad_queries, cos_table[:, None], sin_table[:, None]),
                rotary_back(grad_kv[0], cos_table, sin_table)[:, None],
                grad_kv[1][:, None],
            ],
            axis=1,
        )
        .astype(BF)
        .reshape(count, -1)
    )
    qkv_away = turned(normed_placed, grad_project, 1).astype(BF)
    qkv_core = flip(qkv_away, "ctx", 1)
    qkv_kept = turned(normed_placed, grad_project, 0, qkv_away)
    partial_one = dot_nt(after(grad_project, qkv_kept), qkv_whole).astype(BF)
    arrived_one = flip(partial_one, "tp", 1)
    qkv_total = split_x(qkv_kept + qkv_core.astype(F32))
    out_grad = add_z(join_x(out_total), result_terms)
    qkv_joined = join_x(qkv_total)
    if n == 4:
        qkv_parts = qkv_joined.reshape(n, rows, -1)
        qkv_grad = pick(qkv_parts, z)
        for k in range(1, n):
            sent = pick(qkv_parts, (z + k) % n).astype(BF)
            qkv_grad = qkv_grad + rotate(sent, "fsdp", k).astype(F32)
    else:
        qkv_grad = add_z(qkv_joined)
    arrived_one = after(arrived_one, *qkv_total)
    output = dot_nt(both_halves(residual), place).astype(BF)

    bias_grad = jnp.sum(grad_project, axis=0, dtype=F32)
    grad_normed_one = partial_one.astype(F32) + arrived_one.astype(F32)
    scaled = grad_normed_one * norm_in
    gain_one_grad = jnp.sum(grad_normed_one * x0 * inverse_one, axis=0)
    grad_tokens = (
        inverse_one * scaled
        - x0 * inverse_one**3 * jnp.mean(scaled * x0, axis=-1, keepdims=True)
        + dot_nt(out_in, place)
    )

    def natural_columns(parts):
        whole = jnp.concatenate([parts[b] for b in range(n)], axis=1)
        return whole[:, :hidden].astype(F32)

    def every_second(parts, which):
        return jnp.concatenate(
            [
                parts[:, :, s : s + tile]
                for s in range(which * tile, 2 * piece, 2 * tile)
            ],
            axis=2,
        )

    down_grad = natural_columns(after(down_dealt, grad_project))
    pair_late = after(pair_dealt, grad_project)
    pair_grad = jnp.stack([natural_columns(every_second(pair_late, c)) for c in range(2)], axis=1)

    gain_two_pair = sum_everywhere(after(gain_two_grad[None], out_in), ("tp",))
    small = jnp.concatenate(
        [gain_one_grad[None], bias_grad[None], to_natural(gain_two_pair)], axis=1
    )
    small_all = sum_everywhere(small, ("ctx", "fsdp"))
    return (
        output,
        grad_tokens,
        small_all[:, :width],
        qkv_grad.reshape(1, rows, 1, -1),
        small_all[:, width:-width].reshape(1, 1, -1),
        out_grad[None],
        small_all[:, -width:],
        pair_grad[None],
        down_grad[None],
    )


def solution(mesh):
    rows = ("fsdp", "ctx")
    in_specs = (
        P(rows, None),
        P(rows, None),
        P(),
        P(None, rows, "tp", None),
        P(None, "tp", None),
        P(None, rows, "tp"),
        P(),
        P(None, rows, None, "tp"),
        P(None, rows, "tp"),
        P(rows),
        P(rows),
    )
    out_specs = (
        P(rows, None),
        P(rows, None),
        P(),
        P(None, rows, "tp", None),
        P(None, "tp", None),
        P(None, rows, "tp"),
        P(),
        P(None, rows, None, "tp"),
        P(None, rows, "tp"),
    )
    return jax.shard_map(body, mesh=mesh, in_specs=in_specs, out_specs=out_specs, check_vma=False)
```

```python
import jax
import jax.numpy as jnp
from jax import lax
from jax.experimental import pallas as pl
from jax.experimental.pallas import tpu as pltpu
from jax.sharding import PartitionSpec as P

HD = 128
EPS = 1e-06
THETA = 1000000.0
BF = jnp.bfloat16
F32 = jnp.float32


def angle_tables(positions):
    exponent = jnp.arange(HD // 2, dtype=F32) * (2.0 / HD)
    inverse = THETA ** (-exponent)
    phase_angle = positions.astype(F32)[:, None] * inverse[None, :]
    phase_angle = jnp.concatenate([phase_angle, phase_angle], axis=-1)
    return (jnp.cos(phase_angle), jnp.sin(phase_angle))


def rotary(vectors, cos_table, sin_table):
    half_width = vectors.shape[-1] // 2
    turned = jnp.concatenate([-vectors[..., half_width:], vectors[..., :half_width]], axis=-1)
    return vectors * cos_table + turned * sin_table


def rotary_back(gradient, cos_table, sin_table):
    scaled = gradient * sin_table
    half_width = gradient.shape[-1] // 2
    turned = jnp.concatenate([scaled[..., half_width:], -scaled[..., :half_width]], axis=-1)
    return gradient * cos_table + turned


def dot(left, right):
    return jnp.dot(left, right, preferred_element_type=F32)


def dot_nt(left, right):
    return lax.dot_general(left, right, (((1,), (1,)), ((), ())), preferred_element_type=F32)


def dot_tn(left, right):
    return lax.dot_general(left, right, (((0,), (0,)), ((), ())), preferred_element_type=F32)


def after(value, *earlier):
    return lax.optimization_barrier((value,) + earlier)[0]


def together(*values):
    return lax.optimization_barrier(values)


def segment(ready, work, *operands):
    shapes = jax.eval_shape(work, *operands)

    def skip(*operands):
        return jax.tree.map(lambda leaf: jnp.zeros(leaf.shape, leaf.dtype), shapes)

    return lax.cond(ready, work, skip, *operands)


def rotate(block, axis, distance):
    n = lax.axis_size(axis)
    return lax.ppermute(block, axis, [(i, (i + distance) % n) for i in range(n)])


def flip(block, axis, bit):
    n = lax.axis_size(axis)
    return lax.ppermute(block, axis, [(i, i ^ bit) for i in range(n)])


def pick(pieces, index):
    return lax.dynamic_index_in_dim(pieces, index, axis=0, keepdims=False)


def in_order(slots):
    n = len(slots)
    z = lax.axis_index("fsdp")
    if n <= 4:
        return jnp.stack([lax.select_n((z - b) % n, *slots) for b in range(n)])
    whole = jnp.zeros((n,) + slots[0].shape, slots[0].dtype)
    for k, slot in enumerate(slots):
        whole = lax.dynamic_update_index_in_dim(whole, slot, (z - k) % n, axis=0)
    return whole


def deal(blocks, axis):
    return lax.all_to_all(blocks, axis, 0, 0, tiled=True)


def gather_up(block, s):
    n = lax.axis_size("fsdp")
    return lax.ppermute(block, "fsdp", [(i, i + 1) for i in range(s - 1, n - 1)])


def gather_down(block, s):
    n = lax.axis_size("fsdp")
    return lax.ppermute(block, "fsdp", [(i, i - 1) for i in range(1, n - s + 1)])


def slots_of(own, ups, downs):
    n = lax.axis_size("fsdp")
    z = lax.axis_index("fsdp")
    return [own] + [jnp.where(z >= k, ups[k], downs[n - k]) for k in range(1, n)]


def sum_up(block, s):
    n = lax.axis_size("fsdp")
    return lax.ppermute(block.astype(BF), "fsdp", [(i, i + 1) for i in range(s)])


def sum_down(block, s):
    n = lax.axis_size("fsdp")
    return lax.ppermute(block.astype(BF), "fsdp", [(i, i - 1) for i in range(n - s, n)])


def chain_sum(sums, *earlier):
    n = len(sums)
    up, down = sums[1], sums[n - 1]
    if earlier:
        up, down = after(up, *earlier), after(down, *earlier)
    for s in range(1, n):
        up, down = sum_up(up, s), sum_down(down, s)
        if s < n - 1:
            up = sums[s + 1] + up.astype(F32)
            down = sums[n - s - 1] + down.astype(F32)
    return sums[0] + up.astype(F32) + down.astype(F32)


def put_rows(parts, whole):
    rows = parts[0].shape[0]
    for b, part in enumerate(parts):
        whole[b * rows : (b + 1) * rows, :] = part[...]


def hidden_step(x_ref, g_ref, pair_ref, down_ref, act_ref, grad_ref):
    tile = down_ref.shape[1]
    chunk = min(512, x_ref.shape[0])
    for start in range(0, x_ref.shape[0], chunk):
        here = pl.ds(start, chunk)
        both = dot(x_ref[here, :], pair_ref[...])
        grad = dot(g_ref[here, :], down_ref[...])
        gate, upward = both[:, :tile], both[:, tile:]
        sigma = 1.0 / (1.0 + jnp.exp(-gate))
        silu = gate * sigma
        act_ref[here, :] = (silu * upward).astype(BF)
        grad_ref[here, :tile] = (grad * upward * sigma * (1.0 + gate * (1.0 - sigma))).astype(BF)
        grad_ref[here, tile:] = (grad * silu).astype(BF)


def put_weights(parts, early, refs, pair_ref, down_ref):
    refs = list(refs)
    step = pl.program_id(0)
    for b, apart in enumerate(parts):
        down, pair = refs.pop(0), refs.pop(0)
        rows = slice(b * down.shape[0], (b + 1) * down.shape[0])
        down_ref[rows, :] = down[...]
        if not apart:
            pair_ref[rows, :] = pair[...]
            continue
        first = refs.pop(0)
        pair_ref[rows, :] = jnp.where(step < early, first[...], pair[...])


def hidden_kernel(parts, early, x_ref, g_ref, *refs):
    act_ref, grad_ref, pair_ref, down_ref = refs[-4:]
    put_weights(parts, early, refs[:-4], pair_ref, down_ref)
    hidden_step(x_ref, g_ref, pair_ref, down_ref, act_ref, grad_ref)


def hidden_kernel_four(parts, early, place_ref, *refs):
    own, ups, downs = refs[0], refs[1:4], refs[4:7]
    away_own, one, two, three, natural = refs[7:12]
    act_ref, grad_ref, pair_ref, down_ref, x_ref, g_ref, natural_ref = refs[-7:]
    z, y = place_ref[0], place_ref[1]
    h = own.shape[0]
    step = pl.program_id(0)

    def natural_rows(slot):
        index = lax.rem(z + 4 - slot % 4, 4) * 2 + lax.rem(y + slot // 4, 2)
        return pl.ds(pl.multiple_of(index * h, h), h)

    @pl.when(step == 0)
    def _():
        x_ref[:h, :] = own[...]
        for k in range(1, 4):
            x_ref[k * h : (k + 1) * h, :] = jnp.where(z >= k, ups[k - 1][...], downs[3 - k][...])
        x_ref[4 * h : 5 * h, :] = away_own[...]
        x_ref[5 * h : 6 * h, :] = jnp.where(z == 0, three[...], one[...])
        x_ref[6 * h : 7 * h, :] = jnp.where((z == 0) | (z == 3), two[...], three[...])
        last = jnp.where(z == 3, three[...], two[...])
        x_ref[7 * h :, :] = jnp.where(z == 0, one[...], last)
        for slot in range(8):
            g_ref[slot * h : (slot + 1) * h, :] = natural[natural_rows(slot), :]

    put_weights(parts, early, refs[12:-7], pair_ref, down_ref)
    hidden_step(x_ref, g_ref, pair_ref, down_ref, act_ref, grad_ref)
    for slot in range(8):
        natural_ref[natural_rows(slot), :] = act_ref[slot * h : (slot + 1) * h, :]


def hidden_pass(place, tokens, grads, blocks, early, piece, tile):
    count, width = grads.shape
    four = place is not None
    rows = count if four else min(1024, count)
    weights, weight_specs = [], []

    def at(shape, index):
        return pl.BlockSpec(shape, lambda t, r: (0, index(t)))

    for block in blocks:
        (down, d_from), (pair, p_from) = block[:2]
        depth = down.shape[0]
        base = early if len(block) > 2 else 0
        weights += [down, pair]
        weight_specs.append(at((depth, tile), lambda t, first=d_from // tile: first + t))
        weight_specs.append(
            at(
                (depth, 2 * tile),
                lambda t, first=p_from // (2 * tile), base=base: first + jnp.maximum(t - base, 0),
            )
        )
        if base:
            weights.append(block[2][0])
            weight_specs.append(
                at(
                    (depth, 2 * tile),
                    lambda t, first=block[2][1] // (2 * tile): first + jnp.minimum(t, early - 1),
                )
            )
    parts = [len(block) > 2 and early > 0 for block in blocks]
    out_specs = [
        pl.BlockSpec((rows, tile), lambda t, r: (r, t)),
        pl.BlockSpec((rows, 2 * tile), lambda t, r: (r, t)),
        pl.BlockSpec((width, 2 * tile), lambda t, r: (0, t)),
        pl.BlockSpec((width, tile), lambda t, r: (0, t)),
    ]
    out_shape = [
        jax.ShapeDtypeStruct((count, piece), BF),
        jax.ShapeDtypeStruct((count, 2 * piece), BF),
        jax.ShapeDtypeStruct((width, 2 * piece), BF),
        jax.ShapeDtypeStruct((width, piece), BF),
    ]
    if four:
        kernel, operands = hidden_kernel_four, [place] + list(tokens) + [grads]
        in_specs = [pl.BlockSpec(memory_space=pltpu.SMEM)]
        for array in operands[1:]:
            in_specs.append(
                pl.BlockSpec(array.shape, lambda t, r: (0, 0), pipeline_mode=pl.Buffered(1))
            )
        out_specs += [pl.BlockSpec((count, width), lambda t, r: (0, 0))] * 2
        out_shape += [jax.ShapeDtypeStruct((count, width), BF)] * 2
        out_specs.append(pl.BlockSpec((rows, tile), lambda t, r: (r, t)))
        out_shape.append(jax.ShapeDtypeStruct((count, piece), BF))
    else:
        kernel, operands = hidden_kernel, [tokens, grads]
        in_specs = [pl.BlockSpec((rows, width), lambda t, r: (r, 0))] * 2
    outs = pl.pallas_call(
        lambda *refs: kernel(parts, early, *refs),
        grid=(piece // tile, count // rows),
        in_specs=in_specs + weight_specs,
        out_specs=out_specs,
        out_shape=out_shape,
        compiler_params=pltpu.CompilerParams(vmem_limit_bytes=60 * 2**20),
        cost_estimate=pl.CostEstimate(
            flops=6 * count * width * piece,
            bytes_accessed=2 * (4 * count * width + 6 * width * piece + 3 * count * piece),
            transcendentals=count * piece,
        ),
    )(*operands, *weights)
    return outs if four else list(outs) + [tokens, grads, None]


def add_z(total, *earlier):
    n = lax.axis_size("fsdp")
    if earlier:
        total = after(total, *earlier)
    parts = deal(total.astype(BF).reshape(n, total.shape[0] // n, total.shape[1]), "fsdp")
    return jnp.sum(parts.astype(F32), axis=0)


def sum_everywhere(vector, axes):
    for axis in axes:
        bit = 1
        while bit < lax.axis_size(axis):
            vector = vector + flip(vector, axis, bit)
            bit *= 2
    return vector


def body(
    tokens,
    cotangent,
    norm_in,
    w_qkv,
    b_qkv,
    w_out,
    norm_mid,
    w_gate_up,
    w_down,
    segments,
    positions,
):
    n, ctx_size = lax.axis_size("fsdp"), lax.axis_size("ctx")
    z, ctx, y = lax.axis_index("fsdp"), lax.axis_index("ctx"), lax.axis_index("tp")
    count, width = tokens.shape
    h = count // 2
    rows = w_qkv.shape[1]
    heads = w_qkv.shape[3] // HD - 2
    hidden = w_down.shape[2]
    piece = -(-hidden // (n * HD)) * HD
    scale = HD ** (-0.5)

    order = [0]
    bit = ctx_size // 2
    while bit:
        order = order + [j ^ bit for j in order]
        bit //= 2

    def one_hot():
        at = jnp.arange(width, dtype=jnp.int32)
        block = sum(jnp.where(at // (n * rows) == b, ctx ^ j, 0) for b, j in enumerate(order))
        layer = (at // rows) % n
        source = (layer * ctx_size + block) * rows + at % rows
        return (jnp.arange(width, dtype=jnp.int32)[:, None] == source[None, :]).astype(BF)

    def to_relative(values):
        parts = values.reshape(values.shape[0], n, ctx_size, rows)
        picked = [
            lax.dynamic_index_in_dim(parts, ctx ^ j, axis=2, keepdims=False) for j in order
        ]
        return jnp.stack(picked, axis=1).reshape(values.shape)

    def to_natural(values):
        parts = values.reshape(values.shape[0], ctx_size, n, rows)
        where = [order.index(j) for j in range(ctx_size)]
        stacked = jnp.stack([parts[:, place] for place in where], axis=1)
        natural = [
            lax.dynamic_index_in_dim(stacked, ctx ^ j, axis=1, keepdims=False)
            for j in range(ctx_size)
        ]
        return jnp.stack(natural, axis=2).reshape(values.shape)

    def own_half(values):
        return lax.dynamic_slice_in_dim(values, y * h, h, axis=0)

    def other_half(values):
        return lax.dynamic_slice_in_dim(values, (1 - y) * h, h, axis=0)

    def both_halves(own):
        other = flip(own, "tp", 1)
        return jnp.where(
            y == 0, jnp.concatenate([own, other], axis=0), jnp.concatenate([other, own], axis=0)
        )

    half_d = width // 2
    ready = norm_in[0, 0] == norm_in[0, 0]
    qkv_whole = lax.all_gather(w_qkv[0].reshape(rows, -1), ("fsdp", "ctx"), axis=0, tiled=True)
    out_slots = [w_out[0]] + [rotate(w_out[0], "fsdp", k) for k in range(1, n)]

    tile = 3 * HD if piece % (3 * HD) == 0 else HD
    pad = n * piece - hidden

    def lay_out(w_gate_up, w_down):
        gate_rows = jnp.pad(w_gate_up[0, :, 0], ((0, 0), (0, pad)))
        up_rows = jnp.pad(w_gate_up[0, :, 1], ((0, 0), (0, pad)))
        down_rows = jnp.pad(w_down[0], ((0, 0), (0, pad)))
        pair_out, down_out = [], []
        for index in range(n):
            columns = []
            for start in range(index * piece, (index + 1) * piece, tile):
                columns += [gate_rows[:, start : start + tile], up_rows[:, start : start + tile]]
            pair_out.append(jnp.concatenate(columns, axis=1))
            down_out.append(down_rows[:, index * piece : (index + 1) * piece])
        return jnp.stack(pair_out), jnp.stack(down_out)

    pair_out, down_out = lay_out(w_gate_up, w_down)
    pair_block = deal(pair_out, "fsdp").reshape(n * rows, 2 * piece)

    def prepare(tokens, cotangent, norm_in, norm_mid, positions):
        x0 = tokens.astype(F32)
        inverse_one = lax.rsqrt(jnp.mean(x0 * x0, axis=-1, keepdims=True) + EPS)
        normed_one = (x0 * inverse_one * norm_in).astype(BF)
        place = one_hot()
        placed = dot(jnp.concatenate([own_half(tokens), cotangent, normed_one]), place)
        grad_half = own_half(placed[h : h + count].astype(BF))
        normed_placed = placed[h + count :].astype(BF)
        cos_table, sin_table = angle_tables(positions)
        gain_two = to_relative(norm_mid)
        return inverse_one, normed_one, place, placed[:h], grad_half, normed_placed, gain_two, cos_table, sin_table

    x0 = tokens.astype(F32)
    (
        inverse_one,
        normed_one,
        place,
        x0_half,
        grad_half,
        normed_placed,
        gain_two,
        cos_table,
        sin_table,
    ) = prepare(tokens, cotangent, norm_in, norm_mid, positions)

    def over_x(piece_rows):
        held = [piece_rows]
        bit = ctx_size // 2
        while bit > 1:
            held = held + [flip(part, "ctx", bit) for part in held]
            bit //= 2
        return held

    def over_cores(held):
        return held + [flip(part, "ctx", 1) for part in held]

    out_x = over_x(in_order(out_slots).reshape(n * rows, -1))
    out_a = jnp.concatenate(out_x)
    out_b = flip(out_a, "ctx", 1)

    query_index = ctx * count + jnp.arange(count, dtype=jnp.int32)
    key_index = jnp.concatenate(
        [(ctx ^ j) * count + jnp.arange(count, dtype=jnp.int32) for j in range(ctx_size)]
    )
    first_key = query_index - positions
    allowed = (key_index[None, :] <= query_index[:, None]) & (
        key_index[None, :] >= first_key[:, None]
    )
    grad_natural = lax.all_gather(grad_half, ("fsdp", "tp"), axis=0, tiled=True)

    def by_features(values, weight):
        return jnp.concatenate(
            [dot_nt(values, weight[:half_d]), dot_nt(values, weight[half_d:])], axis=1
        )

    def attention_scores(queries, key_rows):
        scores = jnp.einsum("tgd,kd->gtk", queries, key_rows, preferred_element_type=F32) * scale
        return jnp.where(allowed[None], scores, -1e30)

    def project_all(normed_one, qkv_whole):
        project = dot(normed_one, qkv_whole) + b_qkv[0].reshape(-1)
        project = project.reshape(count, heads + 2, HD)
        queries = rotary(project[:, :heads], cos_table[:, None], sin_table[:, None]).astype(BF)
        key_local = rotary(project[:, heads], cos_table, sin_table).astype(BF)
        value_local = project[:, heads + 1].astype(BF)
        local_pair = jnp.stack([key_local, value_local])
        pairs_all = [local_pair] + [flip(local_pair, "ctx", j) for j in range(1, ctx_size)]
        key_rows = jnp.concatenate([p[0] for p in pairs_all], axis=0)
        value_rows = jnp.concatenate([p[1] for p in pairs_all], axis=0)
        return queries, key_rows, value_rows

    def attend(queries, key_rows, value_rows, out_whole):
        scores = attention_scores(queries, key_rows)
        peak = jnp.max(scores, axis=-1, keepdims=True)
        shifted = jnp.exp(scores - peak)
        total = jnp.sum(shifted, axis=-1, keepdims=True)
        probabilities = (shifted / total).astype(BF)
        log_total = peak + jnp.log(total)
        attended = jnp.einsum("gtk,kd->tgd", probabilities, value_rows, preferred_element_type=F32)
        attended = attended.astype(BF).reshape(count, -1)
        branch_away = by_features(other_half(attended), out_whole).astype(BF)
        arrived = flip(branch_away, "tp", 1)
        branch = by_features(own_half(after(attended, branch_away)), out_whole)
        middle = x0_half + branch + arrived.astype(F32)
        inverse_two = lax.rsqrt(jnp.mean(middle * middle, axis=-1, keepdims=True) + EPS)
        normed_two = (middle * inverse_two * gain_two).astype(BF)
        return log_total, attended, middle, inverse_two, normed_two

    out_whole = jnp.concatenate([out_a, out_b])
    queries, key_rows, value_rows = segment(
        ready, project_all, after(normed_one, out_whole), qkv_whole
    )
    early = piece // tile // 2
    cut_at = early * 2 * tile
    down_block = deal(after(down_out, value_rows), "fsdp").reshape(n * rows, piece)
    pair_late = after(pair_block[:, cut_at:], value_rows)
    pair_x = flip(pair_late, "ctx", ctx_size // 2)
    pair_core = flip(after(pair_block, value_rows), "ctx", 1)
    log_total, attended, middle, inverse_two, normed_two = segment(
        ready, attend, queries, key_rows, value_rows, out_whole
    )

    second_out = jnp.concatenate([pair_block[:, :cut_at], down_block], axis=1)
    second_x = flip(after(second_out, normed_two), "ctx", ctx_size // 2)

    def gather_first(block):
        away_own = flip(block, "tp", 1)
        ups, downs, swapped = [block], [block], []
        for step in range(1, n - 1):
            up, down = together(gather_up(ups[-1], step), gather_down(downs[-1], step))
            ups.append(up)
            downs.append(down)
            if n == 4 and step == 1:
                swapped.append(flip(jnp.where(z == 0, down, up), "tp", 1))
        return away_own, ups[1:], downs[1:], swapped

    def gather_last(block, ups, downs):
        if n == 4:
            two = jnp.where(z == 0, downs[1], jnp.where(z == 3, ups[1], downs[0]))
            two = flip(two, "tp", 1)
        up, down = gather_up(ups[-1], n - 1), gather_down(downs[-1], n - 1)
        if n == 4:
            up, down, two = together(up, down, two)
            three = jnp.where(
                z == 0, down, jnp.where(z == 3, up, jnp.where(z == 1, downs[1], ups[1]))
            )
            return up, down, [two, flip(three, "tp", 1)]
        ups = dict(enumerate(list(ups) + [up], start=1))
        downs = dict(enumerate(list(downs) + [down], start=1))
        own_slots = slots_of(block, ups, downs)
        gathered = own_slots + [flip(slot, "tp", 1) for slot in own_slots[1:]]
        return up, down, gathered

    away_own, ups, downs, swapped = segment(ready, gather_first, normed_two)
    second_x = after(second_x, ups[-1])
    second_core = flip(second_x, "ctx", 1)
    pair_x_core = flip(after(pair_x, ups[-1]), "ctx", 1)
    down_core = flip(after(down_block, ups[-1]), "ctx", 1)
    up, down, gathered = segment(ready, gather_last, normed_two, ups, downs)
    blocks = [
        [(down_block, 0), (pair_block, 0)],
        [(second_x, cut_at), (pair_x, 0), (second_x, 0)],
        [(down_core, 0), (pair_core, 0)],
        [(second_core, cut_at), (pair_x_core, 0), (second_core, 0)],
    ]
    if n == 4:
        spot = jnp.stack([z, y]).astype(jnp.int32)
        arrivals = [normed_two, *ups, up, *downs, down, away_own, swapped[0], *gathered]
        operands = (spot, arrivals, grad_natural)
    else:
        normed_all = jnp.concatenate(gathered[:n] + [away_own] + gathered[n:])
        by_slot = grad_natural.reshape(n, 2, h, width)
        by_slot = [pick(by_slot, (z - k) % n) for k in range(n)]
        grad_all = jnp.concatenate(
            [pick(slot, y) for slot in by_slot] + [pick(slot, 1 - y) for slot in by_slot]
        )
        operands = (None, normed_all, grad_all)
    activated, grad_pair, pair_whole, down_whole, normed_all, grad_all, act_natural = hidden_pass(
        *operands, blocks, early, piece, tile
    )

    own_tokens = n * h
    ctx_half, ctx_own = width // 2, width // ctx_size

    def core_term(left, right):
        return dot_tn(left[:, ctx_half:], right).astype(BF)

    def x_terms(left, right, arrived):
        terms = []
        for start in range(ctx_own, ctx_half, ctx_own):
            term = dot_tn(left[:, start : start + ctx_own], right)
            terms.append((term + arrived[start : start + ctx_own].astype(F32)).astype(BF))
        return terms

    def to_x(terms):
        return [flip(term, "ctx", j) for term, j in zip(terms, order[1:], strict=False)]

    def own_rows(left, right, arrived, moved):
        total = dot_tn(left[:, :ctx_own], right) + arrived[:ctx_own].astype(F32)
        for part in moved:
            total = total + part.astype(F32)
        return total

    def deal_rows(total):
        return deal(total.astype(BF).reshape(n, rows, total.shape[1]), "fsdp")

    def add_rows(total):
        if n != 4:
            return add_z(total)
        parts = total.reshape(n, rows, total.shape[1])
        out = pick(parts, z)
        for k in range(1, n):
            out = out + rotate(pick(parts, (z + k) % n).astype(BF), "fsdp", k).astype(F32)
        return out

    away = by_features(grad_pair[own_tokens:], pair_whole).astype(BF).reshape(n, h, width)
    low = z < n // 2
    early = jnp.where(low, 1, n - 1)
    leaving = pick(away, early)

    def beside_first(grad_pair, activated, grad_all, pair_whole):
        kept = by_features(grad_pair[:own_tokens], pair_whole).reshape(n, h, width)
        return kept, core_term(grad_all, activated)

    def result_terms(activated, down_whole):
        return by_features(activated, down_whole).astype(BF)

    def result_order(result):
        result = result.reshape(2, n, h, width)
        by_y = jnp.where(y == 0, result, result[::-1])
        by_z = jnp.stack([by_y[:, k] for k in range(n)])
        return jnp.stack([pick(by_z, (z - b) % n) for b in range(n)]).reshape(-1, width)

    y_early = flip(leaving, "tp", 1)
    pair_leaving = segment(ready, core_term, after(normed_all, leaving), grad_pair)
    pair_core = flip(pair_leaving, "ctx", 1)
    kept, down_leaving = segment(
        ready,
        beside_first,
        after(grad_pair, pair_leaving),
        activated,
        grad_all,
        pair_whole,
    )
    if n == 4:
        y_early = after(y_early, kept)
        acc_up = (kept[1] + y_early.astype(F32)).astype(BF)
        acc_down = (kept[3] + y_early.astype(F32)).astype(BF)
        acc_up, acc_down = together(acc_up, acc_down)
        up, down = sum_up(acc_up, 1), sum_down(acc_down, 1)
        y_mid = flip(after(away[2], acc_up), "tp", 1)
        down_core = flip(after(down_leaving, acc_up), "ctx", 1)
        pair_terms = segment(
            ready, x_terms, after(normed_all, acc_up, acc_down), grad_pair, after(pair_core, kept)
        )
        pair_moved = to_x([after(term, up, down, y_mid) for term in pair_terms])

        def rest_of_sum(kept, away, y_early, y_mid, up, down, down_core, act_natural):
            acc_up = (kept[2] + y_mid.astype(F32) + up.astype(F32)).astype(BF)
            acc_down = (kept[2] + y_mid.astype(F32) + down.astype(F32)).astype(BF)
            acc_up, acc_down = together(acc_up, acc_down)
            up, down = sum_up(acc_up, 2), sum_down(acc_down, 2)
            y_late = flip(after(pick(away, n - early), acc_up), "tp", 1)
            by_z = result_terms(after(act_natural, acc_up, acc_down), down_whole)
            up, down, y_late = together(up, down, y_late, by_z)[:3]
            crossed_three = jnp.where(low, y_late, y_early).astype(F32)
            crossed_one = jnp.where(low, y_early, y_late).astype(F32)
            acc_up = (kept[3] + crossed_three + up.astype(F32)).astype(BF)
            acc_down = (kept[1] + crossed_one + down.astype(F32)).astype(BF)
            acc_up, acc_down = together(acc_up, acc_down)
            up, down = sum_up(acc_up, 3), sum_down(acc_down, 3)
            y_own = flip(after(away[0], acc_up), "tp", 1)
            down_terms = x_terms(after(grad_all, acc_up, acc_down), activated, down_core)
            up, down, y_own = together(up, down, y_own, *down_terms)[:3]
            total = kept[0] + y_own.astype(F32) + up.astype(F32) + down.astype(F32)
            return total, by_z, down_terms

        grad_normed_two, by_z, down_terms = segment(
            ready,
            rest_of_sum,
            kept,
            away,
            y_early,
            y_mid,
            after(up, *pair_terms),
            down,
            down_core,
            act_natural,
        )
    else:
        crossed = [flip(away[k], "tp", 1) for k in range(n)]
        grad_normed_two = chain_sum([kept[k] + crossed[k].astype(F32) for k in range(n)])
        by_z = result_order(result_terms(activated, down_whole))
        down_core, pair_core = flip(down_leaving, "ctx", 1), flip(pair_leaving, "ctx", 1)
        pair_terms = x_terms(normed_all, grad_pair, pair_core)
        pair_moved = to_x(pair_terms)
        down_terms = x_terms(grad_all, activated, down_core)

    scaled = grad_normed_two * gain_two
    gain_two_grad = jnp.sum(grad_normed_two * middle * inverse_two, axis=0)
    grad_middle = (
        inverse_two * scaled
        - middle * inverse_two**3 * jnp.mean(scaled * middle, axis=-1, keepdims=True)
        + grad_half.astype(F32)
    )
    middle_half = grad_middle.astype(BF)

    result_sum = lax.psum_scatter(
        by_z, ("fsdp", "tp"), scatter_dimension=0, tiled=True
    )

    out_other = flip(middle_half, "tp", 1)

    def pair_rows(normed_all, grad_pair, pair_core, pair_moved):
        return own_rows(normed_all, grad_pair, pair_core, pair_moved).astype(BF)

    pair_total = segment(
        ready, pair_rows, after(normed_all, middle_half), grad_pair, pair_core, pair_moved
    )
    if n == 4:
        parts = pair_total.reshape(n, rows, 2 * piece)
        pair_dealt = {0: pick(parts, z)}
        for k in (1, 3):
            pair_dealt[k] = rotate(after(pick(parts, (z + k) % n), out_other), "fsdp", k)
    down_moved = to_x([after(term, pair_total, out_other) for term in down_terms])

    def attend_back(own, other, out_whole, queries, key_rows, value_rows, log_total):
        out_in = jnp.where(y == 0, jnp.concatenate([own, other]), jnp.concatenate([other, own]))
        grad_heads = dot(out_in[:, :half_d], out_whole[:half_d])
        grad_heads = grad_heads + dot(out_in[:, half_d:], out_whole[half_d:])
        grad_heads = grad_heads.astype(BF).reshape(count, heads, HD)
        exact = jnp.exp(attention_scores(queries, key_rows) - log_total)
        grad_probs = jnp.einsum("tgd,kd->gtk", grad_heads, value_rows, preferred_element_type=F32)
        grad_scores = exact * (grad_probs - jnp.sum(exact * grad_probs, axis=-1, keepdims=True))
        grad_scores = grad_scores.astype(BF)
        grad_queries = (
            jnp.einsum("gtk,kd->tgd", grad_scores, key_rows, preferred_element_type=F32) * scale
        )
        grad_key_rows = (
            jnp.einsum("gtk,tgd->kd", grad_scores, queries, preferred_element_type=F32) * scale
        )
        grad_value_rows = jnp.einsum(
            "gtk,tgd->kd", exact.astype(BF), grad_heads, preferred_element_type=F32
        )
        grad_pairs = jnp.stack([grad_key_rows, grad_value_rows]).reshape(2, ctx_size, count, HD)
        sent = [grad_pairs[:, j].astype(BF) for j in range(1, ctx_size)]
        return out_in, grad_queries, grad_pairs[:, 0], sent, core_term(out_in, attended)

    out_in, grad_queries, grad_kv, sent, out_leaving = segment(
        ready,
        attend_back,
        middle_half,
        after(out_other, pair_total),
        out_whole,
        queries,
        key_rows,
        value_rows,
        log_total,
    )
    first_way = [*down_moved] + ([pair_dealt[1], pair_dealt[3]] if n == 4 else [])
    moved = [flip(after(part, *first_way), "ctx", j) for j, part in enumerate(sent, start=1)]
    if n == 4:
        pair_dealt[2] = rotate(after(pick(parts, (z + 2) % n), *sent), "fsdp", 2)
        last_way = [pair_dealt[2]]
    else:
        pair_dealt = deal_rows(after(pair_total, *sent))
        last_way = []

    out_core = flip(after(out_leaving, *first_way), "ctx", 1)

    def down_rows(grad_all, activated, down_core, down_moved):
        return own_rows(grad_all, activated, down_core, down_moved).astype(BF)

    down_total = segment(
        ready, down_rows, after(grad_all, *sent), activated, down_core, down_moved
    )
    out_terms = x_terms(out_in, attended, after(out_core, *moved, down_total))
    out_moved = to_x(out_terms)
    if n == 4:
        parts = down_total.reshape(n, rows, piece)
        down_dealt = [pick(parts, z)]
        down_dealt += [rotate(pick(parts, (z + k) % n), "fsdp", k) for k in range(1, n)]
    else:
        down_dealt = deal_rows(down_total)

    def project_back(grad_queries, grad_kv, moved, normed_placed, qkv_whole):
        for part in moved:
            grad_kv = grad_kv + part.astype(F32)
        grad_project = (
            jnp.concatenate(
                [
                    rotary_back(grad_queries, cos_table[:, None], sin_table[:, None]),
                    rotary_back(grad_kv[0], cos_table, sin_table)[:, None],
                    grad_kv[1][:, None],
                ],
                axis=1,
            )
            .astype(BF)
            .reshape(count, -1)
        )
        away = core_term(normed_placed, grad_project)
        arrived = flip(away, "ctx", 1)
        partial_one = dot_nt(after(grad_project, away), qkv_whole).astype(BF)
        terms = x_terms(normed_placed, grad_project, after(arrived, partial_one))
        return grad_project, partial_one, arrived, terms

    grad_project, partial_one, qkv_core, qkv_terms = segment(
        ready,
        project_back,
        grad_queries,
        grad_kv,
        [after(part, *out_terms, *last_way, down_total) for part in moved],
        normed_placed,
        qkv_whole,
    )
    down_there = down_dealt[1:] if n == 4 else []
    qkv_moved = to_x([after(term, *down_there) for term in qkv_terms])
    arrived_one = flip(after(partial_one, *qkv_terms), "tp", 1)

    def natural_columns(parts):
        whole = jnp.concatenate([parts[b] for b in range(n)], axis=1)
        return whole[:, :hidden].astype(F32)

    out_total = own_rows(
        after(out_in, *qkv_terms), attended, out_core, [after(p, *qkv_terms) for p in out_moved]
    )
    out_parts = out_total.reshape(n, rows, -1)
    if n == 4:
        out_dealt = [rotate(pick(out_parts, (z + k) % n).astype(BF), "fsdp", k) for k in range(1, n)]
        out_grad = pick(out_parts, z)
        for part in out_dealt:
            out_grad = out_grad + part.astype(F32)
    else:
        out_dealt = []
        out_grad = add_z(out_total)

    def beside_x(grad_project, out_in, result_sum):
        bias_grad = jnp.sum(grad_project, axis=0, dtype=F32)
        residual = (middle + result_sum.astype(F32)).astype(BF)
        return bias_grad, dot_nt(out_in, place), residual

    bias_grad, middle_natural, residual = segment(
        ready, beside_x, after(grad_project, out_total), out_in, result_sum
    )
    residual_other = flip(residual, "tp", 1)
    qkv_moved = [after(part, bias_grad, *out_dealt) for part in qkv_moved]
    qkv_total = own_rows(normed_placed, grad_project, qkv_core, qkv_moved)
    qkv_grad = add_rows(qkv_total)
    arrived_one = after(arrived_one, qkv_total)

    def beside_z(residual, residual_other, pair_dealt, down_dealt):
        first, second = [residual, residual_other], [residual_other, residual]
        whole = jnp.where(y == 0, jnp.concatenate(first), jnp.concatenate(second))
        if n == 4:
            pair_dealt = in_order([pair_dealt[k] for k in range(n)])
            down_dealt = in_order(down_dealt)
        pair_grad = [natural_columns(every_second(pair_dealt, c)) for c in range(2)]
        output = dot_nt(whole, place).astype(BF)
        return output, jnp.stack(pair_grad, axis=1), natural_columns(down_dealt)

    def every_second(parts, which):
        return jnp.concatenate(
            [parts[:, :, s : s + tile] for s in range(which * tile, 2 * piece, 2 * tile)], axis=2
        )

    output, pair_grad, down_grad = segment(
        ready, beside_z, after(residual, qkv_total), residual_other, pair_dealt, down_dealt
    )
    grad_normed_one = partial_one.astype(F32) + arrived_one.astype(F32)
    scaled = grad_normed_one * norm_in
    gain_one_grad = jnp.sum(grad_normed_one * x0 * inverse_one, axis=0)
    grad_tokens = (
        inverse_one * scaled
        - x0 * inverse_one**3 * jnp.mean(scaled * x0, axis=-1, keepdims=True)
        + middle_natural
    )

    gain_two_pair = sum_everywhere(after(gain_two_grad[None], *sent), ("tp",))
    small = jnp.concatenate(
        [gain_one_grad[None], bias_grad[None], to_natural(gain_two_pair)], axis=1
    )
    small_all = sum_everywhere(small, ("ctx", "fsdp"))
    return (
        output,
        grad_tokens,
        small_all[:, :width],
        qkv_grad.reshape(1, rows, 1, -1),
        small_all[:, width:-width].reshape(1, 1, -1),
        out_grad[None],
        small_all[:, -width:],
        pair_grad[None],
        down_grad[None],
    )


def solution(mesh):
    rows = ("fsdp", "ctx")
    in_specs = (
        P(rows, None),
        P(rows, None),
        P(),
        P(None, rows, "tp", None),
        P(None, "tp", None),
        P(None, rows, "tp"),
        P(),
        P(None, rows, None, "tp"),
        P(None, rows, "tp"),
        P(rows),
        P(rows),
    )
    out_specs = (
        P(rows, None),
        P(rows, None),
        P(),
        P(None, rows, "tp", None),
        P(None, "tp", None),
        P(None, rows, "tp"),
        P(),
        P(None, rows, None, "tp"),
        P(None, rows, "tp"),
    )
    return jax.shard_map(body, mesh=mesh, in_specs=in_specs, out_specs=out_specs, check_vma=False)
```

```python
import jax
import jax.numpy as jnp
from jax import lax
from jax.experimental import pallas as pl
from jax.experimental.pallas import tpu as pltpu
from jax.sharding import PartitionSpec as P

HD = 128
EPS = 1e-06
THETA = 1000000.0
BF = jnp.bfloat16
F32 = jnp.float32


def angle_tables(positions):
    exponent = jnp.arange(HD // 2, dtype=F32) * (2.0 / HD)
    inverse = THETA ** (-exponent)
    phase_angle = positions.astype(F32)[:, None] * inverse[None, :]
    phase_angle = jnp.concatenate([phase_angle, phase_angle], axis=-1)
    return (jnp.cos(phase_angle), jnp.sin(phase_angle))


def rotary(vectors, cos_table, sin_table):
    half_width = vectors.shape[-1] // 2
    turned = jnp.concatenate([-vectors[..., half_width:], vectors[..., :half_width]], axis=-1)
    return vectors * cos_table + turned * sin_table


def rotary_back(gradient, cos_table, sin_table):
    scaled = gradient * sin_table
    half_width = gradient.shape[-1] // 2
    turned = jnp.concatenate([scaled[..., half_width:], -scaled[..., :half_width]], axis=-1)
    return gradient * cos_table + turned


def dot(left, right):
    return jnp.dot(left, right, preferred_element_type=F32)


def dot_nt(left, right):
    return lax.dot_general(left, right, (((1,), (1,)), ((), ())), preferred_element_type=F32)


def dot_tn(left, right):
    return lax.dot_general(left, right, (((0,), (0,)), ((), ())), preferred_element_type=F32)


def after(value, *earlier):
    return lax.optimization_barrier((value,) + earlier)[0]


def together(*values):
    return lax.optimization_barrier(values)


def segment(ready, work, *operands):
    shapes = jax.eval_shape(work, *operands)

    def skip(*operands):
        return jax.tree.map(lambda leaf: jnp.zeros(leaf.shape, leaf.dtype), shapes)

    return lax.cond(ready, work, skip, *operands)


def nothing_of(*arrays):
    total = jnp.zeros((), F32)
    for array in arrays:
        total = total + array[(0,) * array.ndim].astype(F32) * 0.0
    return total


def rotate(block, axis, distance):
    n = lax.axis_size(axis)
    return lax.ppermute(block, axis, [(i, (i + distance) % n) for i in range(n)])


def flip(block, axis, bit):
    n = lax.axis_size(axis)
    return lax.ppermute(block, axis, [(i, i ^ bit) for i in range(n)])


def pick(pieces, index):
    return lax.dynamic_index_in_dim(pieces, index, axis=0, keepdims=False)


def in_order(slots):
    n = len(slots)
    z = lax.axis_index("fsdp")
    if n <= 4:
        return jnp.stack([lax.select_n((z - b) % n, *slots) for b in range(n)])
    whole = jnp.zeros((n,) + slots[0].shape, slots[0].dtype)
    for k, slot in enumerate(slots):
        whole = lax.dynamic_update_index_in_dim(whole, slot, (z - k) % n, axis=0)
    return whole


def deal(blocks, axis):
    return lax.all_to_all(blocks, axis, 0, 0, tiled=True)


def gather_up(block, s):
    n = lax.axis_size("fsdp")
    return lax.ppermute(block, "fsdp", [(i, i + 1) for i in range(s - 1, n - 1)])


def gather_down(block, s):
    n = lax.axis_size("fsdp")
    return lax.ppermute(block, "fsdp", [(i, i - 1) for i in range(1, n - s + 1)])


def slots_of(own, ups, downs):
    n = lax.axis_size("fsdp")
    z = lax.axis_index("fsdp")
    return [own] + [jnp.where(z >= k, ups[k], downs[n - k]) for k in range(1, n)]


def sum_up(block, s):
    n = lax.axis_size("fsdp")
    return lax.ppermute(block.astype(BF), "fsdp", [(i, i + 1) for i in range(s)])


def sum_down(block, s):
    n = lax.axis_size("fsdp")
    return lax.ppermute(block.astype(BF), "fsdp", [(i, i - 1) for i in range(n - s, n)])


def chain_sum(sums, *earlier):
    n = len(sums)
    up, down = sums[1], sums[n - 1]
    if earlier:
        up, down = after(up, *earlier), after(down, *earlier)
    for s in range(1, n):
        up, down = sum_up(up, s), sum_down(down, s)
        if s < n - 1:
            up = sums[s + 1] + up.astype(F32)
            down = sums[n - s - 1] + down.astype(F32)
    return sums[0] + up.astype(F32) + down.astype(F32)


def put_rows(parts, whole):
    rows = parts[0].shape[0]
    for b, part in enumerate(parts):
        whole[b * rows : (b + 1) * rows, :] = part[...]


def hidden_step(x_ref, g_ref, pair_ref, down_ref, act_ref, grad_ref):
    tile = down_ref.shape[1]
    chunk = min(512, x_ref.shape[0])
    for start in range(0, x_ref.shape[0], chunk):
        here = pl.ds(start, chunk)
        both = dot(x_ref[here, :], pair_ref[...])
        grad = dot(g_ref[here, :], down_ref[...])
        gate, upward = both[:, :tile], both[:, tile:]
        sigma = 1.0 / (1.0 + jnp.exp(-gate))
        silu = gate * sigma
        act_ref[here, :] = (silu * upward).astype(BF)
        grad_ref[here, :tile] = (grad * upward * sigma * (1.0 + gate * (1.0 - sigma))).astype(BF)
        grad_ref[here, tile:] = (grad * silu).astype(BF)


def put_weights(parts, early, refs, pair_ref, down_ref):
    refs = list(refs)
    step = pl.program_id(0)
    for b, apart in enumerate(parts):
        down, pair = refs.pop(0), refs.pop(0)
        rows = slice(b * down.shape[0], (b + 1) * down.shape[0])
        down_ref[rows, :] = down[...]
        if not apart:
            pair_ref[rows, :] = pair[...]
            continue
        first = refs.pop(0)
        pair_ref[rows, :] = jnp.where(step < early, first[...], pair[...])


def hidden_kernel(parts, early, x_ref, g_ref, *refs):
    act_ref, grad_ref, pair_ref, down_ref = refs[-4:]
    put_weights(parts, early, refs[:-4], pair_ref, down_ref)
    hidden_step(x_ref, g_ref, pair_ref, down_ref, act_ref, grad_ref)


def hidden_kernel_four(parts, early, place_ref, *refs):
    own, ups, downs = refs[0], refs[1:4], refs[4:7]
    away_own, one, two, three, natural = refs[7:12]
    act_ref, grad_ref, pair_ref, down_ref, x_ref, g_ref, natural_ref = refs[-7:]
    z, y = place_ref[0], place_ref[1]
    h = own.shape[0]
    step = pl.program_id(0)

    def natural_rows(slot):
        index = lax.rem(z + 4 - slot % 4, 4) * 2 + lax.rem(y + slot // 4, 2)
        return pl.ds(pl.multiple_of(index * h, h), h)

    @pl.when(step == 0)
    def _():
        x_ref[:h, :] = own[...]
        for k in range(1, 4):
            x_ref[k * h : (k + 1) * h, :] = jnp.where(z >= k, ups[k - 1][...], downs[3 - k][...])
        x_ref[4 * h : 5 * h, :] = away_own[...]
        x_ref[5 * h : 6 * h, :] = jnp.where(z == 0, three[...], one[...])
        x_ref[6 * h : 7 * h, :] = jnp.where((z == 0) | (z == 3), two[...], three[...])
        last = jnp.where(z == 3, three[...], two[...])
        x_ref[7 * h :, :] = jnp.where(z == 0, one[...], last)
        for slot in range(8):
            g_ref[slot * h : (slot + 1) * h, :] = natural[natural_rows(slot), :]

    put_weights(parts, early, refs[12:-7], pair_ref, down_ref)
    hidden_step(x_ref, g_ref, pair_ref, down_ref, act_ref, grad_ref)
    for slot in range(8):
        natural_ref[natural_rows(slot), :] = act_ref[slot * h : (slot + 1) * h, :]


def hidden_pass(place, tokens, grads, blocks, early, piece, tile):
    count, width = grads.shape
    four = place is not None
    rows = count if four else min(1024, count)
    weights, weight_specs = [], []

    def at(shape, index):
        return pl.BlockSpec(shape, lambda t, r: (0, index(t)))

    for block in blocks:
        (down, d_from), (pair, p_from) = block[:2]
        depth = down.shape[0]
        base = early if len(block) > 2 else 0
        weights += [down, pair]
        weight_specs.append(at((depth, tile), lambda t, first=d_from // tile: first + t))
        weight_specs.append(
            at(
                (depth, 2 * tile),
                lambda t, first=p_from // (2 * tile), base=base: first + jnp.maximum(t - base, 0),
            )
        )
        if base:
            weights.append(block[2][0])
            weight_specs.append(
                at(
                    (depth, 2 * tile),
                    lambda t, first=block[2][1] // (2 * tile): first + jnp.minimum(t, early - 1),
                )
            )
    parts = [len(block) > 2 and early > 0 for block in blocks]
    out_specs = [
        pl.BlockSpec((rows, tile), lambda t, r: (r, t)),
        pl.BlockSpec((rows, 2 * tile), lambda t, r: (r, t)),
        pl.BlockSpec((width, 2 * tile), lambda t, r: (0, t)),
        pl.BlockSpec((width, tile), lambda t, r: (0, t)),
    ]
    out_shape = [
        jax.ShapeDtypeStruct((count, piece), BF),
        jax.ShapeDtypeStruct((count, 2 * piece), BF),
        jax.ShapeDtypeStruct((width, 2 * piece), BF),
        jax.ShapeDtypeStruct((width, piece), BF),
    ]
    if four:
        kernel, operands = hidden_kernel_four, [place] + list(tokens) + [grads]
        in_specs = [pl.BlockSpec(memory_space=pltpu.SMEM)]
        for array in operands[1:]:
            in_specs.append(
                pl.BlockSpec(array.shape, lambda t, r: (0, 0), pipeline_mode=pl.Buffered(1))
            )
        out_specs += [pl.BlockSpec((count, width), lambda t, r: (0, 0))] * 2
        out_shape += [jax.ShapeDtypeStruct((count, width), BF)] * 2
        out_specs.append(pl.BlockSpec((rows, tile), lambda t, r: (r, t)))
        out_shape.append(jax.ShapeDtypeStruct((count, piece), BF))
    else:
        kernel, operands = hidden_kernel, [tokens, grads]
        in_specs = [pl.BlockSpec((rows, width), lambda t, r: (r, 0))] * 2
    outs = pl.pallas_call(
        lambda *refs: kernel(parts, early, *refs),
        grid=(piece // tile, count // rows),
        in_specs=in_specs + weight_specs,
        out_specs=out_specs,
        out_shape=out_shape,
        compiler_params=pltpu.CompilerParams(vmem_limit_bytes=60 * 2**20),
        cost_estimate=pl.CostEstimate(
            flops=6 * count * width * piece,
            bytes_accessed=2 * (4 * count * width + 6 * width * piece + 3 * count * piece),
            transcendentals=count * piece,
        ),
    )(*operands, *weights)
    return outs if four else list(outs) + [tokens, grads, None]


def add_z(total, *earlier):
    n = lax.axis_size("fsdp")
    if earlier:
        total = after(total, *earlier)
    parts = deal(total.astype(BF).reshape(n, total.shape[0] // n, total.shape[1]), "fsdp")
    return jnp.sum(parts.astype(F32), axis=0)


def sum_everywhere(vector, axes):
    for axis in axes:
        bit = 1
        while bit < lax.axis_size(axis):
            vector = vector + flip(vector, axis, bit)
            bit *= 2
    return vector


def body(
    tokens,
    cotangent,
    norm_in,
    w_qkv,
    b_qkv,
    w_out,
    norm_mid,
    w_gate_up,
    w_down,
    segments,
    positions,
):
    n, ctx_size = lax.axis_size("fsdp"), lax.axis_size("ctx")
    z, ctx, y = lax.axis_index("fsdp"), lax.axis_index("ctx"), lax.axis_index("tp")
    count, width = tokens.shape
    h = count // 2
    rows = w_qkv.shape[1]
    heads = w_qkv.shape[3] // HD - 2
    hidden = w_down.shape[2]
    piece = -(-hidden // (n * HD)) * HD
    scale = HD ** (-0.5)

    order = [0]
    bit = ctx_size // 2
    while bit:
        order = order + [j ^ bit for j in order]
        bit //= 2

    def one_hot():
        at = jnp.arange(width, dtype=jnp.int32)
        block = sum(jnp.where(at // (n * rows) == b, ctx ^ j, 0) for b, j in enumerate(order))
        layer = (at // rows) % n
        source = (layer * ctx_size + block) * rows + at % rows
        return (jnp.arange(width, dtype=jnp.int32)[:, None] == source[None, :]).astype(BF)

    def to_relative(values):
        parts = values.reshape(values.shape[0], n, ctx_size, rows)
        picked = [
            lax.dynamic_index_in_dim(parts, ctx ^ j, axis=2, keepdims=False) for j in order
        ]
        return jnp.stack(picked, axis=1).reshape(values.shape)

    def to_natural(values):
        parts = values.reshape(values.shape[0], ctx_size, n, rows)
        where = [order.index(j) for j in range(ctx_size)]
        stacked = jnp.stack([parts[:, place] for place in where], axis=1)
        natural = [
            lax.dynamic_index_in_dim(stacked, ctx ^ j, axis=1, keepdims=False)
            for j in range(ctx_size)
        ]
        return jnp.stack(natural, axis=2).reshape(values.shape)

    def own_half(values):
        return lax.dynamic_slice_in_dim(values, y * h, h, axis=0)

    def other_half(values):
        return lax.dynamic_slice_in_dim(values, (1 - y) * h, h, axis=0)

    def both_halves(own):
        other = flip(own, "tp", 1)
        return jnp.where(
            y == 0, jnp.concatenate([own, other], axis=0), jnp.concatenate([other, own], axis=0)
        )

    half_d = width // 2
    ready = norm_in[0, 0] == norm_in[0, 0]
    qkv_whole = lax.all_gather(w_qkv[0].reshape(rows, -1), ("fsdp", "ctx"), axis=0, tiled=True)
    out_slots = [w_out[0]] + [rotate(w_out[0], "fsdp", k) for k in range(1, n)]

    tile = 3 * HD if piece % (3 * HD) == 0 else HD
    pad = n * piece - hidden

    def lay_out(w_gate_up, w_down):
        gate_rows = jnp.pad(w_gate_up[0, :, 0], ((0, 0), (0, pad)))
        up_rows = jnp.pad(w_gate_up[0, :, 1], ((0, 0), (0, pad)))
        down_rows = jnp.pad(w_down[0], ((0, 0), (0, pad)))
        pair_out, down_out = [], []
        for index in range(n):
            columns = []
            for start in range(index * piece, (index + 1) * piece, tile):
                columns += [gate_rows[:, start : start + tile], up_rows[:, start : start + tile]]
            pair_out.append(jnp.concatenate(columns, axis=1))
            down_out.append(down_rows[:, index * piece : (index + 1) * piece])
        return jnp.stack(pair_out), jnp.stack(down_out)

    pair_out, down_out = lay_out(w_gate_up, w_down)
    pair_block = deal(pair_out, "fsdp").reshape(n * rows, 2 * piece)

    def prepare(tokens, cotangent, norm_in, norm_mid, positions):
        x0 = tokens.astype(F32)
        inverse_one = lax.rsqrt(jnp.mean(x0 * x0, axis=-1, keepdims=True) + EPS)
        normed_one = (x0 * inverse_one * norm_in).astype(BF)
        place = together(one_hot())[0]
        placed = dot(jnp.concatenate([own_half(tokens), cotangent, normed_one]), place)
        grad_half = own_half(placed[h : h + count].astype(BF))
        normed_placed = placed[h + count :].astype(BF)
        cos_table, sin_table = angle_tables(positions)
        gain_two = to_relative(norm_mid)
        return inverse_one, normed_one, place, placed[:h], grad_half, normed_placed, gain_two, cos_table, sin_table

    x0 = tokens.astype(F32)
    (
        inverse_one,
        normed_one,
        place,
        x0_half,
        grad_half,
        normed_placed,
        gain_two,
        cos_table,
        sin_table,
    ) = prepare(tokens, cotangent, norm_in, norm_mid, positions)

    def over_x(piece_rows):
        held = [piece_rows]
        bit = ctx_size // 2
        while bit > 1:
            held = held + [flip(part, "ctx", bit) for part in held]
            bit //= 2
        return held

    def over_cores(held):
        return held + [flip(part, "ctx", 1) for part in held]

    out_x = over_x(in_order(out_slots).reshape(n * rows, -1))
    out_a = jnp.concatenate(out_x)
    out_b = flip(out_a, "ctx", 1)

    query_index = ctx * count + jnp.arange(count, dtype=jnp.int32)
    key_index = jnp.concatenate(
        [(ctx ^ j) * count + jnp.arange(count, dtype=jnp.int32) for j in range(ctx_size)]
    )
    first_key = query_index - positions
    allowed = (key_index[None, :] <= query_index[:, None]) & (
        key_index[None, :] >= first_key[:, None]
    )
    grad_natural = lax.all_gather(grad_half, ("fsdp", "tp"), axis=0, tiled=True)

    def by_features(values, weight):
        return jnp.concatenate(
            [dot_nt(values, weight[:half_d]), dot_nt(values, weight[half_d:])], axis=1
        )

    def attention_scores(queries, key_rows):
        scores = jnp.einsum("tgd,kd->gtk", queries, key_rows, preferred_element_type=F32) * scale
        return jnp.where(allowed[None], scores, -1e30)

    def project_all(normed_one, qkv_whole, out_b):
        project = dot(normed_one, qkv_whole) + (b_qkv[0].reshape(-1) + nothing_of(out_b))
        project = project.reshape(count, heads + 2, HD)
        queries = rotary(project[:, :heads], cos_table[:, None], sin_table[:, None]).astype(BF)
        key_local = rotary(project[:, heads], cos_table, sin_table).astype(BF)
        value_local = project[:, heads + 1].astype(BF)
        local_pair = jnp.stack([key_local, value_local])
        pairs_all = [local_pair] + [flip(local_pair, "ctx", j) for j in range(1, ctx_size)]
        key_rows = jnp.concatenate([p[0] for p in pairs_all], axis=0)
        value_rows = jnp.concatenate([p[1] for p in pairs_all], axis=0)
        return queries, key_rows, value_rows

    def attend(queries, key_rows, value_rows, out_whole):
        scores = attention_scores(queries, key_rows)
        peak = jnp.max(scores, axis=-1, keepdims=True)
        shifted = jnp.exp(scores - peak)
        total = jnp.sum(shifted, axis=-1, keepdims=True)
        probabilities = (shifted / total).astype(BF)
        log_total = peak + jnp.log(total)
        attended = jnp.einsum("gtk,kd->tgd", probabilities, value_rows, preferred_element_type=F32)
        attended = attended.astype(BF).reshape(count, -1)
        branch_away = by_features(other_half(attended), out_whole).astype(BF)
        arrived = flip(branch_away, "tp", 1)
        branch = by_features(own_half(after(attended, branch_away)), out_whole)
        middle = x0_half + branch + arrived.astype(F32)
        inverse_two = lax.rsqrt(jnp.mean(middle * middle, axis=-1, keepdims=True) + EPS)
        normed_two = (middle * inverse_two * gain_two).astype(BF)
        return log_total, attended, middle, inverse_two, normed_two

    out_whole = jnp.concatenate([out_a, out_b])
    queries, key_rows, value_rows = segment(
        ready, project_all, normed_one, qkv_whole, out_b
    )
    early = piece // tile // 2
    cut_at = early * 2 * tile
    down_block = deal(after(down_out, value_rows), "fsdp").reshape(n * rows, piece)
    pair_late = after(pair_block[:, cut_at:], value_rows)
    pair_x = flip(pair_late, "ctx", ctx_size // 2)
    pair_core = flip(after(pair_block, value_rows), "ctx", 1)
    log_total, attended, middle, inverse_two, normed_two = segment(
        ready, attend, queries, key_rows, value_rows, out_whole
    )

    second_out = jnp.concatenate([pair_block[:, :cut_at], down_block], axis=1)
    second_x = flip(after(second_out, normed_two, pair_core, pair_x), "ctx", ctx_size // 2)
    down_core = flip(after(down_block, normed_two), "ctx", 1)

    def gather_first(block):
        away_own = flip(block, "tp", 1)
        ups, downs, swapped = [block], [block], []
        for step in range(1, n - 1):
            up, down = together(gather_up(ups[-1], step), gather_down(downs[-1], step))
            ups.append(up)
            downs.append(down)
            if n == 4 and step == 1:
                swapped.append(flip(jnp.where(z == 0, down, up), "tp", 1))
        return away_own, ups[1:], downs[1:], swapped

    def gather_last(block, ups, downs):
        if n == 4:
            two = jnp.where(z == 0, downs[1], jnp.where(z == 3, ups[1], downs[0]))
            two = flip(two, "tp", 1)
        up, down = gather_up(ups[-1], n - 1), gather_down(downs[-1], n - 1)
        if n == 4:
            up, down, two = together(up, down, two)
            three = jnp.where(
                z == 0, down, jnp.where(z == 3, up, jnp.where(z == 1, downs[1], ups[1]))
            )
            return up, down, [two, flip(three, "tp", 1)]
        ups = dict(enumerate(list(ups) + [up], start=1))
        downs = dict(enumerate(list(downs) + [down], start=1))
        own_slots = slots_of(block, ups, downs)
        gathered = own_slots + [flip(slot, "tp", 1) for slot in own_slots[1:]]
        return up, down, gathered

    away_own, ups, downs, swapped = segment(
        ready, gather_first, normed_two
    )
    second_core = flip(after(second_x, ups[-1]), "ctx", 1)
    pair_x_core = flip(after(pair_x, normed_two), "ctx", 1)
    up, down, gathered = segment(
        ready, gather_last, normed_two, ups, downs
    )
    blocks = [
        [(down_block, 0), (pair_block, 0)],
        [(second_x, cut_at), (pair_x, 0), (second_x, 0)],
        [(down_core, 0), (pair_core, 0)],
        [(second_core, cut_at), (pair_x_core, 0), (second_core, 0)],
    ]
    if n == 4:
        spot = jnp.stack([z, y]).astype(jnp.int32)
        arrivals = [normed_two, *ups, up, *downs, down, away_own, swapped[0], *gathered]
        operands = (spot, arrivals, grad_natural)
    else:
        normed_all = jnp.concatenate(gathered[:n] + [away_own] + gathered[n:])
        by_slot = grad_natural.reshape(n, 2, h, width)
        by_slot = [pick(by_slot, (z - k) % n) for k in range(n)]
        grad_all = jnp.concatenate(
            [pick(slot, y) for slot in by_slot] + [pick(slot, 1 - y) for slot in by_slot]
        )
        operands = (None, normed_all, grad_all)
    activated, grad_pair, pair_whole, down_whole, normed_all, grad_all, act_natural = hidden_pass(
        *operands, blocks, early, piece, tile
    )

    own_tokens = n * h
    ctx_half, ctx_own = width // 2, width // ctx_size

    def core_term(left, right):
        return dot_tn(left[:, ctx_half:], right).astype(BF)

    def x_terms(left, right, arrived):
        terms = []
        for start in range(ctx_own, ctx_half, ctx_own):
            term = dot_tn(left[:, start : start + ctx_own], right)
            terms.append((term + arrived[start : start + ctx_own].astype(F32)).astype(BF))
        return terms

    def to_x(terms):
        return [flip(term, "ctx", j) for term, j in zip(terms, order[1:], strict=False)]

    def own_rows(left, right, arrived, moved):
        total = dot_tn(left[:, :ctx_own], right) + arrived[:ctx_own].astype(F32)
        for part in moved:
            total = total + part.astype(F32)
        return total

    def deal_rows(total):
        return deal(total.astype(BF).reshape(n, rows, total.shape[1]), "fsdp")

    away = by_features(grad_pair[own_tokens:], pair_whole).astype(BF).reshape(n, h, width)
    low = z < n // 2
    early = jnp.where(low, 1, n - 1)
    leaving = pick(away, early)

    def beside_first(grad_pair, activated, grad_all, pair_whole):
        kept = by_features(grad_pair[:own_tokens], pair_whole).reshape(n, h, width)
        return kept, core_term(grad_all, activated)

    def result_terms(activated, down_whole):
        return by_features(activated, down_whole).astype(BF)

    def result_order(result):
        result = result.reshape(2, n, h, width)
        by_y = jnp.where(y == 0, result, result[::-1])
        by_z = jnp.stack([by_y[:, k] for k in range(n)])
        return jnp.stack([pick(by_z, (z - b) % n) for b in range(n)]).reshape(-1, width)

    y_early = flip(leaving, "tp", 1)
    kept, down_leaving = segment(
        ready, beside_first, grad_pair, activated, grad_all, pair_whole
    )
    if n == 4:
        y_early = after(y_early, kept)
        acc_up = (kept[1] + y_early.astype(F32)).astype(BF)
        acc_down = (kept[3] + y_early.astype(F32)).astype(BF)
        acc_up, acc_down = together(acc_up, acc_down)
        up, down = sum_up(acc_up, 1), sum_down(acc_down, 1)
        y_mid = flip(after(away[2], acc_up), "tp", 1)
        down_core = flip(after(down_leaving, acc_up), "ctx", 1)
        pair_leaving = segment(
            ready, core_term, after(normed_all, acc_up, acc_down), grad_pair
        )

        up, down, y_mid = after(up, pair_leaving), after(down, pair_leaving), after(y_mid, pair_leaving)
        acc_up = (kept[2] + y_mid.astype(F32) + up.astype(F32)).astype(BF)
        acc_down = (kept[2] + y_mid.astype(F32) + down.astype(F32)).astype(BF)
        acc_up, acc_down, down_core = together(acc_up, acc_down, down_core)
        up, down = sum_up(acc_up, 2), sum_down(acc_down, 2)
        y_late = flip(after(pick(away, n - early), acc_up), "tp", 1)
        pair_core = flip(after(pair_leaving, acc_up), "ctx", 1)

        down_terms = segment(
            ready, x_terms, after(grad_all, acc_up, acc_down), activated, down_core
        )

        down_moved = to_x(down_terms)
        by_z = result_terms(after(act_natural, *down_terms), down_whole)

        up, down, y_late = together(up, down, y_late, by_z)[:3]
        crossed_three = jnp.where(low, y_late, y_early).astype(F32)
        crossed_one = jnp.where(low, y_early, y_late).astype(F32)
        acc_up = (kept[3] + crossed_three + up.astype(F32)).astype(BF)
        acc_down = (kept[1] + crossed_one + down.astype(F32)).astype(BF)
        acc_up, acc_down = together(acc_up, acc_down)
        up, down = sum_up(acc_up, 3), sum_down(acc_down, 3)
        y_own = flip(after(away[0], acc_up), "tp", 1)

        def beside_third(
            normed_all, grad_pair, pair_core, grad_all, activated, down_core, down_moved
        ):
            terms = x_terms(normed_all, grad_pair, pair_core)
            return terms, own_rows(grad_all, activated, down_core, down_moved).astype(BF)

        pair_terms, down_total = segment(
            ready,
            beside_third,
            after(normed_all, acc_up, acc_down),
            grad_pair,
            pair_core,
            grad_all,
            activated,
            down_core,
            down_moved,
        )

        y_own = after(y_own, *pair_terms)
        grad_normed_two = kept[0] + y_own.astype(F32) + up.astype(F32) + down.astype(F32)
    else:
        crossed = [flip(away[k], "tp", 1) for k in range(n)]
        grad_normed_two = chain_sum([kept[k] + crossed[k].astype(F32) for k in range(n)])
        by_z = result_order(result_terms(activated, down_whole))
        down_core = flip(down_leaving, "ctx", 1)
        pair_core = flip(core_term(normed_all, grad_pair), "ctx", 1)
        pair_terms = x_terms(normed_all, grad_pair, pair_core)
        down_moved = to_x(x_terms(grad_all, activated, down_core))
        down_total = own_rows(grad_all, activated, down_core, down_moved).astype(BF)

    scaled = grad_normed_two * gain_two
    gain_two_grad = jnp.sum(grad_normed_two * middle * inverse_two, axis=0)
    grad_middle = (
        inverse_two * scaled
        - middle * inverse_two**3 * jnp.mean(scaled * middle, axis=-1, keepdims=True)
        + grad_half.astype(F32)
    )
    middle_half = grad_middle.astype(BF)

    out_other = flip(middle_half, "tp", 1)
    result_sum = lax.psum_scatter(
        after(by_z, middle_half), ("fsdp", "tp"), scatter_dimension=0, tiled=True
    )

    def whole_rows(left, right, arrived, moved):
        return own_rows(left, right, arrived, moved).astype(BF)

    def deal_by_three(total, *earlier):
        parts = total.reshape(n, rows, total.shape[1])
        slots = {0: pick(parts, z)}
        for k in range(1, n):
            slots[k] = rotate(after(pick(parts, (z + k) % n), *earlier), "fsdp", k)
        return slots

    if n == 4:
        down_dealt = deal_by_three(down_total, middle_half)
        down_there = [down_dealt[k] for k in range(1, n)]
    else:
        down_dealt = deal_rows(down_total)
        down_there = []
    pair_moved = to_x([after(term, middle_half) for term in pair_terms])

    def attend_back(own, other, out_whole, queries, key_rows, value_rows, log_total):
        out_in = jnp.where(y == 0, jnp.concatenate([own, other]), jnp.concatenate([other, own]))
        grad_heads = dot(out_in[:, :half_d], out_whole[:half_d])
        grad_heads = grad_heads + dot(out_in[:, half_d:], out_whole[half_d:])
        grad_heads = grad_heads.astype(BF).reshape(count, heads, HD)
        exact = jnp.exp(attention_scores(queries, key_rows) - log_total)
        grad_probs = jnp.einsum("tgd,kd->gtk", grad_heads, value_rows, preferred_element_type=F32)
        grad_scores = exact * (grad_probs - jnp.sum(exact * grad_probs, axis=-1, keepdims=True))
        grad_scores = grad_scores.astype(BF)
        grad_queries = (
            jnp.einsum("gtk,kd->tgd", grad_scores, key_rows, preferred_element_type=F32) * scale
        )
        grad_key_rows = (
            jnp.einsum("gtk,tgd->kd", grad_scores, queries, preferred_element_type=F32) * scale
        )
        grad_value_rows = jnp.einsum(
            "gtk,tgd->kd", exact.astype(BF), grad_heads, preferred_element_type=F32
        )
        grad_pairs = jnp.stack([grad_key_rows, grad_value_rows]).reshape(2, ctx_size, count, HD)
        sent = [grad_pairs[:, j].astype(BF) for j in range(1, ctx_size)]
        return out_in, grad_queries, grad_pairs[:, 0], sent, core_term(out_in, attended)

    out_in, grad_queries, grad_kv, sent, out_leaving = segment(
        ready,
        attend_back,
        middle_half,
        out_other,
        out_whole,
        queries,
        key_rows,
        value_rows,
        log_total,
    )
    moved = [flip(after(part, *down_there), "ctx", j) for j, part in enumerate(sent, start=1)]
    out_core = flip(after(out_leaving, *down_there), "ctx", 1)

    def pair_rows(normed_all, grad_pair, pair_core, pair_moved):
        total = own_rows(normed_all, grad_pair, pair_core, pair_moved).astype(BF)
        if n != 4:
            return total
        parts = total.reshape(n, rows, total.shape[1])
        return [pick(parts, (z + k) % n) for k in range(n)]

    pair_total = segment(
        ready, pair_rows, after(normed_all, *sent), grad_pair, pair_core, pair_moved
    )
    pair_last = pair_total[0] if n == 4 else pair_total
    out_terms = x_terms(out_in, attended, after(out_core, *moved, pair_last))
    out_moved = to_x(out_terms)

    def project_back(grad_queries, grad_kv, moved, normed_placed, qkv_whole, *bulk):
        sin_back = sin_table + nothing_of(*bulk)
        for part in moved:
            grad_kv = grad_kv + part.astype(F32)
        grad_project = (
            jnp.concatenate(
                [
                    rotary_back(grad_queries, cos_table[:, None], sin_back[:, None]),
                    rotary_back(grad_kv[0], cos_table, sin_back)[:, None],
                    grad_kv[1][:, None],
                ],
                axis=1,
            )
            .astype(BF)
            .reshape(count, -1)
        )
        away = core_term(normed_placed, grad_project)
        arrived = flip(away, "ctx", 1)
        partial_one = dot_nt(after(grad_project, away), qkv_whole).astype(BF)
        terms = x_terms(normed_placed, grad_project, after(arrived, partial_one))
        return grad_project, partial_one, arrived, terms

    grad_project, partial_one, qkv_core, qkv_terms = segment(
        ready,
        project_back,
        grad_queries,
        grad_kv,
        moved,
        normed_placed,
        qkv_whole,
        *out_terms,
        pair_last,
    )
    if n == 4:
        pair_dealt = {0: pair_total[0]}
        for k in (1, 3):
            pair_dealt[k] = rotate(pair_total[k], "fsdp", k)
        two_there = [pair_dealt[1], pair_dealt[3]]
        pair_dealt[2] = rotate(pair_total[2], "fsdp", 2)
        last_there = [pair_dealt[2]]
    else:
        pair_dealt = deal_rows(pair_total)
        two_there = last_there = []
    qkv_moved = to_x([after(term, *two_there) for term in qkv_terms])
    arrived_one = flip(after(partial_one, *qkv_terms), "tp", 1)

    def natural_columns(parts):
        whole = jnp.concatenate([parts[b] for b in range(n)], axis=1)
        return whole[:, :hidden].astype(F32)

    out_total = own_rows(
        after(out_in, *qkv_terms), attended, out_core, [after(p, *qkv_terms) for p in out_moved]
    )

    def beside_x(grad_project, out_in, down_dealt):
        bias_grad = jnp.sum(grad_project, axis=0, dtype=F32)
        if n == 4:
            down_dealt = in_order([down_dealt[k] for k in range(n)])
        return bias_grad, dot_nt(out_in, place), natural_columns(down_dealt)

    bias_grad, middle_natural, down_grad = segment(
        ready, beside_x, after(grad_project, *qkv_terms, out_total), out_in, down_dealt
    )
    qkv_moved = [after(part, bias_grad, *last_there) for part in qkv_moved]
    qkv_total = own_rows(normed_placed, grad_project, qkv_core, qkv_moved)
    last_total = jnp.concatenate([qkv_total, out_total], axis=1)
    last_parts = last_total.reshape(n, rows, -1)
    if n == 4:
        last_dealt = [
            rotate(pick(last_parts, (z + k) % n).astype(BF), "fsdp", k) for k in range(1, n)
        ]
    arrived_one = after(arrived_one, qkv_total)

    def every_second(parts, which):
        return jnp.concatenate(
            [parts[:, :, s : s + tile] for s in range(which * tile, 2 * piece, 2 * tile)], axis=2
        )

    def beside_z(pair_dealt, result_sum, *bulk):
        if n == 4:
            pair_dealt = in_order([pair_dealt[k] for k in range(n)])
        pair_grad = [
            natural_columns(every_second(pair_dealt, c)) + nothing_of(*bulk) for c in range(2)
        ]
        residual = (middle + result_sum.astype(F32)).astype(BF)
        return jnp.stack(pair_grad, axis=1), residual

    pair_grad, residual = segment(ready, beside_z, pair_dealt, result_sum, qkv_total)
    if n == 4:
        last_grad = pick(last_parts, z)
        for part in last_dealt:
            last_grad = last_grad + after(part, pair_grad).astype(F32)
    else:
        last_grad = add_z(last_total)
    split = qkv_total.shape[1]
    qkv_grad, out_grad = last_grad[:, :split], last_grad[:, split:]
    residual_other = flip(residual, "tp", 1)
    residual_whole = jnp.where(
        y == 0,
        jnp.concatenate([residual, residual_other]),
        jnp.concatenate([residual_other, residual]),
    )
    output = dot_nt(residual_whole, place).astype(BF)
    grad_normed_one = partial_one.astype(F32) + arrived_one.astype(F32)
    scaled = grad_normed_one * norm_in
    gain_one_grad = jnp.sum(grad_normed_one * x0 * inverse_one, axis=0)
    grad_tokens = (
        inverse_one * scaled
        - x0 * inverse_one**3 * jnp.mean(scaled * x0, axis=-1, keepdims=True)
        + middle_natural
    )

    gain_two_pair = sum_everywhere(after(gain_two_grad[None], *qkv_terms), ("tp",))
    small = jnp.concatenate(
        [gain_one_grad[None], bias_grad[None], to_natural(gain_two_pair)], axis=1
    )
    small = sum_everywhere(small, ("ctx",))
    small_all = after(small, residual_other)
    small_all = sum_everywhere(small_all, ("fsdp",))
    return (
        output,
        grad_tokens,
        small_all[:, :width],
        qkv_grad.reshape(1, rows, 1, -1),
        small_all[:, width:-width].reshape(1, 1, -1),
        out_grad[None],
        small_all[:, -width:],
        pair_grad[None],
        down_grad[None],
    )


def solution(mesh):
    rows = ("fsdp", "ctx")
    in_specs = (
        P(rows, None),
        P(rows, None),
        P(),
        P(None, rows, "tp", None),
        P(None, "tp", None),
        P(None, rows, "tp"),
        P(),
        P(None, rows, None, "tp"),
        P(None, rows, "tp"),
        P(rows),
        P(rows),
    )
    out_specs = (
        P(rows, None),
        P(rows, None),
        P(),
        P(None, rows, "tp", None),
        P(None, "tp", None),
        P(None, rows, "tp"),
        P(),
        P(None, rows, None, "tp"),
        P(None, rows, "tp"),
    )
    return jax.shard_map(body, mesh=mesh, in_specs=in_specs, out_specs=out_specs, check_vma=False)
```

```python
import jax
import jax.numpy as jnp
from jax import lax
from jax.experimental import pallas as pl
from jax.experimental.pallas import tpu as pltpu
from jax.sharding import PartitionSpec as P

HD = 128
EPS = 1e-06
THETA = 1000000.0
BF = jnp.bfloat16
F32 = jnp.float32


def angle_tables(positions):
    exponent = jnp.arange(HD // 2, dtype=F32) * (2.0 / HD)
    inverse = THETA ** (-exponent)
    phase_angle = positions.astype(F32)[:, None] * inverse[None, :]
    phase_angle = jnp.concatenate([phase_angle, phase_angle], axis=-1)
    return (jnp.cos(phase_angle), jnp.sin(phase_angle))


def rotary(vectors, cos_table, sin_table):
    half_width = vectors.shape[-1] // 2
    turned = jnp.concatenate([-vectors[..., half_width:], vectors[..., :half_width]], axis=-1)
    return vectors * cos_table + turned * sin_table


def rotary_back(gradient, cos_table, sin_table):
    scaled = gradient * sin_table
    half_width = gradient.shape[-1] // 2
    turned = jnp.concatenate([scaled[..., half_width:], -scaled[..., :half_width]], axis=-1)
    return gradient * cos_table + turned


def dot(left, right):
    return jnp.dot(left, right, preferred_element_type=F32)


def dot_nt(left, right):
    return lax.dot_general(left, right, (((1,), (1,)), ((), ())), preferred_element_type=F32)


def dot_tn(left, right):
    return lax.dot_general(left, right, (((0,), (0,)), ((), ())), preferred_element_type=F32)


def after(value, *earlier):
    return lax.optimization_barrier((value,) + earlier)[0]


def together(*values):
    return lax.optimization_barrier(values)


def segment(ready, work, *operands):
    shapes = jax.eval_shape(work, *operands)

    def skip(*operands):
        return jax.tree.map(lambda leaf: jnp.zeros(leaf.shape, leaf.dtype), shapes)

    return lax.cond(ready, work, skip, *operands)


def nothing_of(*arrays):
    total = jnp.zeros((), F32)
    for array in arrays:
        total = total + array[(0,) * array.ndim].astype(F32) * 0.0
    return total


def rotate(block, axis, distance):
    n = lax.axis_size(axis)
    return lax.ppermute(block, axis, [(i, (i + distance) % n) for i in range(n)])


def flip(block, axis, bit):
    n = lax.axis_size(axis)
    return lax.ppermute(block, axis, [(i, i ^ bit) for i in range(n)])


def pick(pieces, index):
    return lax.dynamic_index_in_dim(pieces, index, axis=0, keepdims=False)


def in_order(slots):
    n = len(slots)
    z = lax.axis_index("fsdp")
    if n <= 4:
        return jnp.stack([lax.select_n((z - b) % n, *slots) for b in range(n)])
    whole = jnp.zeros((n,) + slots[0].shape, slots[0].dtype)
    for k, slot in enumerate(slots):
        whole = lax.dynamic_update_index_in_dim(whole, slot, (z - k) % n, axis=0)
    return whole


def deal(blocks, axis):
    return lax.all_to_all(blocks, axis, 0, 0, tiled=True)


def gather_up(block, s):
    n = lax.axis_size("fsdp")
    return lax.ppermute(block, "fsdp", [(i, i + 1) for i in range(s - 1, n - 1)])


def gather_down(block, s):
    n = lax.axis_size("fsdp")
    return lax.ppermute(block, "fsdp", [(i, i - 1) for i in range(1, n - s + 1)])


def slots_of(own, ups, downs):
    n = lax.axis_size("fsdp")
    z = lax.axis_index("fsdp")
    return [own] + [jnp.where(z >= k, ups[k], downs[n - k]) for k in range(1, n)]


def sum_up(block, s):
    n = lax.axis_size("fsdp")
    return lax.ppermute(block.astype(BF), "fsdp", [(i, i + 1) for i in range(s)])


def sum_down(block, s):
    n = lax.axis_size("fsdp")
    return lax.ppermute(block.astype(BF), "fsdp", [(i, i - 1) for i in range(n - s, n)])


def chain_sum(sums, *earlier):
    n = len(sums)
    up, down = sums[1], sums[n - 1]
    if earlier:
        up, down = after(up, *earlier), after(down, *earlier)
    for s in range(1, n):
        up, down = sum_up(up, s), sum_down(down, s)
        if s < n - 1:
            up = sums[s + 1] + up.astype(F32)
            down = sums[n - s - 1] + down.astype(F32)
    return sums[0] + up.astype(F32) + down.astype(F32)


def put_rows(parts, whole):
    rows = parts[0].shape[0]
    for b, part in enumerate(parts):
        whole[b * rows : (b + 1) * rows, :] = part[...]


def hidden_step(x_ref, g_ref, pair_ref, down_ref, act_ref, grad_ref):
    tile = down_ref.shape[1]
    chunk = min(1024, x_ref.shape[0])
    for start in range(0, x_ref.shape[0], chunk):
        here = pl.ds(start, chunk)
        both = dot(x_ref[here, :], pair_ref[...])
        grad = dot(g_ref[here, :], down_ref[...])
        gate, upward = both[:, :tile], both[:, tile:]
        sigma = 1.0 / (1.0 + jnp.exp(-gate))
        silu = gate * sigma
        act_ref[here, :] = (silu * upward).astype(BF)
        grad_ref[here, :tile] = (grad * upward * sigma * (1.0 + gate * (1.0 - sigma))).astype(BF)
        grad_ref[here, tile:] = (grad * silu).astype(BF)


def put_weights(parts, early, refs, pair_ref, down_ref):
    refs = list(refs)
    step = pl.program_id(0)
    for b, apart in enumerate(parts):
        down, pair = refs.pop(0), refs.pop(0)
        rows = slice(b * down.shape[0], (b + 1) * down.shape[0])
        down_ref[rows, :] = down[...]
        if not apart:
            pair_ref[rows, :] = pair[...]
            continue
        first = refs.pop(0)
        pair_ref[rows, :] = jnp.where(step < early, first[...], pair[...])


def hidden_kernel(parts, early, x_ref, g_ref, *refs):
    act_ref, grad_ref, pair_ref, down_ref = refs[-4:]
    put_weights(parts, early, refs[:-4], pair_ref, down_ref)
    hidden_step(x_ref, g_ref, pair_ref, down_ref, act_ref, grad_ref)


def hidden_kernel_four(parts, early, place_ref, *refs):
    own, ups, downs = refs[0], refs[1:4], refs[4:7]
    away_own, one, two, three, natural = refs[7:12]
    act_ref, grad_ref, pair_ref, down_ref, x_ref, g_ref, natural_ref = refs[-7:]
    z, y = place_ref[0], place_ref[1]
    h = own.shape[0]
    step = pl.program_id(0)

    def natural_rows(slot):
        index = lax.rem(z + 4 - slot % 4, 4) * 2 + lax.rem(y + slot // 4, 2)
        return pl.ds(pl.multiple_of(index * h, h), h)

    @pl.when(step == 0)
    def _():
        x_ref[:h, :] = own[...]
        for k in range(1, 4):
            x_ref[k * h : (k + 1) * h, :] = jnp.where(z >= k, ups[k - 1][...], downs[3 - k][...])
        x_ref[4 * h : 5 * h, :] = away_own[...]
        x_ref[5 * h : 6 * h, :] = jnp.where(z == 0, three[...], one[...])
        x_ref[6 * h : 7 * h, :] = jnp.where((z == 0) | (z == 3), two[...], three[...])
        last = jnp.where(z == 3, three[...], two[...])
        x_ref[7 * h :, :] = jnp.where(z == 0, one[...], last)
        for slot in range(8):
            g_ref[slot * h : (slot + 1) * h, :] = natural[natural_rows(slot), :]

    put_weights(parts, early, refs[12:-7], pair_ref, down_ref)
    hidden_step(x_ref, g_ref, pair_ref, down_ref, act_ref, grad_ref)
    for slot in range(8):
        natural_ref[natural_rows(slot), :] = act_ref[slot * h : (slot + 1) * h, :]


def hidden_pass(place, tokens, grads, blocks, early, piece, tile):
    count, width = grads.shape
    four = place is not None
    rows = count if four else min(1024, count)
    weights, weight_specs = [], []

    def at(shape, index):
        return pl.BlockSpec(shape, lambda t, r: (0, index(t)))

    for block in blocks:
        (down, d_from), (pair, p_from) = block[:2]
        depth = down.shape[0]
        base = early if len(block) > 2 else 0
        weights += [down, pair]
        weight_specs.append(at((depth, tile), lambda t, first=d_from // tile: first + t))
        weight_specs.append(
            at(
                (depth, 2 * tile),
                lambda t, first=p_from // (2 * tile), base=base: first + jnp.maximum(t - base, 0),
            )
        )
        if base:
            weights.append(block[2][0])
            weight_specs.append(
                at(
                    (depth, 2 * tile),
                    lambda t, first=block[2][1] // (2 * tile): first + jnp.minimum(t, early - 1),
                )
            )
    parts = [len(block) > 2 and early > 0 for block in blocks]
    out_specs = [
        pl.BlockSpec((rows, tile), lambda t, r: (r, t)),
        pl.BlockSpec((rows, 2 * tile), lambda t, r: (r, t)),
        pl.BlockSpec((width, 2 * tile), lambda t, r: (0, t)),
        pl.BlockSpec((width, tile), lambda t, r: (0, t)),
    ]
    out_shape = [
        jax.ShapeDtypeStruct((count, piece), BF),
        jax.ShapeDtypeStruct((count, 2 * piece), BF),
        jax.ShapeDtypeStruct((width, 2 * piece), BF),
        jax.ShapeDtypeStruct((width, piece), BF),
    ]
    if four:
        kernel, operands = hidden_kernel_four, [place] + list(tokens) + [grads]
        in_specs = [pl.BlockSpec(memory_space=pltpu.SMEM)]
        for array in operands[1:]:
            in_specs.append(
                pl.BlockSpec(array.shape, lambda t, r: (0, 0), pipeline_mode=pl.Buffered(1))
            )
        out_specs += [pl.BlockSpec((count, width), lambda t, r: (0, 0))] * 2
        out_shape += [jax.ShapeDtypeStruct((count, width), BF)] * 2
        out_specs.append(pl.BlockSpec((rows, tile), lambda t, r: (r, t)))
        out_shape.append(jax.ShapeDtypeStruct((count, piece), BF))
    else:
        kernel, operands = hidden_kernel, [tokens, grads]
        in_specs = [pl.BlockSpec((rows, width), lambda t, r: (r, 0))] * 2
    outs = pl.pallas_call(
        lambda *refs: kernel(parts, early, *refs),
        grid=(piece // tile, count // rows),
        in_specs=in_specs + weight_specs,
        out_specs=out_specs,
        out_shape=out_shape,
        compiler_params=pltpu.CompilerParams(vmem_limit_bytes=60 * 2**20),
        cost_estimate=pl.CostEstimate(
            flops=6 * count * width * piece,
            bytes_accessed=2 * (4 * count * width + 6 * width * piece + 3 * count * piece),
            transcendentals=count * piece,
        ),
    )(*operands, *weights)
    return outs if four else list(outs) + [tokens, grads, None]


def add_z(total, *earlier):
    n = lax.axis_size("fsdp")
    if earlier:
        total = after(total, *earlier)
    parts = deal(total.astype(BF).reshape(n, total.shape[0] // n, total.shape[1]), "fsdp")
    return jnp.sum(parts.astype(F32), axis=0)


def sum_everywhere(vector, axes):
    for axis in axes:
        bit = 1
        while bit < lax.axis_size(axis):
            vector = vector + flip(vector, axis, bit)
            bit *= 2
    return vector


def body(
    tokens,
    cotangent,
    norm_in,
    w_qkv,
    b_qkv,
    w_out,
    norm_mid,
    w_gate_up,
    w_down,
    segments,
    positions,
):
    n, ctx_size = lax.axis_size("fsdp"), lax.axis_size("ctx")
    z, ctx, y = lax.axis_index("fsdp"), lax.axis_index("ctx"), lax.axis_index("tp")
    count, width = tokens.shape
    h = count // 2
    rows = w_qkv.shape[1]
    heads = w_qkv.shape[3] // HD - 2
    hidden = w_down.shape[2]
    piece = -(-hidden // (n * HD)) * HD
    scale = HD ** (-0.5)

    order = [0]
    bit = ctx_size // 2
    while bit:
        order = order + [j ^ bit for j in order]
        bit //= 2

    def one_hot():
        at = jnp.arange(width, dtype=jnp.int32)
        block = sum(jnp.where(at // (n * rows) == b, ctx ^ j, 0) for b, j in enumerate(order))
        layer = (at // rows) % n
        source = (layer * ctx_size + block) * rows + at % rows
        return (jnp.arange(width, dtype=jnp.int32)[:, None] == source[None, :]).astype(BF)

    def to_relative(values):
        parts = values.reshape(values.shape[0], n, ctx_size, rows)
        picked = [
            lax.dynamic_index_in_dim(parts, ctx ^ j, axis=2, keepdims=False) for j in order
        ]
        return jnp.stack(picked, axis=1).reshape(values.shape)

    def to_natural(values):
        parts = values.reshape(values.shape[0], ctx_size, n, rows)
        where = [order.index(j) for j in range(ctx_size)]
        stacked = jnp.stack([parts[:, place] for place in where], axis=1)
        natural = [
            lax.dynamic_index_in_dim(stacked, ctx ^ j, axis=1, keepdims=False)
            for j in range(ctx_size)
        ]
        return jnp.stack(natural, axis=2).reshape(values.shape)

    def own_half(values):
        return lax.dynamic_slice_in_dim(values, y * h, h, axis=0)

    def other_half(values):
        return lax.dynamic_slice_in_dim(values, (1 - y) * h, h, axis=0)

    def both_halves(own):
        other = flip(own, "tp", 1)
        return jnp.where(
            y == 0, jnp.concatenate([own, other], axis=0), jnp.concatenate([other, own], axis=0)
        )

    half_d = width // 2
    ready = norm_in[0, 0] == norm_in[0, 0]
    qkv_whole = lax.all_gather(w_qkv[0].reshape(rows, -1), ("fsdp", "ctx"), axis=0, tiled=True)
    out_slots = [w_out[0]] + [rotate(w_out[0], "fsdp", k) for k in range(1, n)]

    tile = 3 * HD if piece % (3 * HD) == 0 else HD
    pad = n * piece - hidden

    def lay_out(w_gate_up, w_down):
        gate_rows = jnp.pad(w_gate_up[0, :, 0], ((0, 0), (0, pad)))
        up_rows = jnp.pad(w_gate_up[0, :, 1], ((0, 0), (0, pad)))
        down_rows = jnp.pad(w_down[0], ((0, 0), (0, pad)))
        pair_out, down_out = [], []
        for index in range(n):
            columns = []
            for start in range(index * piece, (index + 1) * piece, tile):
                columns += [gate_rows[:, start : start + tile], up_rows[:, start : start + tile]]
            pair_out.append(jnp.concatenate(columns, axis=1))
            down_out.append(down_rows[:, index * piece : (index + 1) * piece])
        return jnp.stack(pair_out), jnp.stack(down_out)

    pair_out, down_out = lay_out(w_gate_up, w_down)
    pair_block = deal(pair_out, "fsdp").reshape(n * rows, 2 * piece)

    def prepare(tokens, cotangent, norm_in, norm_mid, positions):
        x0 = tokens.astype(F32)
        inverse_one = lax.rsqrt(jnp.mean(x0 * x0, axis=-1, keepdims=True) + EPS)
        normed_one = (x0 * inverse_one * norm_in).astype(BF)
        place = together(one_hot())[0]
        placed = dot(jnp.concatenate([own_half(tokens), cotangent, normed_one]), place)
        grad_half = own_half(placed[h : h + count].astype(BF))
        normed_placed = placed[h + count :].astype(BF)
        cos_table, sin_table = angle_tables(positions)
        gain_two = to_relative(norm_mid)
        return inverse_one, normed_one, place, placed[:h], grad_half, normed_placed, gain_two, cos_table, sin_table

    x0 = tokens.astype(F32)
    (
        inverse_one,
        normed_one,
        place,
        x0_half,
        grad_half,
        normed_placed,
        gain_two,
        cos_table,
        sin_table,
    ) = prepare(tokens, cotangent, norm_in, norm_mid, positions)

    def over_x(piece_rows):
        held = [piece_rows]
        bit = ctx_size // 2
        while bit > 1:
            held = held + [flip(part, "ctx", bit) for part in held]
            bit //= 2
        return held

    def over_cores(held):
        return held + [flip(part, "ctx", 1) for part in held]

    out_x = over_x(in_order(out_slots).reshape(n * rows, -1))
    out_a = jnp.concatenate(out_x)
    out_b = flip(out_a, "ctx", 1)

    query_index = ctx * count + jnp.arange(count, dtype=jnp.int32)
    key_index = jnp.concatenate(
        [(ctx ^ j) * count + jnp.arange(count, dtype=jnp.int32) for j in range(ctx_size)]
    )
    first_key = query_index - positions
    allowed = (key_index[None, :] <= query_index[:, None]) & (
        key_index[None, :] >= first_key[:, None]
    )
    grad_natural = lax.all_gather(grad_half, ("fsdp", "tp"), axis=0, tiled=True)

    def by_features(values, weight):
        return jnp.concatenate(
            [dot_nt(values, weight[:half_d]), dot_nt(values, weight[half_d:])], axis=1
        )

    def attention_scores(queries, key_rows):
        scores = jnp.einsum("tgd,kd->gtk", queries, key_rows, preferred_element_type=F32) * scale
        return jnp.where(allowed[None], scores, -1e30)

    def project_all(normed_one, qkv_whole, out_b):
        project = dot(normed_one, qkv_whole) + (b_qkv[0].reshape(-1) + nothing_of(out_b))
        project = project.reshape(count, heads + 2, HD)
        queries = rotary(project[:, :heads], cos_table[:, None], sin_table[:, None]).astype(BF)
        key_local = rotary(project[:, heads], cos_table, sin_table).astype(BF)
        value_local = project[:, heads + 1].astype(BF)
        local_pair = jnp.stack([key_local, value_local])
        pairs_all = [local_pair] + [flip(local_pair, "ctx", j) for j in range(1, ctx_size)]
        key_rows = jnp.concatenate([p[0] for p in pairs_all], axis=0)
        value_rows = jnp.concatenate([p[1] for p in pairs_all], axis=0)
        return queries, key_rows, value_rows

    def attend(queries, key_rows, value_rows, out_whole):
        scores = attention_scores(queries, key_rows)
        peak = jnp.max(scores, axis=-1, keepdims=True)
        shifted = jnp.exp(scores - peak)
        total = jnp.sum(shifted, axis=-1, keepdims=True)
        probabilities = (shifted / total).astype(BF)
        log_total = peak + jnp.log(total)
        attended = jnp.einsum("gtk,kd->tgd", probabilities, value_rows, preferred_element_type=F32)
        attended = attended.astype(BF).reshape(count, -1)
        branch_away = by_features(other_half(attended), out_whole).astype(BF)
        arrived = flip(branch_away, "tp", 1)
        branch = by_features(own_half(after(attended, branch_away)), out_whole)
        middle = x0_half + branch + arrived.astype(F32)
        inverse_two = lax.rsqrt(jnp.mean(middle * middle, axis=-1, keepdims=True) + EPS)
        normed_two = (middle * inverse_two * gain_two).astype(BF)
        return log_total, attended, middle, inverse_two, normed_two

    out_whole = jnp.concatenate([out_a, out_b])
    queries, key_rows, value_rows = segment(
        ready, project_all, normed_one, qkv_whole, out_b
    )
    early = piece // tile // 2
    cut_at = early * 2 * tile
    down_block = deal(after(down_out, value_rows), "fsdp").reshape(n * rows, piece)
    pair_late = after(pair_block[:, cut_at:], value_rows)
    pair_x = flip(pair_late, "ctx", ctx_size // 2)
    pair_core = flip(after(pair_block, value_rows), "ctx", 1)
    log_total, attended, middle, inverse_two, normed_two = segment(
        ready, attend, queries, key_rows, value_rows, out_whole
    )

    second_out = jnp.concatenate([pair_block[:, :cut_at], down_block], axis=1)
    second_x = flip(after(second_out, normed_two, pair_core, pair_x), "ctx", ctx_size // 2)
    down_core = flip(after(down_block, normed_two), "ctx", 1)

    def gather_first(block):
        away_own = flip(block, "tp", 1)
        ups, downs, swapped = [block], [block], []
        for step in range(1, n - 1):
            up, down = together(gather_up(ups[-1], step), gather_down(downs[-1], step))
            ups.append(up)
            downs.append(down)
            if n == 4 and step == 1:
                swapped.append(flip(jnp.where(z == 0, down, up), "tp", 1))
        return away_own, ups[1:], downs[1:], swapped

    def gather_last(block, ups, downs):
        if n == 4:
            two = jnp.where(z == 0, downs[1], jnp.where(z == 3, ups[1], downs[0]))
            two = flip(two, "tp", 1)
        up, down = gather_up(ups[-1], n - 1), gather_down(downs[-1], n - 1)
        if n == 4:
            up, down, two = together(up, down, two)
            three = jnp.where(
                z == 0, down, jnp.where(z == 3, up, jnp.where(z == 1, downs[1], ups[1]))
            )
            return up, down, [two, flip(three, "tp", 1)]
        ups = dict(enumerate(list(ups) + [up], start=1))
        downs = dict(enumerate(list(downs) + [down], start=1))
        own_slots = slots_of(block, ups, downs)
        gathered = own_slots + [flip(slot, "tp", 1) for slot in own_slots[1:]]
        return up, down, gathered

    away_own, ups, downs, swapped = segment(
        ready, gather_first, normed_two
    )
    second_core = flip(after(second_x, ups[-1]), "ctx", 1)
    pair_x_core = flip(after(pair_x, normed_two), "ctx", 1)
    up, down, gathered = segment(
        ready, gather_last, normed_two, ups, downs
    )
    blocks = [
        [(down_block, 0), (pair_block, 0)],
        [(second_x, cut_at), (pair_x, 0), (second_x, 0)],
        [(down_core, 0), (pair_core, 0)],
        [(second_core, cut_at), (pair_x_core, 0), (second_core, 0)],
    ]
    if n == 4:
        spot = jnp.stack([z, y]).astype(jnp.int32)
        arrivals = [normed_two, *ups, up, *downs, down, away_own, swapped[0], *gathered]
        operands = (spot, arrivals, grad_natural)
    else:
        normed_all = jnp.concatenate(gathered[:n] + [away_own] + gathered[n:])
        by_slot = grad_natural.reshape(n, 2, h, width)
        by_slot = [pick(by_slot, (z - k) % n) for k in range(n)]
        grad_all = jnp.concatenate(
            [pick(slot, y) for slot in by_slot] + [pick(slot, 1 - y) for slot in by_slot]
        )
        operands = (None, normed_all, grad_all)
    activated, grad_pair, pair_whole, down_whole, normed_all, grad_all, act_natural = hidden_pass(
        *operands, blocks, early, piece, tile
    )

    own_tokens = n * h
    ctx_half, ctx_own = width // 2, width // ctx_size

    def core_term(left, right):
        return dot_tn(left[:, ctx_half:], right).astype(BF)

    def x_terms(left, right, arrived):
        terms = []
        for start in range(ctx_own, ctx_half, ctx_own):
            term = dot_tn(left[:, start : start + ctx_own], right)
            terms.append((term + arrived[start : start + ctx_own].astype(F32)).astype(BF))
        return terms

    def to_x(terms):
        return [flip(term, "ctx", j) for term, j in zip(terms, order[1:], strict=False)]

    def own_rows(left, right, arrived, moved):
        total = dot_tn(left[:, :ctx_own], right) + arrived[:ctx_own].astype(F32)
        for part in moved:
            total = total + part.astype(F32)
        return total

    def deal_rows(total):
        return deal(total.astype(BF).reshape(n, rows, total.shape[1]), "fsdp")

    away = by_features(grad_pair[own_tokens:], pair_whole).astype(BF).reshape(n, h, width)
    low = z < n // 2
    early = jnp.where(low, 1, n - 1)
    leaving = pick(away, early)

    def beside_first(grad_pair, activated, grad_all, pair_whole):
        kept = by_features(grad_pair[:own_tokens], pair_whole).reshape(n, h, width)
        return kept, core_term(grad_all, activated)

    def result_terms(activated, down_whole):
        return by_features(activated, down_whole).astype(BF)

    def result_order(result):
        result = result.reshape(2, n, h, width)
        by_y = jnp.where(y == 0, result, result[::-1])
        by_z = jnp.stack([by_y[:, k] for k in range(n)])
        return jnp.stack([pick(by_z, (z - b) % n) for b in range(n)]).reshape(-1, width)

    y_early = flip(leaving, "tp", 1)
    kept, down_leaving = segment(
        ready, beside_first, grad_pair, activated, grad_all, pair_whole
    )
    if n == 4:
        y_early = after(y_early, kept)
        acc_up = (kept[1] + y_early.astype(F32)).astype(BF)
        acc_down = (kept[3] + y_early.astype(F32)).astype(BF)
        acc_up, acc_down = together(acc_up, acc_down)
        up, down = sum_up(acc_up, 1), sum_down(acc_down, 1)
        y_mid = flip(after(away[2], acc_up), "tp", 1)
        down_core = flip(after(down_leaving, acc_up), "ctx", 1)
        pair_leaving = segment(
            ready, core_term, after(normed_all, acc_up, acc_down), grad_pair
        )

        up, down, y_mid = after(up, pair_leaving), after(down, pair_leaving), after(y_mid, pair_leaving)
        acc_up = (kept[2] + y_mid.astype(F32) + up.astype(F32)).astype(BF)
        acc_down = (kept[2] + y_mid.astype(F32) + down.astype(F32)).astype(BF)
        acc_up, acc_down, down_core = together(acc_up, acc_down, down_core)
        up, down = sum_up(acc_up, 2), sum_down(acc_down, 2)
        y_late = flip(after(pick(away, n - early), acc_up), "tp", 1)
        pair_core = flip(after(pair_leaving, acc_up), "ctx", 1)

        down_terms = segment(
            ready, x_terms, after(grad_all, acc_up, acc_down), activated, down_core
        )

        down_moved = to_x(down_terms)
        by_z = result_terms(after(act_natural, *down_terms), down_whole)

        up, down, y_late = together(up, down, y_late, by_z)[:3]
        crossed_three = jnp.where(low, y_late, y_early).astype(F32)
        crossed_one = jnp.where(low, y_early, y_late).astype(F32)
        acc_up = (kept[3] + crossed_three + up.astype(F32)).astype(BF)
        acc_down = (kept[1] + crossed_one + down.astype(F32)).astype(BF)
        acc_up, acc_down = together(acc_up, acc_down)
        up, down = sum_up(acc_up, 3), sum_down(acc_down, 3)
        y_own = flip(after(away[0], acc_up), "tp", 1)

        def beside_third(
            normed_all, grad_pair, pair_core, grad_all, activated, down_core, down_moved
        ):
            terms = x_terms(normed_all, grad_pair, pair_core)
            return terms, own_rows(grad_all, activated, down_core, down_moved).astype(BF)

        pair_terms, down_total = segment(
            ready,
            beside_third,
            after(normed_all, acc_up, acc_down),
            grad_pair,
            pair_core,
            grad_all,
            activated,
            down_core,
            down_moved,
        )

        y_own = after(y_own, *pair_terms)
        grad_normed_two = kept[0] + y_own.astype(F32) + up.astype(F32) + down.astype(F32)
    else:
        crossed = [flip(away[k], "tp", 1) for k in range(n)]
        grad_normed_two = chain_sum([kept[k] + crossed[k].astype(F32) for k in range(n)])
        by_z = result_order(result_terms(activated, down_whole))
        down_core = flip(down_leaving, "ctx", 1)
        pair_core = flip(core_term(normed_all, grad_pair), "ctx", 1)
        pair_terms = x_terms(normed_all, grad_pair, pair_core)
        down_moved = to_x(x_terms(grad_all, activated, down_core))
        down_total = own_rows(grad_all, activated, down_core, down_moved).astype(BF)

    scaled = grad_normed_two * gain_two
    gain_two_grad = jnp.sum(grad_normed_two * middle * inverse_two, axis=0)
    grad_middle = (
        inverse_two * scaled
        - middle * inverse_two**3 * jnp.mean(scaled * middle, axis=-1, keepdims=True)
        + grad_half.astype(F32)
    )
    middle_half = grad_middle.astype(BF)

    out_other = flip(middle_half, "tp", 1)
    result_sum = lax.psum_scatter(
        after(by_z, middle_half), ("fsdp", "tp"), scatter_dimension=0, tiled=True
    )

    def whole_rows(left, right, arrived, moved):
        return own_rows(left, right, arrived, moved).astype(BF)

    def deal_by_three(total, *earlier):
        parts = total.reshape(n, rows, total.shape[1])
        slots = {0: pick(parts, z)}
        for k in range(1, n):
            slots[k] = rotate(after(pick(parts, (z + k) % n), *earlier), "fsdp", k)
        return slots

    if n == 4:
        down_dealt = deal_by_three(down_total, middle_half)
        down_there = [down_dealt[k] for k in range(1, n)]
    else:
        down_dealt = deal_rows(down_total)
        down_there = []
    pair_moved = to_x([after(term, middle_half) for term in pair_terms])

    def attend_back(own, other, out_whole, queries, key_rows, value_rows, log_total):
        out_in = jnp.where(y == 0, jnp.concatenate([own, other]), jnp.concatenate([other, own]))
        grad_heads = dot(out_in[:, :half_d], out_whole[:half_d])
        grad_heads = grad_heads + dot(out_in[:, half_d:], out_whole[half_d:])
        grad_heads = grad_heads.astype(BF).reshape(count, heads, HD)
        exact = jnp.exp(attention_scores(queries, key_rows) - log_total)
        grad_probs = jnp.einsum("tgd,kd->gtk", grad_heads, value_rows, preferred_element_type=F32)
        grad_scores = exact * (grad_probs - jnp.sum(exact * grad_probs, axis=-1, keepdims=True))
        grad_scores = grad_scores.astype(BF)
        grad_queries = (
            jnp.einsum("gtk,kd->tgd", grad_scores, key_rows, preferred_element_type=F32) * scale
        )
        grad_key_rows = (
            jnp.einsum("gtk,tgd->kd", grad_scores, queries, preferred_element_type=F32) * scale
        )
        grad_value_rows = jnp.einsum(
            "gtk,tgd->kd", exact.astype(BF), grad_heads, preferred_element_type=F32
        )
        grad_pairs = jnp.stack([grad_key_rows, grad_value_rows]).reshape(2, ctx_size, count, HD)
        sent = [grad_pairs[:, j].astype(BF) for j in range(1, ctx_size)]
        return out_in, grad_queries, grad_pairs[:, 0], sent, core_term(out_in, attended)

    out_in, grad_queries, grad_kv, sent, out_leaving = segment(
        ready,
        attend_back,
        middle_half,
        out_other,
        out_whole,
        queries,
        key_rows,
        value_rows,
        log_total,
    )
    moved = [flip(after(part, *down_there), "ctx", j) for j, part in enumerate(sent, start=1)]
    out_core = flip(after(out_leaving, *down_there), "ctx", 1)

    def pair_rows(normed_all, grad_pair, pair_core, pair_moved):
        total = own_rows(normed_all, grad_pair, pair_core, pair_moved).astype(BF)
        if n != 4:
            return total
        parts = total.reshape(n, rows, total.shape[1])
        return [pick(parts, (z + k) % n) for k in range(n)]

    pair_total = segment(
        ready, pair_rows, after(normed_all, *sent), grad_pair, pair_core, pair_moved
    )
    pair_last = pair_total[0] if n == 4 else pair_total
    out_terms = x_terms(out_in, attended, after(out_core, *moved, pair_last))
    out_moved = to_x(out_terms)

    def project_back(grad_queries, grad_kv, moved, normed_placed, qkv_whole, *bulk):
        sin_back = sin_table + nothing_of(*bulk)
        for part in moved:
            grad_kv = grad_kv + part.astype(F32)
        grad_project = (
            jnp.concatenate(
                [
                    rotary_back(grad_queries, cos_table[:, None], sin_back[:, None]),
                    rotary_back(grad_kv[0], cos_table, sin_back)[:, None],
                    grad_kv[1][:, None],
                ],
                axis=1,
            )
            .astype(BF)
            .reshape(count, -1)
        )
        away = core_term(normed_placed, grad_project)
        arrived = flip(away, "ctx", 1)
        partial_one = dot_nt(after(grad_project, away), qkv_whole).astype(BF)
        terms = x_terms(normed_placed, grad_project, after(arrived, partial_one))
        return grad_project, partial_one, arrived, terms

    grad_project, partial_one, qkv_core, qkv_terms = segment(
        ready,
        project_back,
        grad_queries,
        grad_kv,
        moved,
        normed_placed,
        qkv_whole,
        *out_terms,
        pair_last,
    )
    if n == 4:
        pair_dealt = {0: pair_total[0]}
        for k in (1, 3):
            pair_dealt[k] = rotate(pair_total[k], "fsdp", k)
        two_there = [pair_dealt[1], pair_dealt[3]]
        pair_dealt[2] = rotate(pair_total[2], "fsdp", 2)
        last_there = [pair_dealt[2]]
    else:
        pair_dealt = deal_rows(pair_total)
        two_there = last_there = []
    qkv_moved = to_x([after(term, *two_there) for term in qkv_terms])
    arrived_one = flip(after(partial_one, *qkv_terms), "tp", 1)

    def natural_columns(parts):
        whole = jnp.concatenate([parts[b] for b in range(n)], axis=1)
        return whole[:, :hidden].astype(F32)

    out_total = own_rows(
        after(out_in, *qkv_terms), attended, out_core, [after(p, *qkv_terms) for p in out_moved]
    )

    def beside_x(grad_project, out_in, down_dealt):
        bias_grad = jnp.sum(grad_project, axis=0, dtype=F32)
        if n == 4:
            down_dealt = in_order([down_dealt[k] for k in range(n)])
        return bias_grad, dot_nt(out_in, place), natural_columns(down_dealt)

    bias_grad, middle_natural, down_grad = segment(
        ready, beside_x, after(grad_project, *qkv_terms, out_total), out_in, down_dealt
    )
    qkv_moved = [after(part, bias_grad, *last_there) for part in qkv_moved]
    qkv_total = own_rows(normed_placed, grad_project, qkv_core, qkv_moved)
    last_total = jnp.concatenate([qkv_total, out_total], axis=1)
    last_parts = last_total.reshape(n, rows, -1)
    if n == 4:
        last_dealt = [
            rotate(pick(last_parts, (z + k) % n).astype(BF), "fsdp", k) for k in range(1, n)
        ]
    arrived_one = after(arrived_one, qkv_total)

    def every_second(parts, which):
        return jnp.concatenate(
            [parts[:, :, s : s + tile] for s in range(which * tile, 2 * piece, 2 * tile)], axis=2
        )

    def beside_z(pair_dealt, result_sum, *bulk):
        if n == 4:
            pair_dealt = in_order([pair_dealt[k] for k in range(n)])
        pair_grad = [
            natural_columns(every_second(pair_dealt, c)) + nothing_of(*bulk) for c in range(2)
        ]
        residual = (middle + result_sum.astype(F32)).astype(BF)
        return jnp.stack(pair_grad, axis=1), residual

    pair_grad, residual = segment(ready, beside_z, pair_dealt, result_sum, qkv_total)
    residual_other = flip(residual, "tp", 1)
    if n == 4:
        last_grad = pick(last_parts, z)
        for part in last_dealt:
            last_grad = last_grad + after(part, residual_other).astype(F32)
    else:
        last_grad = add_z(last_total)
    split = qkv_total.shape[1]
    qkv_grad, out_grad = last_grad[:, :split], last_grad[:, split:]
    residual_whole = jnp.where(
        y == 0,
        jnp.concatenate([residual, residual_other]),
        jnp.concatenate([residual_other, residual]),
    )
    output = dot_nt(residual_whole, place).astype(BF)
    grad_normed_one = partial_one.astype(F32) + arrived_one.astype(F32)
    scaled = grad_normed_one * norm_in
    gain_one_grad = jnp.sum(grad_normed_one * x0 * inverse_one, axis=0)
    grad_tokens = (
        inverse_one * scaled
        - x0 * inverse_one**3 * jnp.mean(scaled * x0, axis=-1, keepdims=True)
        + middle_natural
    )

    gain_two_pair = sum_everywhere(after(gain_two_grad[None], *qkv_terms), ("tp",))
    small = jnp.concatenate(
        [gain_one_grad[None], bias_grad[None], to_natural(gain_two_pair)], axis=1
    )
    small = sum_everywhere(small, ("ctx",))
    small_all = after(small, pair_grad)
    bit = 1
    while bit < n:
        small_all = small_all + flip(small_all, "fsdp", bit)
        if bit == 1:
            small_all = after(small_all, residual_other)
        bit *= 2
    return (
        output,
        grad_tokens,
        small_all[:, :width],
        qkv_grad.reshape(1, rows, 1, -1),
        small_all[:, width:-width].reshape(1, 1, -1),
        out_grad[None],
        small_all[:, -width:],
        pair_grad[None],
        down_grad[None],
    )


def solution(mesh):
    rows = ("fsdp", "ctx")
    in_specs = (
        P(rows, None),
        P(rows, None),
        P(),
        P(None, rows, "tp", None),
        P(None, "tp", None),
        P(None, rows, "tp"),
        P(),
        P(None, rows, None, "tp"),
        P(None, rows, "tp"),
        P(rows),
        P(rows),
    )
    out_specs = (
        P(rows, None),
        P(rows, None),
        P(),
        P(None, rows, "tp", None),
        P(None, "tp", None),
        P(None, rows, "tp"),
        P(),
        P(None, rows, None, "tp"),
        P(None, rows, "tp"),
    )
    return jax.shard_map(body, mesh=mesh, in_specs=in_specs, out_specs=out_specs, check_vma=False)
```

```python
import jax
import jax.numpy as jnp
from jax import lax
from jax.experimental import pallas as pl
from jax.experimental.pallas import tpu as pltpu
from jax.sharding import PartitionSpec as P

HD = 128
EPS = 1e-06
THETA = 1000000.0
BF = jnp.bfloat16
F32 = jnp.float32


def angle_tables(positions):
    exponent = jnp.arange(HD // 2, dtype=F32) * (2.0 / HD)
    inverse = THETA ** (-exponent)
    phase_angle = positions.astype(F32)[:, None] * inverse[None, :]
    phase_angle = jnp.concatenate([phase_angle, phase_angle], axis=-1)
    return (jnp.cos(phase_angle), jnp.sin(phase_angle))


def rotary(vectors, cos_table, sin_table):
    half_width = vectors.shape[-1] // 2
    turned = jnp.concatenate([-vectors[..., half_width:], vectors[..., :half_width]], axis=-1)
    return vectors * cos_table + turned * sin_table


def rotary_back(gradient, cos_table, sin_table):
    scaled = gradient * sin_table
    half_width = gradient.shape[-1] // 2
    turned = jnp.concatenate([scaled[..., half_width:], -scaled[..., :half_width]], axis=-1)
    return gradient * cos_table + turned


def dot(left, right):
    return jnp.dot(left, right, preferred_element_type=F32)


def dot_nt(left, right):
    return lax.dot_general(left, right, (((1,), (1,)), ((), ())), preferred_element_type=F32)


def dot_tn(left, right):
    return lax.dot_general(left, right, (((0,), (0,)), ((), ())), preferred_element_type=F32)


def after(value, *earlier):
    return lax.optimization_barrier((value,) + earlier)[0]


def together(*values):
    return lax.optimization_barrier(values)


def segment(ready, work, *operands):
    shapes = jax.eval_shape(work, *operands)

    def skip(*operands):
        return jax.tree.map(lambda leaf: jnp.zeros(leaf.shape, leaf.dtype), shapes)

    return lax.cond(ready, work, skip, *operands)


def nothing_of(*arrays):
    total = jnp.zeros((), F32)
    for array in arrays:
        total = total + array[(0,) * array.ndim].astype(F32) * 0.0
    return total


def rotate(block, axis, distance):
    n = lax.axis_size(axis)
    return lax.ppermute(block, axis, [(i, (i + distance) % n) for i in range(n)])


def flip(block, axis, bit):
    n = lax.axis_size(axis)
    return lax.ppermute(block, axis, [(i, i ^ bit) for i in range(n)])


def pick(pieces, index):
    return lax.dynamic_index_in_dim(pieces, index, axis=0, keepdims=False)


def in_order(slots):
    n = len(slots)
    z = lax.axis_index("fsdp")
    if n <= 4:
        return jnp.stack([lax.select_n((z - b) % n, *slots) for b in range(n)])
    whole = jnp.zeros((n,) + slots[0].shape, slots[0].dtype)
    for k, slot in enumerate(slots):
        whole = lax.dynamic_update_index_in_dim(whole, slot, (z - k) % n, axis=0)
    return whole


def deal(blocks, axis):
    return lax.all_to_all(blocks, axis, 0, 0, tiled=True)


def gather_up(block, s):
    n = lax.axis_size("fsdp")
    return lax.ppermute(block, "fsdp", [(i, i + 1) for i in range(s - 1, n - 1)])


def gather_down(block, s):
    n = lax.axis_size("fsdp")
    return lax.ppermute(block, "fsdp", [(i, i - 1) for i in range(1, n - s + 1)])


def slots_of(own, ups, downs):
    n = lax.axis_size("fsdp")
    z = lax.axis_index("fsdp")
    return [own] + [jnp.where(z >= k, ups[k], downs[n - k]) for k in range(1, n)]


def sum_up(block, s):
    n = lax.axis_size("fsdp")
    return lax.ppermute(block.astype(BF), "fsdp", [(i, i + 1) for i in range(s)])


def sum_down(block, s):
    n = lax.axis_size("fsdp")
    return lax.ppermute(block.astype(BF), "fsdp", [(i, i - 1) for i in range(n - s, n)])


def chain_sum(sums, *earlier):
    n = len(sums)
    up, down = sums[1], sums[n - 1]
    if earlier:
        up, down = after(up, *earlier), after(down, *earlier)
    for s in range(1, n):
        up, down = sum_up(up, s), sum_down(down, s)
        if s < n - 1:
            up = sums[s + 1] + up.astype(F32)
            down = sums[n - s - 1] + down.astype(F32)
    return sums[0] + up.astype(F32) + down.astype(F32)


def put_rows(parts, whole):
    rows = parts[0].shape[0]
    for b, part in enumerate(parts):
        whole[b * rows : (b + 1) * rows, :] = part[...]


def hidden_step(x_ref, g_ref, pair_ref, down_ref, act_ref, grad_ref):
    tile = down_ref.shape[1]
    chunk = min(1024, x_ref.shape[0])
    for start in range(0, x_ref.shape[0], chunk):
        here = pl.ds(start, chunk)
        both = dot(x_ref[here, :], pair_ref[...])
        grad = dot(g_ref[here, :], down_ref[...])
        gate, upward = both[:, :tile], both[:, tile:]
        sigma = 1.0 / (1.0 + jnp.exp(-gate))
        silu = gate * sigma
        act_ref[here, :] = (silu * upward).astype(BF)
        grad_ref[here, :tile] = (grad * upward * sigma * (1.0 + gate * (1.0 - sigma))).astype(BF)
        grad_ref[here, tile:] = (grad * silu).astype(BF)


def put_weights(parts, early, refs, pair_ref, down_ref):
    refs = list(refs)
    step = pl.program_id(0)
    for b, apart in enumerate(parts):
        down, pair = refs.pop(0), refs.pop(0)
        rows = slice(b * down.shape[0], (b + 1) * down.shape[0])
        down_ref[rows, :] = down[...]
        if not apart:
            pair_ref[rows, :] = pair[...]
            continue
        first = refs.pop(0)
        pair_ref[rows, :] = jnp.where(step < early, first[...], pair[...])


def hidden_kernel(parts, early, x_ref, g_ref, *refs):
    act_ref, grad_ref, pair_ref, down_ref = refs[-4:]
    put_weights(parts, early, refs[:-4], pair_ref, down_ref)
    hidden_step(x_ref, g_ref, pair_ref, down_ref, act_ref, grad_ref)


def hidden_kernel_four(parts, early, place_ref, *refs):
    own, ups, downs = refs[0], refs[1:4], refs[4:7]
    away_own, one, two, three, natural = refs[7:12]
    act_ref, grad_ref, pair_ref, down_ref, x_ref, g_ref, natural_ref = refs[-7:]
    z, y = place_ref[0], place_ref[1]
    h = own.shape[0]
    step = pl.program_id(0)

    def natural_rows(slot):
        index = lax.rem(z + 4 - slot % 4, 4) * 2 + lax.rem(y + slot // 4, 2)
        return pl.ds(pl.multiple_of(index * h, h), h)

    @pl.when(step == 0)
    def _():
        x_ref[:h, :] = own[...]
        for k in range(1, 4):
            x_ref[k * h : (k + 1) * h, :] = jnp.where(z >= k, ups[k - 1][...], downs[3 - k][...])
        x_ref[4 * h : 5 * h, :] = away_own[...]
        x_ref[5 * h : 6 * h, :] = jnp.where(z == 0, three[...], one[...])
        x_ref[6 * h : 7 * h, :] = jnp.where((z == 0) | (z == 3), two[...], three[...])
        last = jnp.where(z == 3, three[...], two[...])
        x_ref[7 * h :, :] = jnp.where(z == 0, one[...], last)
        for slot in range(8):
            g_ref[slot * h : (slot + 1) * h, :] = natural[natural_rows(slot), :]

    put_weights(parts, early, refs[12:-7], pair_ref, down_ref)
    hidden_step(x_ref, g_ref, pair_ref, down_ref, act_ref, grad_ref)
    for slot in range(8):
        natural_ref[natural_rows(slot), :] = act_ref[slot * h : (slot + 1) * h, :]


def hidden_pass(place, tokens, grads, blocks, early, piece, tile):
    count, width = grads.shape
    four = place is not None
    rows = count if four else min(1024, count)
    weights, weight_specs = [], []

    def at(shape, index):
        return pl.BlockSpec(shape, lambda t, r: (0, index(t)))

    for block in blocks:
        (down, d_from), (pair, p_from) = block[:2]
        depth = down.shape[0]
        base = early if len(block) > 2 else 0
        weights += [down, pair]
        weight_specs.append(at((depth, tile), lambda t, first=d_from // tile: first + t))
        weight_specs.append(
            at(
                (depth, 2 * tile),
                lambda t, first=p_from // (2 * tile), base=base: first + jnp.maximum(t - base, 0),
            )
        )
        if base:
            weights.append(block[2][0])
            weight_specs.append(
                at(
                    (depth, 2 * tile),
                    lambda t, first=block[2][1] // (2 * tile): first + jnp.minimum(t, early - 1),
                )
            )
    parts = [len(block) > 2 and early > 0 for block in blocks]
    out_specs = [
        pl.BlockSpec((rows, tile), lambda t, r: (r, t)),
        pl.BlockSpec((rows, 2 * tile), lambda t, r: (r, t)),
        pl.BlockSpec((width, 2 * tile), lambda t, r: (0, t)),
        pl.BlockSpec((width, tile), lambda t, r: (0, t)),
    ]
    out_shape = [
        jax.ShapeDtypeStruct((count, piece), BF),
        jax.ShapeDtypeStruct((count, 2 * piece), BF),
        jax.ShapeDtypeStruct((width, 2 * piece), BF),
        jax.ShapeDtypeStruct((width, piece), BF),
    ]
    if four:
        kernel, operands = hidden_kernel_four, [place] + list(tokens) + [grads]
        in_specs = [pl.BlockSpec(memory_space=pltpu.SMEM)]
        for array in operands[1:]:
            in_specs.append(
                pl.BlockSpec(array.shape, lambda t, r: (0, 0), pipeline_mode=pl.Buffered(1))
            )
        out_specs += [pl.BlockSpec((count, width), lambda t, r: (0, 0))] * 2
        out_shape += [jax.ShapeDtypeStruct((count, width), BF)] * 2
        out_specs.append(pl.BlockSpec((rows, tile), lambda t, r: (r, t)))
        out_shape.append(jax.ShapeDtypeStruct((count, piece), BF))
    else:
        kernel, operands = hidden_kernel, [tokens, grads]
        in_specs = [pl.BlockSpec((rows, width), lambda t, r: (r, 0))] * 2
    outs = pl.pallas_call(
        lambda *refs: kernel(parts, early, *refs),
        grid=(piece // tile, count // rows),
        in_specs=in_specs + weight_specs,
        out_specs=out_specs,
        out_shape=out_shape,
        compiler_params=pltpu.CompilerParams(vmem_limit_bytes=60 * 2**20),
        cost_estimate=pl.CostEstimate(
            flops=6 * count * width * piece,
            bytes_accessed=2 * (4 * count * width + 6 * width * piece + 3 * count * piece),
            transcendentals=count * piece,
        ),
    )(*operands, *weights)
    return outs if four else list(outs) + [tokens, grads, None]


def add_z(total, *earlier):
    n = lax.axis_size("fsdp")
    if earlier:
        total = after(total, *earlier)
    parts = deal(total.astype(BF).reshape(n, total.shape[0] // n, total.shape[1]), "fsdp")
    return jnp.sum(parts.astype(F32), axis=0)


def sum_everywhere(vector, axes):
    for axis in axes:
        bit = 1
        while bit < lax.axis_size(axis):
            vector = vector + flip(vector, axis, bit)
            bit *= 2
    return vector


def body(
    tokens,
    cotangent,
    norm_in,
    w_qkv,
    b_qkv,
    w_out,
    norm_mid,
    w_gate_up,
    w_down,
    segments,
    positions,
):
    n, ctx_size = lax.axis_size("fsdp"), lax.axis_size("ctx")
    z, ctx, y = lax.axis_index("fsdp"), lax.axis_index("ctx"), lax.axis_index("tp")
    count, width = tokens.shape
    h = count // 2
    rows = w_qkv.shape[1]
    heads = w_qkv.shape[3] // HD - 2
    hidden = w_down.shape[2]
    piece = -(-hidden // (n * HD)) * HD
    scale = HD ** (-0.5)

    order = [0]
    bit = ctx_size // 2
    while bit:
        order = order + [j ^ bit for j in order]
        bit //= 2

    def one_hot():
        at = jnp.arange(width, dtype=jnp.int32)
        block = sum(jnp.where(at // (n * rows) == b, ctx ^ j, 0) for b, j in enumerate(order))
        layer = (at // rows) % n
        source = (layer * ctx_size + block) * rows + at % rows
        return (jnp.arange(width, dtype=jnp.int32)[:, None] == source[None, :]).astype(BF)

    def to_relative(values):
        parts = values.reshape(values.shape[0], n, ctx_size, rows)
        picked = [
            lax.dynamic_index_in_dim(parts, ctx ^ j, axis=2, keepdims=False) for j in order
        ]
        return jnp.stack(picked, axis=1).reshape(values.shape)

    def to_natural(values):
        parts = values.reshape(values.shape[0], ctx_size, n, rows)
        where = [order.index(j) for j in range(ctx_size)]
        stacked = jnp.stack([parts[:, place] for place in where], axis=1)
        natural = [
            lax.dynamic_index_in_dim(stacked, ctx ^ j, axis=1, keepdims=False)
            for j in range(ctx_size)
        ]
        return jnp.stack(natural, axis=2).reshape(values.shape)

    def own_half(values):
        return lax.dynamic_slice_in_dim(values, y * h, h, axis=0)

    def other_half(values):
        return lax.dynamic_slice_in_dim(values, (1 - y) * h, h, axis=0)

    def both_halves(own):
        other = flip(own, "tp", 1)
        return jnp.where(
            y == 0, jnp.concatenate([own, other], axis=0), jnp.concatenate([other, own], axis=0)
        )

    half_d = width // 2
    ready = norm_in[0, 0] == norm_in[0, 0]
    qkv_whole = lax.all_gather(w_qkv[0].reshape(rows, -1), ("fsdp", "ctx"), axis=0, tiled=True)
    out_slots = [w_out[0]] + [rotate(w_out[0], "fsdp", k) for k in range(1, n)]

    tile = 3 * HD if piece % (3 * HD) == 0 else HD
    pad = n * piece - hidden

    def lay_out(w_gate_up, w_down):
        gate_rows = jnp.pad(w_gate_up[0, :, 0], ((0, 0), (0, pad)))
        up_rows = jnp.pad(w_gate_up[0, :, 1], ((0, 0), (0, pad)))
        down_rows = jnp.pad(w_down[0], ((0, 0), (0, pad)))
        pair_out, down_out = [], []
        for index in range(n):
            columns = []
            for start in range(index * piece, (index + 1) * piece, tile):
                columns += [gate_rows[:, start : start + tile], up_rows[:, start : start + tile]]
            pair_out.append(jnp.concatenate(columns, axis=1))
            down_out.append(down_rows[:, index * piece : (index + 1) * piece])
        return jnp.stack(pair_out), jnp.stack(down_out)

    pair_out, down_out = lay_out(w_gate_up, w_down)
    pair_block = deal(pair_out, "fsdp").reshape(n * rows, 2 * piece)

    def prepare(tokens, cotangent, norm_in, norm_mid, positions):
        x0 = tokens.astype(F32)
        inverse_one = lax.rsqrt(jnp.mean(x0 * x0, axis=-1, keepdims=True) + EPS)
        normed_one = (x0 * inverse_one * norm_in).astype(BF)
        place = together(one_hot())[0]
        placed = dot(jnp.concatenate([own_half(tokens), cotangent, normed_one]), place)
        grad_half = own_half(placed[h : h + count].astype(BF))
        normed_placed = placed[h + count :].astype(BF)
        cos_table, sin_table = angle_tables(positions)
        gain_two = to_relative(norm_mid)
        return inverse_one, normed_one, place, placed[:h], grad_half, normed_placed, gain_two, cos_table, sin_table

    x0 = tokens.astype(F32)
    (
        inverse_one,
        normed_one,
        place,
        x0_half,
        grad_half,
        normed_placed,
        gain_two,
        cos_table,
        sin_table,
    ) = prepare(tokens, cotangent, norm_in, norm_mid, positions)

    def over_x(piece_rows):
        held = [piece_rows]
        bit = ctx_size // 2
        while bit > 1:
            held = held + [flip(part, "ctx", bit) for part in held]
            bit //= 2
        return held

    def over_cores(held):
        return held + [flip(part, "ctx", 1) for part in held]

    out_x = over_x(in_order(out_slots).reshape(n * rows, -1))
    out_a = jnp.concatenate(out_x)
    out_b = flip(out_a, "ctx", 1)

    query_index = ctx * count + jnp.arange(count, dtype=jnp.int32)
    key_index = jnp.concatenate(
        [(ctx ^ j) * count + jnp.arange(count, dtype=jnp.int32) for j in range(ctx_size)]
    )
    first_key = query_index - positions
    allowed = (key_index[None, :] <= query_index[:, None]) & (
        key_index[None, :] >= first_key[:, None]
    )
    grad_natural = lax.all_gather(grad_half, ("fsdp", "tp"), axis=0, tiled=True)

    def by_features(values, weight):
        return jnp.concatenate(
            [dot_nt(values, weight[:half_d]), dot_nt(values, weight[half_d:])], axis=1
        )

    def attention_scores(queries, key_rows):
        scores = jnp.einsum("tgd,kd->gtk", queries, key_rows, preferred_element_type=F32) * scale
        return jnp.where(allowed[None], scores, -1e30)

    def project_all(normed_one, qkv_whole, out_b):
        project = dot(normed_one, qkv_whole) + (b_qkv[0].reshape(-1) + nothing_of(out_b))
        project = project.reshape(count, heads + 2, HD)
        queries = rotary(project[:, :heads], cos_table[:, None], sin_table[:, None]).astype(BF)
        key_local = rotary(project[:, heads], cos_table, sin_table).astype(BF)
        value_local = project[:, heads + 1].astype(BF)
        local_pair = jnp.stack([key_local, value_local])
        pairs_all = [local_pair] + [flip(local_pair, "ctx", j) for j in range(1, ctx_size)]
        key_rows = jnp.concatenate([p[0] for p in pairs_all], axis=0)
        value_rows = jnp.concatenate([p[1] for p in pairs_all], axis=0)
        return queries, key_rows, value_rows

    def attend(queries, key_rows, value_rows, out_whole):
        scores = attention_scores(queries, key_rows)
        peak = jnp.max(scores, axis=-1, keepdims=True)
        shifted = jnp.exp(scores - peak)
        total = jnp.sum(shifted, axis=-1, keepdims=True)
        probabilities = (shifted / total).astype(BF)
        log_total = peak + jnp.log(total)
        attended = jnp.einsum("gtk,kd->tgd", probabilities, value_rows, preferred_element_type=F32)
        attended = attended.astype(BF).reshape(count, -1)
        branch_away = by_features(other_half(attended), out_whole).astype(BF)
        arrived = flip(branch_away, "tp", 1)
        branch = by_features(own_half(after(attended, branch_away)), out_whole)
        middle = x0_half + branch + arrived.astype(F32)
        inverse_two = lax.rsqrt(jnp.mean(middle * middle, axis=-1, keepdims=True) + EPS)
        normed_two = (middle * inverse_two * gain_two).astype(BF)
        return log_total, attended, middle, inverse_two, normed_two

    out_whole = jnp.concatenate([out_a, out_b])
    queries, key_rows, value_rows = segment(
        ready, project_all, normed_one, qkv_whole, out_b
    )
    early = piece // tile // 2
    cut_at = early * 2 * tile
    down_block = deal(after(down_out, value_rows), "fsdp").reshape(n * rows, piece)
    pair_late = after(pair_block[:, cut_at:], value_rows)
    pair_x = flip(pair_late, "ctx", ctx_size // 2)
    pair_core = flip(after(pair_block, value_rows), "ctx", 1)
    log_total, attended, middle, inverse_two, normed_two = segment(
        ready, attend, queries, key_rows, value_rows, out_whole
    )

    second_out = jnp.concatenate([pair_block[:, :cut_at], down_block], axis=1)
    second_x = flip(after(second_out, normed_two, pair_core, pair_x), "ctx", ctx_size // 2)
    down_core = flip(after(down_block, normed_two), "ctx", 1)

    def gather_first(block):
        away_own = flip(block, "tp", 1)
        ups, downs, swapped = [block], [block], []
        for step in range(1, n - 1):
            up, down = together(gather_up(ups[-1], step), gather_down(downs[-1], step))
            ups.append(up)
            downs.append(down)
            if n == 4 and step == 1:
                swapped.append(flip(jnp.where(z == 0, down, up), "tp", 1))
        return away_own, ups[1:], downs[1:], swapped

    def gather_last(block, ups, downs):
        if n == 4:
            two = jnp.where(z == 0, downs[1], jnp.where(z == 3, ups[1], downs[0]))
            two = flip(two, "tp", 1)
        up, down = gather_up(ups[-1], n - 1), gather_down(downs[-1], n - 1)
        if n == 4:
            up, down, two = together(up, down, two)
            three = jnp.where(
                z == 0, down, jnp.where(z == 3, up, jnp.where(z == 1, downs[1], ups[1]))
            )
            return up, down, [two, flip(three, "tp", 1)]
        ups = dict(enumerate(list(ups) + [up], start=1))
        downs = dict(enumerate(list(downs) + [down], start=1))
        own_slots = slots_of(block, ups, downs)
        gathered = own_slots + [flip(slot, "tp", 1) for slot in own_slots[1:]]
        return up, down, gathered

    away_own, ups, downs, swapped = segment(
        ready, gather_first, normed_two
    )
    second_core = flip(after(second_x, ups[-1]), "ctx", 1)
    pair_x_core = flip(after(pair_x, normed_two), "ctx", 1)
    up, down, gathered = segment(
        ready, gather_last, normed_two, ups, downs
    )
    blocks = [
        [(down_block, 0), (pair_block, 0)],
        [(second_x, cut_at), (pair_x, 0), (second_x, 0)],
        [(down_core, 0), (pair_core, 0)],
        [(second_core, cut_at), (pair_x_core, 0), (second_core, 0)],
    ]
    if n == 4:
        spot = jnp.stack([z, y]).astype(jnp.int32)
        arrivals = [normed_two, *ups, up, *downs, down, away_own, swapped[0], *gathered]
        operands = (spot, arrivals, grad_natural)
    else:
        normed_all = jnp.concatenate(gathered[:n] + [away_own] + gathered[n:])
        by_slot = grad_natural.reshape(n, 2, h, width)
        by_slot = [pick(by_slot, (z - k) % n) for k in range(n)]
        grad_all = jnp.concatenate(
            [pick(slot, y) for slot in by_slot] + [pick(slot, 1 - y) for slot in by_slot]
        )
        operands = (None, normed_all, grad_all)
    activated, grad_pair, pair_whole, down_whole, normed_all, grad_all, act_natural = hidden_pass(
        *operands, blocks, early, piece, tile
    )

    own_tokens = n * h
    ctx_half, ctx_own = width // 2, width // ctx_size

    def core_term(left, right):
        return dot_tn(left[:, ctx_half:], right).astype(BF)

    def x_terms(left, right, arrived):
        terms = []
        for start in range(ctx_own, ctx_half, ctx_own):
            term = dot_tn(left[:, start : start + ctx_own], right)
            terms.append((term + arrived[start : start + ctx_own].astype(F32)).astype(BF))
        return terms

    def to_x(terms):
        return [flip(term, "ctx", j) for term, j in zip(terms, order[1:], strict=False)]

    def own_rows(left, right, arrived, moved):
        total = dot_tn(left[:, :ctx_own], right) + arrived[:ctx_own].astype(F32)
        for part in moved:
            total = total + part.astype(F32)
        return total

    def deal_rows(total):
        return deal(total.astype(BF).reshape(n, rows, total.shape[1]), "fsdp")

    away = by_features(grad_pair[own_tokens:], pair_whole).astype(BF).reshape(n, h, width)
    low = z < n // 2
    early = jnp.where(low, 1, n - 1)
    leaving = pick(away, early)

    def beside_first(grad_pair, activated, grad_all, pair_whole):
        kept = by_features(grad_pair[:own_tokens], pair_whole).reshape(n, h, width)
        return kept, core_term(grad_all, activated)

    def result_terms(activated, down_whole):
        return by_features(activated, down_whole).astype(BF)

    def result_order(result):
        result = result.reshape(2, n, h, width)
        by_y = jnp.where(y == 0, result, result[::-1])
        by_z = jnp.stack([by_y[:, k] for k in range(n)])
        return jnp.stack([pick(by_z, (z - b) % n) for b in range(n)]).reshape(-1, width)

    y_early = flip(leaving, "tp", 1)
    kept, down_leaving = segment(
        ready, beside_first, grad_pair, activated, grad_all, pair_whole
    )
    if n == 4:
        y_early = after(y_early, kept)
        acc_up = (kept[1] + y_early.astype(F32)).astype(BF)
        acc_down = (kept[3] + y_early.astype(F32)).astype(BF)
        acc_up, acc_down = together(acc_up, acc_down)
        up, down = sum_up(acc_up, 1), sum_down(acc_down, 1)
        y_mid = flip(after(away[2], acc_up), "tp", 1)
        down_core = flip(after(down_leaving, acc_up), "ctx", 1)
        pair_leaving = segment(
            ready, core_term, after(normed_all, acc_up, acc_down), grad_pair
        )

        up, down, y_mid = after(up, pair_leaving), after(down, pair_leaving), after(y_mid, pair_leaving)
        acc_up = (kept[2] + y_mid.astype(F32) + up.astype(F32)).astype(BF)
        acc_down = (kept[2] + y_mid.astype(F32) + down.astype(F32)).astype(BF)
        acc_up, acc_down, down_core = together(acc_up, acc_down, down_core)
        up, down = sum_up(acc_up, 2), sum_down(acc_down, 2)
        y_late = flip(after(pick(away, n - early), acc_up), "tp", 1)
        pair_core = flip(after(pair_leaving, acc_up), "ctx", 1)

        down_terms = segment(
            ready, x_terms, after(grad_all, acc_up, acc_down), activated, down_core
        )

        down_moved = to_x(down_terms)
        by_z = segment(ready, result_terms, after(act_natural, *down_terms), down_whole)

        up, down, y_late = together(up, down, y_late, by_z)[:3]
        crossed_three = jnp.where(low, y_late, y_early).astype(F32)
        crossed_one = jnp.where(low, y_early, y_late).astype(F32)
        acc_up = (kept[3] + crossed_three + up.astype(F32)).astype(BF)
        acc_down = (kept[1] + crossed_one + down.astype(F32)).astype(BF)
        acc_up, acc_down = together(acc_up, acc_down)
        up, down = sum_up(acc_up, 3), sum_down(acc_down, 3)
        y_own = flip(after(away[0], acc_up), "tp", 1)

        def beside_third(
            normed_all, grad_pair, pair_core, grad_all, activated, down_core, down_moved
        ):
            terms = x_terms(normed_all, grad_pair, pair_core)
            return terms, own_rows(grad_all, activated, down_core, down_moved).astype(BF)

        pair_terms, down_total = segment(
            ready,
            beside_third,
            after(normed_all, acc_up, acc_down),
            grad_pair,
            pair_core,
            grad_all,
            activated,
            down_core,
            down_moved,
        )

        y_own = after(y_own, *pair_terms)
        grad_normed_two = kept[0] + y_own.astype(F32) + up.astype(F32) + down.astype(F32)
    else:
        crossed = [flip(away[k], "tp", 1) for k in range(n)]
        grad_normed_two = chain_sum([kept[k] + crossed[k].astype(F32) for k in range(n)])
        by_z = result_order(result_terms(activated, down_whole))
        down_core = flip(down_leaving, "ctx", 1)
        pair_core = flip(core_term(normed_all, grad_pair), "ctx", 1)
        pair_terms = x_terms(normed_all, grad_pair, pair_core)
        down_moved = to_x(x_terms(grad_all, activated, down_core))
        down_total = own_rows(grad_all, activated, down_core, down_moved).astype(BF)

    scaled = grad_normed_two * gain_two
    gain_two_grad = jnp.sum(grad_normed_two * middle * inverse_two, axis=0)
    grad_middle = (
        inverse_two * scaled
        - middle * inverse_two**3 * jnp.mean(scaled * middle, axis=-1, keepdims=True)
        + grad_half.astype(F32)
    )
    middle_half = grad_middle.astype(BF)

    out_other = flip(middle_half, "tp", 1)
    result_sum = lax.psum_scatter(
        after(by_z, middle_half), ("fsdp", "tp"), scatter_dimension=0, tiled=True
    )

    def whole_rows(left, right, arrived, moved):
        return own_rows(left, right, arrived, moved).astype(BF)

    def deal_by_three(total, *earlier):
        parts = total.reshape(n, rows, total.shape[1])
        slots = {0: pick(parts, z)}
        for k in range(1, n):
            slots[k] = rotate(after(pick(parts, (z + k) % n), *earlier), "fsdp", k)
        return slots

    if n == 4:
        down_dealt = deal_by_three(down_total, middle_half)
        down_there = [down_dealt[k] for k in (1, n - 1)]
    else:
        down_dealt = deal_rows(down_total)
        down_there = []
    pair_moved = to_x([after(term, middle_half) for term in pair_terms])

    def attend_back(own, other, out_whole, queries, key_rows, value_rows, log_total):
        out_in = jnp.where(y == 0, jnp.concatenate([own, other]), jnp.concatenate([other, own]))
        grad_heads = dot(out_in[:, :half_d], out_whole[:half_d])
        grad_heads = grad_heads + dot(out_in[:, half_d:], out_whole[half_d:])
        grad_heads = grad_heads.astype(BF).reshape(count, heads, HD)
        exact = jnp.exp(attention_scores(queries, key_rows) - log_total)
        grad_probs = jnp.einsum("tgd,kd->gtk", grad_heads, value_rows, preferred_element_type=F32)
        grad_scores = exact * (grad_probs - jnp.sum(exact * grad_probs, axis=-1, keepdims=True))
        grad_scores = grad_scores.astype(BF)
        grad_queries = (
            jnp.einsum("gtk,kd->tgd", grad_scores, key_rows, preferred_element_type=F32) * scale
        )
        grad_key_rows = (
            jnp.einsum("gtk,tgd->kd", grad_scores, queries, preferred_element_type=F32) * scale
        )
        grad_value_rows = jnp.einsum(
            "gtk,tgd->kd", exact.astype(BF), grad_heads, preferred_element_type=F32
        )
        grad_pairs = jnp.stack([grad_key_rows, grad_value_rows]).reshape(2, ctx_size, count, HD)
        sent = [grad_pairs[:, j].astype(BF) for j in range(1, ctx_size)]
        return out_in, grad_queries, grad_pairs[:, 0], sent, core_term(out_in, attended)

    out_in, grad_queries, grad_kv, sent, out_leaving = segment(
        ready,
        attend_back,
        middle_half,
        out_other,
        out_whole,
        queries,
        key_rows,
        value_rows,
        log_total,
    )
    moved = [flip(after(part, *down_there), "ctx", j) for j, part in enumerate(sent, start=1)]
    out_core = flip(after(out_leaving, *down_there), "ctx", 1)

    def pair_rows(normed_all, grad_pair, pair_core, pair_moved):
        total = own_rows(normed_all, grad_pair, pair_core, pair_moved).astype(BF)
        if n != 4:
            return total
        parts = total.reshape(n, rows, total.shape[1])
        return [pick(parts, (z + k) % n) for k in range(n)]

    pair_total = segment(
        ready, pair_rows, after(normed_all, *sent), grad_pair, pair_core, pair_moved
    )
    pair_last = pair_total[0] if n == 4 else pair_total
    out_terms = x_terms(out_in, attended, after(out_core, *moved, pair_last))
    out_moved = to_x(out_terms)

    def project_back(grad_queries, grad_kv, moved, normed_placed, qkv_whole, *bulk):
        sin_back = sin_table + nothing_of(*bulk)
        for part in moved:
            grad_kv = grad_kv + part.astype(F32)
        grad_project = (
            jnp.concatenate(
                [
                    rotary_back(grad_queries, cos_table[:, None], sin_back[:, None]),
                    rotary_back(grad_kv[0], cos_table, sin_back)[:, None],
                    grad_kv[1][:, None],
                ],
                axis=1,
            )
            .astype(BF)
            .reshape(count, -1)
        )
        away = core_term(normed_placed, grad_project)
        arrived = flip(away, "ctx", 1)
        partial_one = dot_nt(after(grad_project, away), qkv_whole).astype(BF)
        terms = x_terms(normed_placed, grad_project, after(arrived, partial_one))
        return grad_project, partial_one, arrived, terms

    grad_project, partial_one, qkv_core, qkv_terms = segment(
        ready,
        project_back,
        grad_queries,
        grad_kv,
        moved,
        normed_placed,
        qkv_whole,
        *out_terms,
        pair_last,
    )
    if n == 4:
        pair_dealt = {0: pair_total[0]}
        for k in (1, 3):
            pair_dealt[k] = rotate(pair_total[k], "fsdp", k)
        two_there = [pair_dealt[1], pair_dealt[3]]
        pair_dealt[2] = rotate(pair_total[2], "fsdp", 2)
        last_there = [pair_dealt[2]]
    else:
        pair_dealt = deal_rows(pair_total)
        two_there = last_there = []
    qkv_moved = to_x([after(term, *two_there) for term in qkv_terms])
    arrived_one = flip(after(partial_one, *qkv_terms), "tp", 1)

    def natural_columns(parts):
        whole = jnp.concatenate([parts[b] for b in range(n)], axis=1)
        return whole[:, :hidden].astype(F32)

    out_total = own_rows(
        after(out_in, *qkv_terms), attended, out_core, [after(p, *qkv_terms) for p in out_moved]
    )

    def beside_x(grad_project, out_in, down_dealt):
        bias_grad = jnp.sum(grad_project, axis=0, dtype=F32)
        if n == 4:
            down_dealt = in_order([down_dealt[k] for k in range(n)])
        return bias_grad, dot_nt(out_in, place), natural_columns(down_dealt)

    bias_grad, middle_natural, down_grad = segment(
        ready, beside_x, after(grad_project, *qkv_terms, out_total), out_in, down_dealt
    )
    qkv_moved = [after(part, bias_grad, *last_there) for part in qkv_moved]
    qkv_total = own_rows(normed_placed, grad_project, qkv_core, qkv_moved)
    last_total = jnp.concatenate([qkv_total, out_total], axis=1)
    last_parts = last_total.reshape(n, rows, -1)
    if n == 4:
        last_dealt = [
            rotate(pick(last_parts, (z + k) % n).astype(BF), "fsdp", k) for k in range(1, n)
        ]
    arrived_one = after(arrived_one, qkv_total)

    def every_second(parts, which):
        return jnp.concatenate(
            [parts[:, :, s : s + tile] for s in range(which * tile, 2 * piece, 2 * tile)], axis=2
        )

    def beside_z(pair_dealt, result_sum, *bulk):
        if n == 4:
            pair_dealt = in_order([pair_dealt[k] for k in range(n)])
        pair_grad = [
            natural_columns(every_second(pair_dealt, c)) + nothing_of(*bulk) for c in range(2)
        ]
        residual = (middle + result_sum.astype(F32)).astype(BF)
        return jnp.stack(pair_grad, axis=1), residual

    pair_grad, residual = segment(ready, beside_z, pair_dealt, result_sum, qkv_total)
    residual_other = flip(residual, "tp", 1)
    if n == 4:
        last_grad = pick(last_parts, z)
        for part in last_dealt:
            last_grad = last_grad + after(part, residual_other).astype(F32)
    else:
        last_grad = add_z(last_total)
    split = qkv_total.shape[1]
    qkv_grad, out_grad = last_grad[:, :split], last_grad[:, split:]
    residual_whole = jnp.where(
        y == 0,
        jnp.concatenate([residual, residual_other]),
        jnp.concatenate([residual_other, residual]),
    )
    output = dot_nt(residual_whole, place).astype(BF)
    grad_normed_one = partial_one.astype(F32) + arrived_one.astype(F32)
    scaled = grad_normed_one * norm_in
    gain_one_grad = jnp.sum(grad_normed_one * x0 * inverse_one, axis=0)
    grad_tokens = (
        inverse_one * scaled
        - x0 * inverse_one**3 * jnp.mean(scaled * x0, axis=-1, keepdims=True)
        + middle_natural
    )

    gain_two_pair = sum_everywhere(after(gain_two_grad[None], *qkv_terms), ("tp",))
    small = jnp.concatenate(
        [gain_one_grad[None], bias_grad[None], to_natural(gain_two_pair)], axis=1
    )
    small = sum_everywhere(small, ("ctx",))
    small_all = after(small, pair_grad)
    bit = 1
    while bit < n:
        small_all = small_all + flip(small_all, "fsdp", bit)
        if bit == 1:
            small_all = after(small_all, residual_other)
        bit *= 2
    return (
        output,
        grad_tokens,
        small_all[:, :width],
        qkv_grad.reshape(1, rows, 1, -1),
        small_all[:, width:-width].reshape(1, 1, -1),
        out_grad[None],
        small_all[:, -width:],
        pair_grad[None],
        down_grad[None],
    )


def solution(mesh):
    rows = ("fsdp", "ctx")
    in_specs = (
        P(rows, None),
        P(rows, None),
        P(),
        P(None, rows, "tp", None),
        P(None, "tp", None),
        P(None, rows, "tp"),
        P(),
        P(None, rows, None, "tp"),
        P(None, rows, "tp"),
        P(rows),
        P(rows),
    )
    out_specs = (
        P(rows, None),
        P(rows, None),
        P(),
        P(None, rows, "tp", None),
        P(None, "tp", None),
        P(None, rows, "tp"),
        P(),
        P(None, rows, None, "tp"),
        P(None, rows, "tp"),
    )
    return jax.shard_map(body, mesh=mesh, in_specs=in_specs, out_specs=out_specs, check_vma=False)
```
